128 devices in a mesh: gx: 16 (over z, x), gy: 8 (over y, core).
Axes of the slice: x: 4, y: 4, z: 4, core: 2. Of those that a mesh axis runs over, the one named last changes fastest.
Arguments:
- offsets: float32 [24576, 3, 128], P(('gx', 'gy')), may hold values from 0 to 1
- velocity: float32 [24576, 3, 128], P(('gx', 'gy')), may hold values from -6 to 6
- strain: float32 [24576, 6, 128], P(('gx', 'gy')), may hold values from -3 to 3
- cells: int32 [24576, 128], P(('gx', 'gy')), may hold values from 0 to 511
- materials: int32 [24576, 128], P(('gx', 'gy')), may hold values from 0 to 3
- counts: int32 [24576], P(('gx', 'gy')), may hold values from 1 to 128, 2359296 in all
- block_dest: int32 [24576, 1], P(('gx', 'gy')), may hold values from 0 to 127; in each aligned block of 192 rows (0 to 191, 192 to 383, ...) at most 2 rows name the same one
- material_params: float32 [3, 4], replicated, may hold values from 0.5 to 2
Outputs:
- new_velocity: float32 [24576, 3, 128], P(('gx', 'gy'))
- new_strain: float32 [24576, 6, 128], P(('gx', 'gy'))
- grid_velocity: float32 [3, 32, 16, 128], P(None, 'gx', 'gy')
The draws below stay inside these ranges and needn't reach their ends.
Inputs may be any that keep to these rules, and one draw needn't show every extreme that they name: `block_dest`: the 192 blocks of one owner device name one patch at most 2 times, and some owner reaches 2.
All inputs are finite; a program needn't handle non-finite values. No bound on the sum of `counts` on one device may be relied on, other than what follows from the above.
Results may differ from the reference program's by a relative error of at most 0.00015.
Values sent between devices are 32-bit elements; how exact they have to be, the bound alone decides.
A program may use at most 64 MiB of HBM per device.

```python
import math
import jax
import jax.numpy as jnp
import numpy as np

PXC = 2
PYC = 2
NZ = 128
NB_DEV = 192
BLK = 128
NMAT = 4
CAP = 2
NBLOCKS = 24576
NX = 32
NY = 16
N_GY = 8
DEVICES = 128


def place_ends(drawn, key, smallest, high):
    index_at = [jax.random.randint(jax.random.fold_in(key, axis), (), 0, length) for axis, length in enumerate(drawn.shape)]
    widest = drawn.shape.index(max(drawn.shape))
    beside = index_at[:widest] + [(index_at[widest] + 1) % drawn.shape[widest]] + index_at[widest + 1:]
    return drawn.at[tuple(index_at)].set(smallest).at[tuple(beside)].set(high)


def shard_levels(own_key, extent, pieces, low, largest):
    factor_of, own = 1.0, jax.random.fold_in(own_key, 6)
    for position, blocks in pieces:
        draws = jnp.exp(jax.random.uniform(jax.random.fold_in(own, position), (blocks,), jnp.float32, low / len(pieces), largest / len(pieces)))
        factor_of = factor_of * jnp.repeat(draws, extent[position] // blocks).reshape([-1 if axis == position else 1 for axis in range(len(extent))])
    return factor_of


def profile(number_of, total, bound, skew):
    loads = [(1 << 20) // math.isqrt(grade ** skew) + 1 for grade in range(2, number_of + 1)]
    rest, given = total - bound - (number_of - 1), [1] * (number_of - 1)
    while rest > 0:
        candidates = [i for i in range(number_of - 1) if given[i] < bound]
        pool, budget = sum([loads[i] for i in candidates]), rest
        for i in candidates:
            addition = min(bound - given[i], max(1, budget * loads[i] // pool), rest)
            given[i] = given[i] + addition
            rest = rest - addition
    return np.array([bound] + given)


def uneven_parts(rng, count, total, reach, lean):
    if count == 2:
        one = jax.random.randint(rng, (), max(1, total - reach), min(reach, total - 1) + 1)
        return jnp.stack([one, total - one])
    tallies = jnp.asarray(profile(count, total, reach, lean), jnp.int32)
    pairs = (count - 1) // 2
    donor, taker = tallies[1:1 + 2 * pairs:2], tallies[2:2 + 2 * pairs:2]
    room = jnp.minimum(donor - 1, reach - taker)
    moved = jax.random.randint(jax.random.fold_in(rng, 1), (pairs,), 0, 1 << 20) % (room + 1)
    tallies = tallies.at[1:1 + 2 * pairs:2].set(donor - moved).at[2:2 + 2 * pairs:2].set(taker + moved)
    return tallies[jax.random.permutation(jax.random.fold_in(rng, 2), count)]


def routed_block(own_key, own, number, rows, count, top, most, lean):
    sequence = jax.random.permutation(own_key, count)
    crowded, ordinary = shares(count, rows * top, most, lean, True), shares(count, rows * top, most, lean, False)
    places = jnp.arange(count)

    def named(sizes, rotation):
        used = int((sizes > 0).sum())
        fixed = max(1, used // 4)
        shifted = fixed + (places - fixed + rotation * (used - fixed)) % max(1, count - fixed)
        return jnp.zeros((count,), jnp.int32).at[sequence[jnp.where(places < fixed, places, shifted)]].set(jnp.asarray(sizes, jnp.int32))

    sizes = jnp.where(number % 4 == 0, named(crowded, number // 4), named(ordinary, number - number // 4 - 1))
    mixed = jax.random.permutation(jax.random.fold_in(own, 3), count)
    donor, receiver = mixed[0:count // 2 * 2:2], mixed[1:count // 2 * 2:2]
    margin = jnp.minimum(sizes[donor] - 1, most - sizes[receiver]) // 2
    margin = jnp.where((donor == sequence[0]) | (receiver == sequence[0]) | (sizes[receiver] == 0), 0, jnp.maximum(margin, 0))
    shifted = jax.random.randint(jax.random.fold_in(own, 4), (count // 2,), 0, 1 << 20) % (margin + 1)
    sizes = sizes.at[donor].add(-shifted).at[receiver].add(shifted)
    members = jnp.searchsorted(jnp.cumsum(sizes), jnp.arange(rows * top), side="right").astype(jnp.int32)
    table = members.reshape(top, rows).T
    table = table[jax.random.permutation(jax.random.fold_in(own, 1), rows)]
    rotation = jax.random.randint(jax.random.fold_in(own, 2), (rows, 1), 0, top)
    return jnp.take_along_axis(table, (jnp.arange(top)[None, :] + rotation) % top, axis=1)


def shares(amount, total, reach, slope, full):
    loads = [(1 << 20) // math.isqrt(rank ** slope) + 1 for rank in range(1, amount + 1)]
    largest = reach if full else min(reach, max(-(-total // amount), total * loads[0] // sum(loads)))
    least = 1 if total - largest >= amount - 1 else 0
    holding, rest = [largest] + [least] * (amount - 1), total - largest - least * (amount - 1)
    while rest > 0:
        free = [i for i in range(1, amount) if holding[i] < largest] or [i for i in range(1, amount) if holding[i] < reach]
        whole, remaining = sum([loads[i] for i in free]), rest
        for i in free:
            addition = min(reach - holding[i], max(1, remaining * loads[i] // whole), rest)
            holding[i] = holding[i] + addition
            rest = rest - addition
    return np.array(holding)


def normal_values(own_key, shape, scale, reach, cuts=(), held_as=jnp.bfloat16):
    level = shard_levels(own_key, shape, cuts, -0.22, 0.18) if cuts else 1.0
    drawn = jax.random.normal(own_key, shape, jnp.float32) * scale * level
    return jnp.minimum(jnp.maximum(drawn, -reach), reach).astype(held_as)


def setup_inputs(seed: int = 0) -> dict:
    key_list = jax.random.split(jax.random.key(seed), 9)
    offsets = jnp.clip(1.0 * jax.random.uniform(key_list[0], (NBLOCKS, 3, BLK), jnp.float32) ** shard_levels(key_list[0], (NBLOCKS, 3, BLK), ((0, 128),), -0.2, 0.2), 0.0, 1.0)
    velocity = normal_values(key_list[1], (NBLOCKS, 3, BLK), 1.0, 6.0, ((0, 128),), jnp.float32)
    strain = normal_values(key_list[2], (NBLOCKS, 6, BLK), 0.5, 3.0, ((0, 128),), jnp.float32)
    cells = place_ends(jax.random.randint(key_list[3], (NBLOCKS, BLK), 0, PXC * PYC * NZ), jax.random.fold_in(key_list[3], 1), 0, (PXC * PYC * NZ) - 1).astype(jnp.int32)
    materials = place_ends(jax.random.randint(key_list[4], (NBLOCKS, BLK), 0, NMAT), jax.random.fold_in(key_list[4], 1), 0, NMAT - 1).astype(jnp.int32)
    counts = uneven_parts(key_list[5], NBLOCKS, NBLOCKS * BLK * 3 // 4, BLK, 1).astype(jnp.int32)
    block_dest_keys = jax.random.split(jax.random.fold_in(key_list[6], 1), NBLOCKS // NB_DEV)
    block_dest_turns = jax.random.permutation(jax.random.fold_in(key_list[6], 3), NBLOCKS // NB_DEV)
    block_dest = jax.vmap(lambda own, number: routed_block(jax.random.fold_in(key_list[6], 2), own, number, NB_DEV, DEVICES, 1, CAP, 2))(block_dest_keys, block_dest_turns).reshape((NBLOCKS, 1))
    material_params = jnp.clip(jnp.exp(jax.random.uniform(key_list[7], (3, NMAT), jnp.float32, math.log(0.5), math.log(2.0))), 0.5, 2.0)
    return dict(offsets=offsets, velocity=velocity, strain=strain, cells=cells, materials=materials, counts=counts, block_dest=block_dest, material_params=material_params)


DT_STEP = 0.25
VOLUME = 0.5
GRAVITY = 1.0
MASS_FLOOR = 0.25
CORNERS = [(0, 0, 0), (0, 0, 1), (0, 1, 0), (0, 1, 1), (1, 0, 0), (1, 0, 1), (1, 1, 0), (1, 1, 1)]

def corner_terms(fracs, corner):
    weights = []
    signs = []
    for axis_num in range(3):
        if corner[axis_num]:
            weights.append(fracs[axis_num])
            signs.append(1.0)
        else:
            weights.append(1.0 - fracs[axis_num])
            signs.append(-1.0)
    weight = weights[0] * weights[1] * weights[2]
    gradient = (signs[0] * weights[1] * weights[2], weights[0] * signs[1] * weights[2], weights[0] * weights[1] * signs[2])
    return (weight, gradient)

def stress_rows(strains, shear):
    trace_term = shear * (strains[0] + strains[1] + strains[2])
    s_xx = 2.0 * shear * strains[0] + trace_term
    s_yy = 2.0 * shear * strains[1] + trace_term
    s_zz = 2.0 * shear * strains[2] + trace_term
    s_xy = 2.0 * shear * strains[3]
    s_xz = 2.0 * shear * strains[4]
    s_yz = 2.0 * shear * strains[5]
    return ((s_xx, s_xy, s_xz), (s_xy, s_yy, s_yz), (s_xz, s_yz, s_zz))

def return_map(strains, grads, limit):
    trial = [strains[0] + DT_STEP * grads[0][0], strains[1] + DT_STEP * grads[1][1], strains[2] + DT_STEP * grads[2][2], strains[3] + DT_STEP * 0.5 * (grads[0][1] + grads[1][0]), strains[4] + DT_STEP * 0.5 * (grads[0][2] + grads[2][0]), strains[5] + DT_STEP * 0.5 * (grads[1][2] + grads[2][1])]
    mean_part = (trial[0] + trial[1] + trial[2]) / 3.0
    devs = [trial[0] - mean_part, trial[1] - mean_part, trial[2] - mean_part, trial[3], trial[4], trial[5]]
    magnitude = jnp.sqrt(devs[0] * devs[0] + devs[1] * devs[1] + devs[2] * devs[2] + 2.0 * (devs[3] * devs[3] + devs[4] * devs[4] + devs[5] * devs[5]))
    factor = limit / jnp.maximum(magnitude, limit)
    return [mean_part + factor * devs[0], mean_part + factor * devs[1], mean_part + factor * devs[2], factor * devs[3], factor * devs[4], factor * devs[5]]

def reference(offsets, velocity, strain, cells, materials, counts, block_dest, material_params):
    dest = block_dest[:, 0]
    patch_x = (dest // N_GY)[:, None]
    patch_y = (dest % N_GY)[:, None]
    is_live = jnp.arange(BLK, dtype=jnp.int32)[None, :] < counts[:, None]
    live_float = is_live.astype(jnp.float32)
    cell_z = cells % NZ
    cell_y = cells // NZ % PYC
    cell_x = cells // (NZ * PYC)
    node_x = patch_x * PXC + cell_x
    node_y = patch_y * PYC + cell_y
    masses = material_params[0][materials]
    shear = material_params[1][materials]
    limit = material_params[2][materials]
    fracs = (offsets[:, 0], offsets[:, 1], offsets[:, 2])
    speeds = [velocity[:, 0], velocity[:, 1], velocity[:, 2]]
    strains = [strain[:, comp] for comp in range(6)]
    stress = stress_rows(strains, shear)
    nodes_total = NX * NY * NZ
    grid = jnp.zeros((4, nodes_total), jnp.float32)
    flats = []
    valids = []
    for corner in CORNERS:
        weight, gradient = corner_terms(fracs, corner)
        valid = is_live & (node_x + corner[0] < NX) & (node_y + corner[1] < NY) & (cell_z + corner[2] < NZ)
        flat = ((node_x + corner[0]) * NY + node_y + corner[1]) * NZ + cell_z + corner[2]
        flats.append(flat)
        valids.append(valid)
        dropped = jnp.where(valid, flat, nodes_total).reshape(-1)
        rows = [weight * masses]
        for comp in range(3):
            force = stress[comp][0] * gradient[0] + stress[comp][1] * gradient[1] + stress[comp][2] * gradient[2]
            rows.append(weight * masses * speeds[comp] - DT_STEP * VOLUME * force)
        contrib = jnp.stack(rows) * live_float[None]
        grid = grid.at[:, dropped].add(contrib.reshape(4, -1), mode='drop')
    node_mass = grid[0]
    momentum = grid[1:4]
    momentum = momentum.at[2].add(-DT_STEP * GRAVITY * node_mass)
    node_vel = momentum / jnp.maximum(node_mass, MASS_FLOOR)[None]
    node_vel = node_vel.reshape(3, NX, NY, NZ)
    above = (jnp.arange(NZ, dtype=jnp.int32) > 0).astype(jnp.float32)
    node_vel = node_vel * above[None, None, None, :]
    flat_vel = node_vel.reshape(3, nodes_total)
    new_speed = [jnp.zeros_like(fracs[0]) for comp in range(3)]
    grads = [[jnp.zeros_like(fracs[0]) for col in range(3)] for row in range(3)]
    for pos, corner in enumerate(CORNERS):
        weight, gradient = corner_terms(fracs, corner)
        valid_float = valids[pos].astype(jnp.float32)
        safe = jnp.where(valids[pos], flats[pos], 0)
        for comp in range(3):
            picked = flat_vel[comp][safe] * valid_float
            new_speed[comp] = new_speed[comp] + weight * picked
            for col in range(3):
                grads[comp][col] = grads[comp][col] + picked * gradient[col]
    new_strains = return_map(strains, grads, limit)
    new_velocity = jnp.stack(new_speed, axis=1) * live_float[:, None, :]
    new_strain = jnp.stack(new_strains, axis=1) * live_float[:, None, :]
    return (new_velocity, new_strain, node_vel)
```

```python
import functools

import jax
import jax.numpy as jnp
from jax import lax
from jax.experimental import pallas as pl
from jax.experimental.pallas import tpu as pltpu
from jax.sharding import PartitionSpec as P

GX = 16
GY = 8
PY = 4
NZ = 128
NB = 192
DT = 0.25
VOLUME = 0.5
GRAVITY = 1.0
FLOOR = 0.25
MESH = pl.DeviceIdType.MESH
F32 = jnp.float32
BF16 = jnp.bfloat16
VMEM = pl.BlockSpec(memory_space=pltpu.VMEM)
SMEM = pl.BlockSpec(memory_space=pltpu.SMEM)
LIMIT = 48 * 1024 * 1024


def iota(shape, dim):
    return lax.broadcasted_iota(jnp.int32, shape, dim)


def live_mask(counts, group):
    sub = iota((8, 128), 0)
    limit = jnp.zeros((8, 128), jnp.int32)
    for s in range(8):
        limit = jnp.where(sub == s, counts[group * 8 + s], limit)
    return iota((8, 128), 1) < limit


def by_material(params, row, mats):
    value = jnp.where(mats == 1, params[row, 1], params[row, 0])
    value = jnp.where(mats == 2, params[row, 2], value)
    return jnp.where(mats == 3, params[row, 3], value)


def source_rows(counts, params, off, vel, strain, mats, rows, group):
    at = pl.ds(pl.multiple_of(group * 8, 8), 8)
    live = live_mask(counts, group)
    material = mats[at, :]
    mass = jnp.where(live, by_material(params, 0, material), 0.0)
    shear = jnp.where(live, by_material(params, 1, material), 0.0) * (-DT * VOLUME)
    e = [strain[k, at, :] for k in range(6)]
    trace = shear * (e[0] + e[1] + e[2])
    twice = 2.0 * shear
    xx, yy, zz = (twice * e[k] + trace for k in range(3))
    xy, xz, yz = (twice * e[k] for k in range(3, 6))
    fz = off[2, at, :]
    zero = jnp.zeros((8, 128), F32)
    full = [mass] + [mass * vel[k, at, :] for k in range(3)]
    base = group * 192

    def put(row, value):
        rows[pl.ds(base + row, 8, stride=24), :] = value

    for q, sz in enumerate((None, xz, yz, zz)):
        upper = fz * full[q]
        if sz is not None:
            upper = upper + sz
        put(4 + q, upper)
        put(q, full[q] - upper)
    for start, terms in ((8, (None, xx, xy, xz)), (16, (None, xy, yy, yz))):
        for q, term in enumerate(terms):
            if term is None:
                put(start + q, zero)
                put(start + 4 + q, zero)
            else:
                upper = fz * term
                put(start + 4 + q, upper)
                put(start + q, term - upper)


def node_rows(rows, off, cells, block):
    base = pl.multiple_of(block * 24, 8)
    t = rows[pl.ds(base, 8), :]
    sx = rows[pl.ds(base + 8, 8), :]
    sy = rows[pl.ds(base + 16, 8), :]
    fx = jnp.broadcast_to(off[0, pl.ds(block, 1), :], (8, 128))
    fy = jnp.broadcast_to(off[1, pl.ds(block, 1), :], (8, 128))
    cell = jnp.broadcast_to(cells[pl.ds(block, 1), :], (8, 128))
    in_x = cell >= 2 * NZ
    in_y = (cell & NZ) != 0
    u1 = fx * t + sx
    u0 = t - u1
    w1 = fx * sy
    w0 = sy - w1
    c11 = fy * u1 + w1
    c10 = u1 - c11
    c01 = fy * u0 + w0
    c00 = u0 - c01
    d = []
    for low, high in ((c00, c10), (c01, c11)):
        d.append(
            (jnp.where(in_x, 0.0, low), jnp.where(in_x, low, high), jnp.where(in_x, high, 0.0))
        )
    tiles = []
    for i in range(3):
        low, high = d[0][i], d[1][i]
        tiles += [jnp.where(in_y, 0.0, low), jnp.where(in_y, low, high), jnp.where(in_y, high, 0.0)]
    tiles.append(jnp.zeros((8, 128), F32))
    full = jnp.concatenate(tiles, axis=0)
    hi = full.astype(BF16)
    lo = (full - hi.astype(F32)).astype(BF16)
    z = (cell & (NZ - 1)).astype(F32)
    z16 = jnp.concatenate([z, z], axis=0).astype(BF16)
    z_all = jnp.concatenate([z16] * 8, axis=0)
    depth = iota((128, 128), 0).astype(F32).astype(BF16)
    hot = jnp.where(depth == z_all, jnp.ones((), BF16), jnp.zeros((), BF16))
    return hi, lo, hot


def contract(left, right):
    return lax.dot_general(left, right, (((1,), (1,)), ((), ())), preferred_element_type=F32)


def scatter_kernel(dest, counts, params, off, vel, strain, cells, mats, out, rows, acc):
    def clear(x, carry):
        acc[x] = jnp.zeros((17, 8, 128), F32)
        return carry

    lax.fori_loop(0, 33, clear, 0)

    def prepare(group, carry):
        source_rows(counts, params, off, vel, strain, mats, rows, group)
        return carry

    lax.fori_loop(0, NB // 8, prepare, 0)

    def spread(pair, carry):
        for s in range(2):
            block = pair * 2 + s
            hi, lo, hot = node_rows(rows, off, cells, block)
            sums = contract(
                jnp.concatenate([hi, lo], axis=1), jnp.concatenate([hot, hot], axis=1)
            )
            d = dest[block]
            x0 = d // GY * 2
            y0 = d % GY * 2
            for i in range(3):
                for j in range(3):
                    n = i * 3 + j
                    acc[x0 + i, y0 + j] += sums[n * 8 : n * 8 + 8]
        return carry

    lax.fori_loop(0, NB // 2, spread, 0)

    low_half = iota((8, 128), 0) < 4
    above = iota((8, 128), 1) > 0

    def fold(gx, carry):
        for x in range(2):
            for gy in range(GY):
                even = acc[gx * 2 + x, gy * 2]
                odd = acc[gx * 2 + x, gy * 2 + 1]
                first = jnp.where(low_half, even, pltpu.roll(odd, 4, axis=0))
                second = jnp.where(low_half, pltpu.roll(even, 4, axis=0), odd)
                second = jnp.where(above, pltpu.roll(second, 1, axis=1), 0.0)
                out[gy % 2, gx, gy // 2, x] = first + second
        return carry

    lax.fori_loop(0, GX, fold, 0)


def update(total):
    sub = iota((8, 128), 0)
    mass_e = jnp.broadcast_to(total[0:1], (8, 128))
    mass_o = jnp.broadcast_to(total[4:5], (8, 128))
    mass = jnp.where(sub < 4, mass_e, mass_o)
    moved = pltpu.roll(total, 7, axis=0)
    comp = sub % 4
    moved = moved + jnp.where(comp == 2, -DT * GRAVITY, 0.0) * mass
    value = moved / jnp.maximum(mass, FLOOR)
    keep = (comp < 3) & (iota((8, 128), 1) > 0)
    return jnp.where(keep, value, 0.0)


def exchange_kernel(
    part, node_vel, mine, from_sib, summed, landed, sib_send, sib_recv, sum_send, sum_recv,
    vel_send, vel_recv, fwd_send, fwd_recv,
):
    gx = lax.axis_index("gx")
    gy = lax.axis_index("gy")
    core = lax.rem(gy, 2)
    y = gy // 2
    sibling = (gx, gy + 1 - 2 * core)
    chip = gx * PY + y

    def peer(step, dy):
        px = lax.rem(gx + step, GX)
        py = lax.rem(y + dy, PY)
        return px, py, (px, py * 2 + core)

    barrier = pltpu.get_barrier_semaphore()
    pl.semaphore_signal(barrier, inc=1, device_id=sibling, device_id_type=MESH)

    def greet(step, carry):
        for dy in range(PY):
            pl.semaphore_signal(barrier, inc=1, device_id=peer(step, dy)[2], device_id_type=MESH)
        return carry

    lax.fori_loop(1, GX, greet, 0)
    for dy in range(1, PY):
        pl.semaphore_signal(barrier, inc=1, device_id=peer(0, dy)[2], device_id_type=MESH)
    pl.semaphore_wait(barrier, GX * PY)

    def sib_copy(px):
        return pltpu.make_async_remote_copy(
            src_ref=part.at[1 - core, px], dst_ref=from_sib.at[px], send_sem=sib_send.at[px],
            recv_sem=sib_recv.at[px], device_id=sibling, device_id_type=MESH,
        )

    def send_sib(step, carry):
        sib_copy(lax.rem(gx + step, GX)).start()
        return carry

    lax.fori_loop(1, GX + 1, send_sib, 0)

    def sum_copy(step, dy):
        px, py, device = peer(step, dy)
        return pltpu.make_async_remote_copy(
            src_ref=summed.at[px, py], dst_ref=landed.at[chip], send_sem=sum_send,
            recv_sem=sum_recv, device_id=device, device_id_type=MESH,
        )

    def add_sib(step):
        px = lax.rem(gx + step, GX)
        sib_copy(px).wait_recv()
        summed[px] = part[core, px] + from_sib[px]

    def send_sums(step, carry):
        add_sib(step)
        for dy in range(PY):
            sum_copy(step, dy).start()
        return carry

    lax.fori_loop(1, GX, send_sums, 0)
    add_sib(0)
    for dy in range(1, PY):
        sum_copy(0, dy).start()
    landed[chip] = summed[gx, y]

    many = landed.at[pl.ds(0, GX * PY - 1)]
    pltpu.make_async_copy(many, many, sum_recv).wait()
    total = lax.fori_loop(
        0, GX * PY, lambda c, so_far: so_far + landed[c], jnp.zeros((2, 8, 128), F32)
    )
    for x in range(2):
        mine[x] = update(total[x])

    own = pltpu.make_async_copy(mine, node_vel.at[core, gx, y], vel_send.at[1])
    own.start()

    def vel_copy(step, dy):
        px, py, device = peer(step, dy)
        return pltpu.make_async_remote_copy(
            src_ref=mine, dst_ref=node_vel.at[core, gx, y], send_sem=vel_send.at[0],
            recv_sem=vel_recv.at[gx], device_id=device, device_id_type=MESH,
        )

    def send_vel(step, carry):
        for dy in range(PY):
            vel_copy(step, dy).start()
        return carry

    for dy in range(1, PY):
        vel_copy(0, dy).start()
    lax.fori_loop(1, GX, send_vel, 0)
    own.wait()

    def forward(px):
        return pltpu.make_async_remote_copy(
            src_ref=node_vel.at[core, px], dst_ref=node_vel.at[core, px], send_sem=fwd_send.at[px],
            recv_sem=fwd_recv.at[px], device_id=sibling, device_id_type=MESH,
        )

    def pass_on(step, carry):
        px = lax.rem(gx + GX - step, GX)
        here = node_vel.at[core, px]
        pltpu.make_async_copy(here, here, vel_recv.at[px]).wait()
        forward(px).start()
        return carry

    few = node_vel.at[core, gx, pl.ds(0, PY - 1)]
    pltpu.make_async_copy(few, few, vel_recv.at[gx]).wait()
    forward(gx).start()
    lax.fori_loop(1, GX, pass_on, 0)

    def finish(px, carry):
        sib_copy(px).wait_send()
        forward(px).wait()
        return carry

    lax.fori_loop(0, GX, finish, 0)
    pltpu.make_async_copy(many, many, sum_send).wait()
    pltpu.make_async_copy(many, many, vel_send.at[0]).wait()


def gather_kernel(dest, counts, params, off, strain, cells, mats, node_vel, out_vel, out_strain, out_node, table, rows):
    gx = lax.axis_index("gx")
    gy = lax.axis_index("gy")
    for x in range(2):
        own = node_vel[lax.rem(gy, 2), gx, gy // 2, x]
        for y in range(2):
            for c in range(3):
                out_node[c, x, y : y + 1, :] = own[y * 4 + c : y * 4 + c + 1]

    zeros = jnp.zeros((8, 128), F32)
    for y in range(17):
        table[32, y] = zeros

    low_half = iota((8, 128), 0) < 4
    below = iota((8, 128), 1) < NZ - 1

    def build(gx, carry):
        for x in range(2):
            for gy in range(GY):
                level = node_vel[gy % 2, gx, gy // 2, x]
                lifted = jnp.where(below, pltpu.roll(level, NZ - 1, axis=1), 0.0)
                table[gx * 2 + x, gy * 2] = jnp.where(low_half, level, pltpu.roll(lifted, 4, axis=0))
                table[gx * 2 + x, gy * 2 + 1] = jnp.where(low_half, pltpu.roll(level, 4, axis=0), lifted)
            table[gx * 2 + x, 16] = zeros
        return carry

    lax.fori_loop(0, GX, build, 0)

    def one_group(group, carry):
        at = pl.ds(pl.multiple_of(group * 8, 8), 8)
        cell8 = cells[at, :]
        fx8 = off[0, at, :]
        fy8 = off[1, at, :]
        for s in range(8):
            d = dest[group * 8 + s]
            x0 = d // GY * 2
            y0 = d % GY * 2
            cell = jnp.broadcast_to(cell8[s : s + 1], (8, 128))
            fx = jnp.broadcast_to(fx8[s : s + 1], (8, 128))
            fy = jnp.broadcast_to(fy8[s : s + 1], (8, 128))
            z = cell & (NZ - 1)
            in_x = cell >= 2 * NZ
            in_y = (cell & NZ) != 0
            got = [
                [
                    jnp.take_along_axis(table[x0 + i, y0 + j], z, axis=1, mode="promise_in_bounds")
                    for j in range(3)
                ]
                for i in range(3)
            ]
            side = [
                [jnp.where(in_y, got[i][b + 1], got[i][b]) for b in range(2)] for i in range(3)
            ]
            p = [
                [jnp.where(in_x, side[a + 1][b], side[a][b]) for b in range(2)] for a in range(2)
            ]
            dy = [p[a][1] - p[a][0] for a in range(2)]
            ly = [p[a][0] + fy * dy[a] for a in range(2)]
            gx_term = ly[1] - ly[0]
            rows[s * 24 : s * 24 + 8, :] = ly[0] + fx * gx_term
            rows[s * 24 + 8 : s * 24 + 16, :] = gx_term
            rows[s * 24 + 16 : s * 24 + 24, :] = dy[0] + fx * (dy[1] - dy[0])

        def row(r):
            return rows[pl.ds(r, 8, stride=24), :]

        fz = off[2, at, :]
        speed = []
        grads = []
        for c in range(3):
            v0, v1 = row(c), row(4 + c)
            gz = v1 - v0
            speed.append(v0 + fz * gz)
            gx0, gx1 = row(8 + c), row(12 + c)
            gy0, gy1 = row(16 + c), row(20 + c)
            grads.append((gx0 + fz * (gx1 - gx0), gy0 + fz * (gy1 - gy0), gz))
        live = live_mask(counts, group)
        limit = by_material(params, 2, mats[at, :])
        e = [strain[k, at, :] for k in range(6)]
        trial = [e[k] + DT * grads[k][k] for k in range(3)]
        for k, (r, c) in enumerate(((0, 1), (0, 2), (1, 2))):
            trial.append(e[3 + k] + (0.5 * DT) * (grads[r][c] + grads[c][r]))
        mean = (trial[0] + trial[1] + trial[2]) * (1.0 / 3.0)
        dev = [trial[k] - mean for k in range(3)] + trial[3:]
        square = [x * x for x in dev]
        size = jnp.sqrt(
            square[0] + square[1] + square[2] + 2.0 * (square[3] + square[4] + square[5])
        )
        factor = limit / jnp.maximum(size, limit)
        for k in range(3):
            out_vel[k, at, :] = jnp.where(live, speed[k], 0.0)
            out_strain[k, at, :] = jnp.where(live, mean + factor * dev[k], 0.0)
            out_strain[3 + k, at, :] = jnp.where(live, factor * dev[3 + k], 0.0)
        return carry

    lax.fori_loop(0, NB // 8, one_group, 0)


def scatter(dest, counts, params, off, vel, strain, cells, mats):
    return pl.pallas_call(
        scatter_kernel,
        out_shape=jax.ShapeDtypeStruct((2, GX, PY, 2, 8, 128), F32),
        in_specs=[SMEM] * 3 + [VMEM] * 5,
        out_specs=VMEM,
        scratch_shapes=[pltpu.VMEM((NB * 24, 128), F32), pltpu.VMEM((33, 17, 8, 128), F32)],
        compiler_params=pltpu.CompilerParams(vmem_limit_bytes=LIMIT),
        name="scatter",
    )(dest, counts, params, off, vel, strain, cells, mats)


def exchange(part):
    dma = pltpu.SemaphoreType.DMA
    return pl.pallas_call(
        exchange_kernel,
        out_shape=jax.ShapeDtypeStruct((2, GX, PY, 2, 8, 128), F32),
        in_specs=[VMEM],
        out_specs=pl.BlockSpec(memory_space=pl.ANY),
        scratch_shapes=[
            pltpu.VMEM((2, 8, 128), F32),
            pltpu.VMEM((GX, PY, 2, 8, 128), F32),
            pltpu.VMEM((GX, PY, 2, 8, 128), F32),
            pltpu.VMEM((GX * PY, 2, 8, 128), F32),
            dma((GX,)), dma((GX,)), dma, dma, dma((2,)), dma((GX,)), dma((GX,)), dma((GX,)),
        ],
        compiler_params=pltpu.CompilerParams(
            collective_id=0, has_side_effects=True, vmem_limit_bytes=LIMIT
        ),
        name="exchange",
    )(part)


def gather(dest, counts, params, off, strain, cells, mats, node_vel):
    return pl.pallas_call(
        gather_kernel,
        out_shape=(
            jax.ShapeDtypeStruct((3, NB, 128), F32),
            jax.ShapeDtypeStruct((6, NB, 128), F32),
            jax.ShapeDtypeStruct((3, 2, 2, 128), F32),
        ),
        in_specs=[SMEM] * 3 + [VMEM] * 5,
        out_specs=(VMEM, VMEM, VMEM),
        scratch_shapes=[pltpu.VMEM((33, 17, 8, 128), F32), pltpu.VMEM((8 * 24, 128), F32)],
        compiler_params=pltpu.CompilerParams(vmem_limit_bytes=LIMIT),
        name="gather",
    )(dest, counts, params, off, strain, cells, mats, node_vel)


def shards(offsets, velocity, strain, cells, materials, counts, block_dest, material_params):
    off, vel, eps = (jnp.transpose(x, (1, 0, 2)) for x in (offsets, velocity, strain))
    dest = block_dest.reshape(NB)
    part = scatter(dest, counts, material_params, off, vel, eps, cells, materials)
    node_vel = exchange(part)
    new_vel, new_eps, own = gather(
        dest, counts, material_params, off, eps, cells, materials, node_vel
    )
    return jnp.transpose(new_vel, (1, 0, 2)), jnp.transpose(new_eps, (1, 0, 2)), own


def solution(mesh):
    blocks = P(("gx", "gy"), None, None)
    rows = P(("gx", "gy"), None)
    in_specs = (blocks, blocks, blocks, rows, rows, P(("gx", "gy")), rows, P())
    out_specs = (blocks, blocks, P(None, "gx", "gy", None))
    return jax.shard_map(shards, mesh=mesh, in_specs=in_specs, out_specs=out_specs, check_vma=False)
```

```python
import jax
import jax.numpy as jnp
from jax import lax
from jax.experimental import pallas as pl
from jax.experimental.pallas import tpu as pltpu
from jax.sharding import PartitionSpec as P

GX = 16
GY = 8
PY = 4
NZ = 128
NB = 192
DT = 0.25
VOLUME = 0.5
GRAVITY = 1.0
FLOOR = 0.25
MESH = pl.DeviceIdType.MESH
F32 = jnp.float32
BF16 = jnp.bfloat16
VMEM = pl.BlockSpec(memory_space=pltpu.VMEM)
SMEM = pl.BlockSpec(memory_space=pltpu.SMEM)
HBM = pl.BlockSpec(memory_space=pltpu.HBM)
LIMIT = 32 * 1024 * 1024
EMPTY = NB
ROWS = 32


def iota(shape, dim):
    return lax.broadcasted_iota(jnp.int32, shape, dim)


def live_mask(counts, group):
    sub = iota((8, 128), 0)
    limit = jnp.zeros((8, 128), jnp.int32)
    for s in range(8):
        limit = jnp.where(sub == s, counts[group * 8 + s], limit)
    return iota((8, 128), 1) < limit


def by_material(params, row, mats):
    value = jnp.where(mats == 1, params[row, 1], params[row, 0])
    value = jnp.where(mats == 2, params[row, 2], value)
    return jnp.where(mats == 3, params[row, 3], value)


def source_rows(counts, params, off, vel, strain, cells, mats, rows, group):
    at = pl.ds(pl.multiple_of(group * 8, 8), 8)
    live = live_mask(counts, group)
    material = mats[at, :]
    mass = jnp.where(live, by_material(params, 0, material), 0.0)
    shear = jnp.where(live, by_material(params, 1, material), 0.0) * (-DT * VOLUME)
    e = [strain[k, at, :] for k in range(6)]
    trace = shear * (e[0] + e[1] + e[2])
    twice = 2.0 * shear
    xx, yy, zz = (twice * e[k] + trace for k in range(3))
    xy, xz, yz = (twice * e[k] for k in range(3, 6))
    fz = off[2, at, :]
    zero = jnp.zeros((8, 128), F32)
    full = [mass] + [mass * vel[k, at, :] for k in range(3)]
    base = group * (8 * ROWS)

    def put(row, value):
        rows[pl.ds(base + row, 8, stride=ROWS), :] = value

    for q, sz in enumerate((None, xz, yz, zz)):
        upper = fz * full[q]
        if sz is not None:
            upper = upper + sz
        put(4 + q, upper)
        put(q, full[q] - upper)
    for start, terms in ((8, (None, xx, xy, xz)), (16, (None, xy, yy, yz))):
        for q, term in enumerate(terms):
            if term is None:
                put(start + q, zero)
                put(start + 4 + q, zero)
            else:
                upper = fz * term
                put(start + 4 + q, upper)
                put(start + q, term - upper)
    cell = cells[at, :]
    put(24, off[0, at, :])
    put(25, off[1, at, :])
    put(26, (cell & (NZ - 1)).astype(F32))
    put(27, cell.astype(F32))
    put(28, (cell & NZ).astype(F32))


def node_rows(source):
    t, sx, sy = source[0:8], source[8:16], source[16:24]
    fx, fy, z, in_x, in_y = (
        jnp.broadcast_to(source[24 + k : 25 + k], (8, 128)) for k in range(5)
    )
    in_x = in_x >= 2.0 * NZ
    in_y = in_y > 0.0
    u1 = fx * t + sx
    u0 = t - u1
    w1 = fx * sy
    w0 = sy - w1
    c11 = fy * u1 + w1
    c10 = u1 - c11
    c01 = fy * u0 + w0
    c00 = u0 - c01
    d = []
    for low, high in ((c00, c10), (c01, c11)):
        d.append(
            (jnp.where(in_x, 0.0, low), jnp.where(in_x, low, high), jnp.where(in_x, high, 0.0))
        )
    tiles = []
    for i in range(3):
        low, high = d[0][i], d[1][i]
        tiles += [jnp.where(in_y, 0.0, low), jnp.where(in_y, low, high), jnp.where(in_y, high, 0.0)]
    tiles.append(jnp.zeros((8, 128), F32))
    full = jnp.concatenate(tiles, axis=0)
    hi = full.astype(BF16)
    lo = (full - hi.astype(F32)).astype(BF16)
    z16 = jnp.concatenate([z, z], axis=0).astype(BF16)
    z_all = jnp.concatenate([z16] * 8, axis=0)
    depth = iota((128, 128), 0).astype(F32).astype(BF16)
    hot = jnp.where(depth == z_all, jnp.ones((), BF16), jnp.zeros((), BF16))
    return hi, lo, hot


def contract(left, right):
    return lax.dot_general(left, right, (((1,), (1,)), ((), ())), preferred_element_type=F32)


def find_blocks(dest):
    lane = iota((8, 128), 1)
    none = jnp.full((8, 128), EMPTY, jnp.int32)

    def look(step, found):
        first, last = found
        for s in range(8):
            block = step * 8 + s
            back = NB - 1 - block
            last = jnp.where(lane == dest[block], block, last)
            first = jnp.where(lane == dest[back], back, first)
        return first, last

    first, last = lax.fori_loop(0, NB // 8, look, (none, none))
    second = jnp.where(last == first, EMPTY, last)
    return jnp.where(iota((8, 128), 0) == 0, first, second)


def update(total):
    sub = iota((8, 128), 0)
    mass_e = jnp.broadcast_to(total[0:1], (8, 128))
    mass_o = jnp.broadcast_to(total[4:5], (8, 128))
    mass = jnp.where(sub < 4, mass_e, mass_o)
    moved = pltpu.roll(total, 7, axis=0)
    comp = sub % 4
    moved = moved + jnp.where(comp == 2, -DT * GRAVITY, 0.0) * mass
    value = moved / jnp.maximum(mass, FLOOR)
    keep = (comp < 3) & (iota((8, 128), 1) > 0)
    return jnp.where(keep, value, 0.0)


def scatter_kernel(
    dest, counts, params, off_in, vel_in, strain_in, cells_in, mats_in, node_vel,
    off, vel, strain, cells, mats, found, blocks, rows, acc, part, for_sib, from_sib, mine, landed,
    in_sem, found_sem, sib_send, sib_recv, sum_send, sum_recv, vel_send, vel_recv, fwd_send, fwd_recv,
):
    gx = lax.axis_index("gx")
    gy = lax.axis_index("gy")
    core = lax.rem(gy, 2)
    y = gy // 2
    sibling = (gx, gy + 1 - 2 * core)
    chip = gx * PY + y

    def peer(step, dy):
        px = lax.rem(gx + step, GX)
        py = lax.rem(y + dy, PY)
        return px, py, (px, py * 2 + core)

    loads = [
        pltpu.make_async_copy(src, dst, in_sem.at[k])
        for k, (src, dst) in enumerate(
            (
                (off_in, off),
                (vel_in, vel),
                (strain_in, strain),
                (mats_in, mats),
                (cells_in, cells),
            )
        )
    ]
    for load in loads:
        load.start()

    barrier = pltpu.get_barrier_semaphore()
    pl.semaphore_signal(barrier, inc=1, device_id=sibling, device_id_type=MESH)

    def greet(step, carry):
        for dy in range(PY):
            pl.semaphore_signal(barrier, inc=1, device_id=peer(step, dy)[2], device_id_type=MESH)
        return carry

    lax.fori_loop(1, GX, greet, 0)
    for dy in range(1, PY):
        pl.semaphore_signal(barrier, inc=1, device_id=peer(0, dy)[2], device_id_type=MESH)

    found[...] = find_blocks(dest)
    to_scalars = pltpu.make_async_copy(found, blocks, found_sem)
    to_scalars.start()

    rows[NB * ROWS : (NB + 1) * ROWS, :] = jnp.zeros((ROWS, 128), F32)
    by_block = rows.reshape(NB + 1, ROWS, 128)

    def clear(x, carry):
        acc[x] = jnp.zeros((17, 8, 128), F32)
        return carry

    lax.fori_loop(0, 33, clear, 0)
    for load in loads:
        load.wait()

    def prepare(group, carry):
        source_rows(counts, params, off, vel, strain, cells, mats, rows, group)
        return carry

    lax.fori_loop(0, NB // 8, prepare, 0)
    to_scalars.wait()
    pl.semaphore_wait(barrier, GX * PY)

    def spread(px):
        for gyp in range(GY):
            left, right = [], []
            for slot in range(2):
                hi, lo, hot = node_rows(by_block[blocks[slot, px * GY + gyp]])
                left += [hi, lo]
                right += [hot, hot]
            sums = contract(jnp.concatenate(left, axis=1), jnp.concatenate(right, axis=1))
            for i in range(3):
                for j in range(3):
                    n = i * 3 + j
                    acc[px * 2 + i, gyp * 2 + j] += sums[n * 8 : n * 8 + 8]

    low_half = iota((8, 128), 0) < 4
    above = iota((8, 128), 1) > 0

    def fold(px):
        for x in range(2):
            for yp in range(PY):
                both = []
                for c in range(2):
                    even = acc[px * 2 + x, yp * 4 + c * 2]
                    odd = acc[px * 2 + x, yp * 4 + c * 2 + 1]
                    first = jnp.where(low_half, even, pltpu.roll(odd, 4, axis=0))
                    second = jnp.where(low_half, pltpu.roll(even, 4, axis=0), odd)
                    second = jnp.where(above, pltpu.roll(second, 1, axis=1), 0.0)
                    both.append(first + second)
                part[px, yp, x] = jnp.where(core == 0, both[0], both[1])
                for_sib[px, yp, x] = jnp.where(core == 0, both[1], both[0])

    def sib_copy(px):
        return pltpu.make_async_remote_copy(
            src_ref=for_sib.at[px], dst_ref=from_sib.at[px], send_sem=sib_send.at[px],
            recv_sem=sib_recv.at[px], device_id=sibling, device_id_type=MESH,
        )

    def sum_copy(step, dy):
        px, py, device = peer(step, dy)
        return pltpu.make_async_remote_copy(
            src_ref=part.at[px, py], dst_ref=landed.at[chip], send_sem=sum_send,
            recv_sem=sum_recv, device_id=device, device_id_type=MESH,
        )

    def add_sib(step):
        px = lax.rem(gx + step, GX)
        sib_copy(px).wait_recv()
        part[px] = part[px] + from_sib[px]

    def send_sums(step):
        add_sib(step)
        for dy in range(PY):
            sum_copy(step, dy).start()

    def finish_chunk(px):
        fold(px)
        sib_copy(px).start()

    def chunk(step, carry):
        px = lax.rem(gx + step, GX)
        spread(px)

        @pl.when(step > 0)
        def _():
            finish_chunk(px)

        @pl.when(step > 1)
        def _():
            send_sums(step - 1)

        return carry

    lax.fori_loop(0, GX, chunk, 0)
    finish_chunk(gx)
    send_sums(GX - 1)
    add_sib(0)
    for dy in range(1, PY):
        sum_copy(0, dy).start()
    landed[chip] = part[gx, y]

    many = landed.at[pl.ds(0, GX * PY - 1)]
    pltpu.make_async_copy(many, many, sum_recv).wait()

    def add_up(c, so_far):
        for k in range(8):
            so_far = so_far + landed[c * 8 + k]
        return so_far

    total = lax.fori_loop(0, GX * PY // 8, add_up, jnp.zeros((2, 8, 128), F32))
    for x in range(2):
        mine[x] = update(total[x])

    own = pltpu.make_async_copy(mine, node_vel.at[core, gx, y], vel_send.at[1])
    own.start()

    def vel_copy(step, dy):
        px, py, device = peer(step, dy)
        return pltpu.make_async_remote_copy(
            src_ref=mine, dst_ref=node_vel.at[core, gx, y], send_sem=vel_send.at[0],
            recv_sem=vel_recv.at[gx], device_id=device, device_id_type=MESH,
        )

    def send_vel(step, carry):
        for dy in range(PY):
            vel_copy(step, dy).start()
        return carry

    lax.fori_loop(1, GX, send_vel, 0)
    for dy in range(1, PY):
        vel_copy(0, dy).start()
    own.wait()

    def forward(px):
        return pltpu.make_async_remote_copy(
            src_ref=node_vel.at[core, px], dst_ref=node_vel.at[core, px], send_sem=fwd_send.at[px],
            recv_sem=fwd_recv.at[px], device_id=sibling, device_id_type=MESH,
        )

    def pass_on(step, carry):
        px = lax.rem(gx + GX - step, GX)
        here = node_vel.at[core, px]
        pltpu.make_async_copy(here, here, vel_recv.at[px]).wait()
        forward(px).start()
        return carry

    few = node_vel.at[core, gx, pl.ds(0, PY - 1)]
    pltpu.make_async_copy(few, few, vel_recv.at[gx]).wait()
    forward(gx).start()
    lax.fori_loop(1, GX, pass_on, 0)

    def finish(px, carry):
        sib_copy(px).wait_send()
        forward(px).wait()
        return carry

    lax.fori_loop(0, GX, finish, 0)
    pltpu.make_async_copy(many, many, sum_send).wait()
    pltpu.make_async_copy(many, many, vel_send.at[0]).wait()


def gather_kernel(dest, counts, params, off, strain, cells, mats, node_vel, out_vel, out_strain, out_node, table, rows):
    gx = lax.axis_index("gx")
    gy = lax.axis_index("gy")
    for x in range(2):
        own = node_vel[lax.rem(gy, 2), gx, gy // 2, x]
        for y in range(2):
            for c in range(3):
                out_node[c, x, y : y + 1, :] = own[y * 4 + c : y * 4 + c + 1]

    zeros = jnp.zeros((8, 128), F32)
    for y in range(17):
        table[32, y] = zeros

    low_half = iota((8, 128), 0) < 4
    below = iota((8, 128), 1) < NZ - 1

    def build(gx, carry):
        for x in range(2):
            for gy in range(GY):
                level = node_vel[gy % 2, gx, gy // 2, x]
                lifted = jnp.where(below, pltpu.roll(level, NZ - 1, axis=1), 0.0)
                table[gx * 2 + x, gy * 2] = jnp.where(low_half, level, pltpu.roll(lifted, 4, axis=0))
                table[gx * 2 + x, gy * 2 + 1] = jnp.where(low_half, pltpu.roll(level, 4, axis=0), lifted)
            table[gx * 2 + x, 16] = zeros
        return carry

    lax.fori_loop(0, GX, build, 0)

    def one_group(group, carry):
        at = pl.ds(pl.multiple_of(group * 8, 8), 8)
        cell8 = cells[at, :]
        fx8 = off[0, at, :]
        fy8 = off[1, at, :]
        for s in range(8):
            d = dest[group * 8 + s]
            x0 = d // GY * 2
            y0 = d % GY * 2
            cell = jnp.broadcast_to(cell8[s : s + 1], (8, 128))
            fx = jnp.broadcast_to(fx8[s : s + 1], (8, 128))
            fy = jnp.broadcast_to(fy8[s : s + 1], (8, 128))
            z = cell & (NZ - 1)
            in_x = cell >= 2 * NZ
            in_y = (cell & NZ) != 0
            got = [
                [
                    jnp.take_along_axis(table[x0 + i, y0 + j], z, axis=1, mode="promise_in_bounds")
                    for j in range(3)
                ]
                for i in range(3)
            ]
            side = [
                [jnp.where(in_y, got[i][b + 1], got[i][b]) for b in range(2)] for i in range(3)
            ]
            p = [
                [jnp.where(in_x, side[a + 1][b], side[a][b]) for b in range(2)] for a in range(2)
            ]
            dy = [p[a][1] - p[a][0] for a in range(2)]
            ly = [p[a][0] + fy * dy[a] for a in range(2)]
            gx_term = ly[1] - ly[0]
            rows[s * 24 : s * 24 + 8, :] = ly[0] + fx * gx_term
            rows[s * 24 + 8 : s * 24 + 16, :] = gx_term
            rows[s * 24 + 16 : s * 24 + 24, :] = dy[0] + fx * (dy[1] - dy[0])

        def row(r):
            return rows[pl.ds(r, 8, stride=24), :]

        fz = off[2, at, :]
        speed = []
        grads = []
        for c in range(3):
            v0, v1 = row(c), row(4 + c)
            gz = v1 - v0
            speed.append(v0 + fz * gz)
            gx0, gx1 = row(8 + c), row(12 + c)
            gy0, gy1 = row(16 + c), row(20 + c)
            grads.append((gx0 + fz * (gx1 - gx0), gy0 + fz * (gy1 - gy0), gz))
        live = live_mask(counts, group)
        limit = by_material(params, 2, mats[at, :])
        e = [strain[k, at, :] for k in range(6)]
        trial = [e[k] + DT * grads[k][k] for k in range(3)]
        for k, (r, c) in enumerate(((0, 1), (0, 2), (1, 2))):
            trial.append(e[3 + k] + (0.5 * DT) * (grads[r][c] + grads[c][r]))
        mean = (trial[0] + trial[1] + trial[2]) * (1.0 / 3.0)
        dev = [trial[k] - mean for k in range(3)] + trial[3:]
        square = [x * x for x in dev]
        size = jnp.sqrt(
            square[0] + square[1] + square[2] + 2.0 * (square[3] + square[4] + square[5])
        )
        factor = limit / jnp.maximum(size, limit)
        for k in range(3):
            out_vel[k, at, :] = jnp.where(live, speed[k], 0.0)
            out_strain[k, at, :] = jnp.where(live, mean + factor * dev[k], 0.0)
            out_strain[3 + k, at, :] = jnp.where(live, factor * dev[3 + k], 0.0)
        return carry

    lax.fori_loop(0, NB // 8, one_group, 0)


def scatter(dest, counts, params, off, vel, strain, cells, mats):
    dma = pltpu.SemaphoreType.DMA
    chunks = pltpu.VMEM((GX, PY, 2, 8, 128), F32)
    return pl.pallas_call(
        scatter_kernel,
        out_shape=jax.ShapeDtypeStruct((2, GX, PY, 2, 8, 128), F32),
        in_specs=[SMEM] * 3 + [HBM] * 5,
        out_specs=pl.BlockSpec(memory_space=pl.ANY),
        scratch_shapes=[
            pltpu.VMEM((3, NB, 128), F32),
            pltpu.VMEM((3, NB, 128), F32),
            pltpu.VMEM((6, NB, 128), F32),
            pltpu.VMEM((NB, 128), jnp.int32),
            pltpu.VMEM((NB, 128), jnp.int32),
            pltpu.VMEM((8, 128), jnp.int32),
            pltpu.SMEM((8, 128), jnp.int32),
            pltpu.VMEM(((NB + 1) * ROWS, 128), F32),
            pltpu.VMEM((33, 17, 8, 128), F32),
            chunks, chunks, chunks,
            pltpu.VMEM((2, 8, 128), F32),
            pltpu.VMEM((GX * PY, 2, 8, 128), F32),
            dma((5,)), dma, dma((GX,)), dma((GX,)), dma, dma, dma((2,)), dma((GX,)), dma((GX,)),
            dma((GX,)),
        ],
        compiler_params=pltpu.CompilerParams(
            collective_id=0, has_side_effects=True, vmem_limit_bytes=60 * 1024 * 1024
        ),
        name="scatter",
    )(dest, counts, params, off, vel, strain, cells, mats)


def gather(dest, counts, params, off, strain, cells, mats, node_vel):
    return pl.pallas_call(
        gather_kernel,
        out_shape=(
            jax.ShapeDtypeStruct((3, NB, 128), F32),
            jax.ShapeDtypeStruct((6, NB, 128), F32),
            jax.ShapeDtypeStruct((3, 2, 2, 128), F32),
        ),
        in_specs=[SMEM] * 3 + [VMEM] * 5,
        out_specs=(VMEM, VMEM, VMEM),
        scratch_shapes=[pltpu.VMEM((33, 17, 8, 128), F32), pltpu.VMEM((8 * 24, 128), F32)],
        compiler_params=pltpu.CompilerParams(vmem_limit_bytes=LIMIT),
        name="gather",
    )(dest, counts, params, off, strain, cells, mats, node_vel)


def shards(offsets, velocity, strain, cells, materials, counts, block_dest, material_params):
    off, vel, eps = (jnp.transpose(x, (1, 0, 2)) for x in (offsets, velocity, strain))
    dest = block_dest.reshape(NB)
    node_vel = scatter(dest, counts, material_params, off, vel, eps, cells, materials)
    new_vel, new_eps, own = gather(
        dest, counts, material_params, off, eps, cells, materials, node_vel
    )
    return jnp.transpose(new_vel, (1, 0, 2)), jnp.transpose(new_eps, (1, 0, 2)), own


def solution(mesh):
    blocks = P(("gx", "gy"), None, None)
    rows = P(("gx", "gy"), None)
    in_specs = (blocks, blocks, blocks, rows, rows, P(("gx", "gy")), rows, P())
    out_specs = (blocks, blocks, P(None, "gx", "gy", None))
    return jax.shard_map(shards, mesh=mesh, in_specs=in_specs, out_specs=out_specs, check_vma=False)
```

```python
import jax
import jax.numpy as jnp
from jax import lax
from jax.experimental import pallas as pl
from jax.experimental.pallas import tpu as pltpu
from jax.sharding import PartitionSpec as P

GX = 16
GY = 8
PY = 4
NZ = 128
NB = 192
DT = 0.25
VOLUME = 0.5
GRAVITY = 1.0
FLOOR = 0.25
MESH = pl.DeviceIdType.MESH
F32 = jnp.float32
BF16 = jnp.bfloat16
VMEM = pl.BlockSpec(memory_space=pltpu.VMEM)
SMEM = pl.BlockSpec(memory_space=pltpu.SMEM)
HBM = pl.BlockSpec(memory_space=pltpu.HBM)
LIMIT = 60 * 1024 * 1024
EMPTY = NB
ROWS = 32
LAG = 3
FIRST = 12
UNROLL = 4
FAR_FIRST = sorted(
    ((dz, dx, dy) for dz in range(4) for dx in range(4) for dy in range(4) if dz + dx + dy),
    key=lambda o: -sum(min(d, 4 - d) for d in o),
)


def iota(shape, dim):
    return lax.broadcasted_iota(jnp.int32, shape, dim)


def live_mask(counts, group):
    sub = iota((8, 128), 0)
    limit = jnp.zeros((8, 128), jnp.int32)
    for s in range(8):
        limit = jnp.where(sub == s, counts[group * 8 + s], limit)
    return iota((8, 128), 1) < limit


def by_material(params, row, mats):
    value = jnp.where(mats == 1, params[row, 1], params[row, 0])
    value = jnp.where(mats == 2, params[row, 2], value)
    return jnp.where(mats == 3, params[row, 3], value)


def source_rows(counts, params, off, vel, strain, cells, mats, rows, group):
    at = pl.ds(pl.multiple_of(group * 8, 8), 8)
    live = live_mask(counts, group)
    material = mats[at, :]
    mass = jnp.where(live, by_material(params, 0, material), 0.0)
    shear = jnp.where(live, by_material(params, 1, material), 0.0) * (-DT * VOLUME)
    e = [strain[k, at, :] for k in range(6)]
    trace = shear * (e[0] + e[1] + e[2])
    twice = 2.0 * shear
    xx, yy, zz = (twice * e[k] + trace for k in range(3))
    xy, xz, yz = (twice * e[k] for k in range(3, 6))
    fz = off[2, at, :]
    zero = jnp.zeros((8, 128), F32)
    full = [mass] + [mass * vel[k, at, :] for k in range(3)]
    base = group * (8 * ROWS)

    def put(row, value):
        rows[pl.ds(base + row, 8, stride=ROWS), :] = value

    for q, sz in enumerate((None, xz, yz, zz)):
        upper = fz * full[q]
        if sz is not None:
            upper = upper + sz
        put(4 + q, upper)
        put(q, full[q] - upper)
    for start, terms in ((8, (None, xx, xy, xz)), (16, (None, xy, yy, yz))):
        for q, term in enumerate(terms):
            if term is None:
                put(start + q, zero)
                put(start + 4 + q, zero)
            else:
                upper = fz * term
                put(start + 4 + q, upper)
                put(start + q, term - upper)
    cell = cells[at, :]
    put(24, off[0, at, :])
    put(25, off[1, at, :])
    put(26, (cell & (NZ - 1)).astype(F32))
    put(27, cell.astype(F32))
    put(28, (cell & NZ).astype(F32))
    put(29, fz)


def node_rows(source):
    t, sx, sy = source[0:8], source[8:16], source[16:24]
    fx, fy, z, in_x, in_y = (
        jnp.broadcast_to(source[24 + k : 25 + k], (8, 128)) for k in range(5)
    )
    in_x = in_x >= 2.0 * NZ
    in_y = in_y > 0.0
    u1 = fx * t + sx
    u0 = t - u1
    w1 = fx * sy
    w0 = sy - w1
    c11 = fy * u1 + w1
    c10 = u1 - c11
    c01 = fy * u0 + w0
    c00 = u0 - c01
    d = []
    for low, high in ((c00, c10), (c01, c11)):
        d.append(
            (jnp.where(in_x, 0.0, low), jnp.where(in_x, low, high), jnp.where(in_x, high, 0.0))
        )
    tiles = []
    for i in range(3):
        low, high = d[0][i], d[1][i]
        tiles += [jnp.where(in_y, 0.0, low), jnp.where(in_y, low, high), jnp.where(in_y, high, 0.0)]
    tiles.append(jnp.zeros((8, 128), F32))
    full = jnp.concatenate(tiles, axis=0)
    hi = full.astype(BF16)
    lo = (full - hi.astype(F32)).astype(BF16)
    z16 = jnp.concatenate([z, z], axis=0).astype(BF16)
    z_all = jnp.concatenate([z16] * 8, axis=0)
    depth = iota((128, 128), 0).astype(F32).astype(BF16)
    hot = jnp.where(depth == z_all, jnp.ones((), BF16), jnp.zeros((), BF16))
    return hi, lo, hot


def contract(left, right):
    return lax.dot_general(left, right, (((1,), (1,)), ((), ())), preferred_element_type=F32)


def find_blocks(dest):
    lane = iota((8, 128), 1)
    none = jnp.full((8, 128), EMPTY, jnp.int32)

    def look(step, found):
        first, last = found
        for s in range(8):
            block = step * 8 + s
            back = NB - 1 - block
            last = jnp.where(lane == dest[block], block, last)
            first = jnp.where(lane == dest[back], back, first)
        return first, last

    first, last = lax.fori_loop(0, NB // 8, look, (none, none))
    second = jnp.where(last == first, EMPTY, last)
    return jnp.where(iota((8, 128), 0) == 0, first, second)


def update(total):
    sub = iota((8, 128), 0)
    mass_e = jnp.broadcast_to(total[0:1], (8, 128))
    mass_o = jnp.broadcast_to(total[4:5], (8, 128))
    mass = jnp.where(sub < 4, mass_e, mass_o)
    moved = pltpu.roll(total, 7, axis=0)
    comp = sub % 4
    moved = moved + jnp.where(comp == 2, -DT * GRAVITY, 0.0) * mass
    value = moved / jnp.maximum(mass, FLOOR)
    keep = (comp < 3) & (iota((8, 128), 1) > 0)
    return jnp.where(keep, value, 0.0)


def scatter_kernel(
    dest, counts, params, off_in, vel_in, strain_in, cells_in, mats_in, slots_out, found_out, mine_out,
    off, vel, strain, cells, mats, found, blocks, rows, acc, part, for_sib, from_sib, mine, landed,
    node_vel, table, slots,
    in_sem, found_sem, sib_send, sib_recv, sum_send, sum_recv, vel_send, vel_recv, fwd_send, fwd_recv,
    out_sem, small_sem,
):
    gx = lax.axis_index("gx")
    gy = lax.axis_index("gy")
    core = lax.rem(gy, 2)
    y = gy // 2
    sibling = (gx, gy + 1 - 2 * core)
    chip = gx * PY + y

    def peer(step, dy):
        px = lax.rem(gx + step, GX)
        py = lax.rem(y + dy, PY)
        return px, py, (px, py * 2 + core)

    loads = [
        pltpu.make_async_copy(src, dst, in_sem.at[k])
        for k, (src, dst) in enumerate(
            (
                (off_in, off),
                (vel_in, vel),
                (strain_in, strain),
                (mats_in, mats),
                (cells_in, cells),
            )
        )
    ]
    for load in loads:
        load.start()

    barrier = pltpu.get_barrier_semaphore()
    pl.semaphore_signal(barrier, inc=1, device_id=sibling, device_id_type=MESH)

    def greet(step, carry):
        for dy in range(PY):
            pl.semaphore_signal(barrier, inc=1, device_id=peer(step, dy)[2], device_id_type=MESH)
        return carry

    lax.fori_loop(1, GX, greet, 0)
    for dy in range(1, PY):
        pl.semaphore_signal(barrier, inc=1, device_id=peer(0, dy)[2], device_id_type=MESH)

    found[...] = find_blocks(dest)
    to_scalars = pltpu.make_async_copy(found, blocks, found_sem)
    to_scalars.start()
    found_copy = pltpu.make_async_copy(found, found_out, small_sem.at[0])
    found_copy.start()

    rows[NB * ROWS : (NB + 1) * ROWS, :] = jnp.zeros((ROWS, 128), F32)
    by_block = rows.reshape(NB + 1, ROWS, 128)

    def clear(x, carry):
        acc[x] = jnp.zeros((17, 8, 128), F32)
        return carry

    lax.fori_loop(0, 33, clear, 0)
    for x in range(33):
        table[x, 16] = jnp.zeros((8, 128), F32)
    for yn in range(16):
        table[32, yn] = jnp.zeros((8, 128), F32)
    for load in loads:
        load.wait()

    def prepare(group, carry):
        source_rows(counts, params, off, vel, strain, cells, mats, rows, group)
        return carry

    lax.fori_loop(0, NB // 8, prepare, 0)
    to_scalars.wait()

    def spread(px):
        for gyp in range(GY):
            left, right = [], []
            for slot in range(2):
                hi, lo, hot = node_rows(by_block[blocks[slot, px * GY + gyp]])
                left += [hi, lo]
                right += [hot, hot]
            sums = contract(jnp.concatenate(left, axis=1), jnp.concatenate(right, axis=1))
            for i in range(3):
                for j in range(3):
                    n = i * 3 + j
                    acc[px * 2 + i, gyp * 2 + j] += sums[n * 8 : n * 8 + 8]

    low_half = iota((8, 128), 0) < 4
    above = iota((8, 128), 1) > 0

    def fold(px):
        for x in range(2):
            for yp in range(PY):
                both = []
                for c in range(2):
                    even = acc[px * 2 + x, yp * 4 + c * 2]
                    odd = acc[px * 2 + x, yp * 4 + c * 2 + 1]
                    first = jnp.where(low_half, even, pltpu.roll(odd, 4, axis=0))
                    second = jnp.where(low_half, pltpu.roll(even, 4, axis=0), odd)
                    second = jnp.where(above, pltpu.roll(second, 1, axis=1), 0.0)
                    both.append(first + second)
                part[px, yp, x] = jnp.where(core == 0, both[0], both[1])
                for_sib[px, yp, x] = jnp.where(core == 0, both[1], both[0])

    def sib_copy(px):
        return pltpu.make_async_remote_copy(
            src_ref=for_sib.at[px], dst_ref=from_sib.at[px], send_sem=sib_send.at[px],
            recv_sem=sib_recv.at[px], device_id=sibling, device_id_type=MESH,
        )

    def sum_copy(step, dy):
        px, py, device = peer(step, dy)
        return pltpu.make_async_remote_copy(
            src_ref=part.at[px, py], dst_ref=landed.at[chip], send_sem=sum_send,
            recv_sem=sum_recv, device_id=device, device_id_type=MESH,
        )

    def add_sib(step):
        px = lax.rem(gx + step, GX)
        sib_copy(px).wait_recv()
        part[px] = part[px] + from_sib[px]

    def send_sums(step):
        add_sib(step)
        for dy in range(PY):
            sum_copy(step, dy).start()

    def finish_chunk(px):
        fold(px)
        sib_copy(px).start()

    def chunk(step, carry):
        px = lax.rem(gx + step, GX)
        spread(px)

        @pl.when(step == 1)
        def _():
            pl.semaphore_wait(barrier, GX * PY)

        @pl.when(step > 0)
        def _():
            finish_chunk(px)

        @pl.when(step > LAG)
        def _():
            send_sums(step - LAG)

        return carry

    lax.fori_loop(0, GX, chunk, 0)
    finish_chunk(gx)
    for step in range(GX - LAG, GX):
        send_sums(step)
    add_sib(0)
    for dy in range(1, PY):
        sum_copy(0, dy).start()
    landed[chip] = part[gx, y]

    many = landed.at[pl.ds(0, GX * PY - 1)]
    pltpu.make_async_copy(many, many, sum_recv).wait()

    def add_up(c, so_far):
        for k in range(8):
            so_far = so_far + landed[c * 8 + k]
        return so_far

    total = lax.fori_loop(0, GX * PY // 8, add_up, jnp.zeros((2, 8, 128), F32))
    for x in range(2):
        value = update(total[x])
        for yn in range(2):
            for c in range(3):
                mine[c, x * 2 + yn : x * 2 + yn + 1, :] = value[yn * 4 + c : yn * 4 + c + 1]

    z, x4 = gx // 4, lax.rem(gx, 4)
    turn = 1 - 2 * core
    for dz, dx, dy in FAR_FIRST:
        pz = lax.rem(z + turn * dz + 4, 4)
        px = lax.rem(x4 + turn * dx + 4, 4)
        py = lax.rem(y + turn * dy + 4, 4)
        pltpu.make_async_remote_copy(
            src_ref=mine, dst_ref=node_vel.at[core, gx, y], send_sem=vel_send,
            recv_sem=vel_recv.at[gx], device_id=(pz * 4 + px, py * 2 + core), device_id_type=MESH,
        ).start()
    node_vel[core, gx, y] = mine[...]
    mine_copy = pltpu.make_async_copy(mine, mine_out, small_sem.at[1])
    mine_copy.start()

    def forward(px):
        return pltpu.make_async_remote_copy(
            src_ref=node_vel.at[core, px], dst_ref=node_vel.at[core, px], send_sem=fwd_send.at[px],
            recv_sem=fwd_recv.at[px], device_id=sibling, device_id_type=MESH,
        )

    def order(step):
        return lax.rem(gx + (FIRST + step), GX)

    def pass_on(step):
        px = order(step)

        @pl.when(step == GX - FIRST)
        def _():
            few = node_vel.at[core, px, pl.ds(0, PY - 1)]
            pltpu.make_async_copy(few, few, vel_recv.at[px]).wait()

        @pl.when(step != GX - FIRST)
        def _():
            here = node_vel.at[core, px]
            pltpu.make_async_copy(here, here, vel_recv.at[px]).wait()

        forward(px).start()

    sub = iota((8, 128), 0)
    below = iota((8, 128), 1) < NZ - 1

    def build(step):
        px = order(step)
        forward(px).wait_recv()
        for x in range(2):
            for yn in range(2 * GY):
                gyp = yn // 2
                n = x * 2 + yn % 2
                c0, c1, c2 = (
                    jnp.broadcast_to(node_vel[gyp % 2, px, gyp // 2, c, n : n + 1, :], (8, 128))
                    for c in range(3)
                )
                level = jnp.where(sub % 4 == 0, c0, jnp.where(sub % 4 == 1, c1, c2))
                lifted = jnp.where(below, pltpu.roll(level, NZ - 1, axis=1), 0.0)
                table[px * 2 + x, yn] = jnp.where(low_half, level, lifted)

    def pick(px):
        for gyp in range(GY):
            tiles = [[table[px * 2 + i, gyp * 2 + j] for j in range(3)] for i in range(3)]
            for slot in range(2):
                patch = px * GY + gyp
                misc = by_block[blocks[slot, patch], 24:32, :]
                fx, fy, cz, in_x, in_y, fz = (
                    jnp.broadcast_to(misc[k : k + 1], (8, 128)) for k in range(6)
                )
                cz = cz.astype(jnp.int32)
                in_x = in_x >= 2.0 * NZ
                in_y = in_y > 0.0
                got = [
                    [
                        jnp.take_along_axis(tile, cz, axis=1, mode="promise_in_bounds")
                        for tile in line
                    ]
                    for line in tiles
                ]
                side = [
                    [jnp.where(in_y, line[b + 1], line[b]) for b in range(2)] for line in got
                ]
                p = [
                    [jnp.where(in_x, side[a + 1][b], side[a][b]) for b in range(2)]
                    for a in range(2)
                ]
                dy = [p[a][1] - p[a][0] for a in range(2)]
                ly = [p[a][0] + fy * dy[a] for a in range(2)]
                dx = ly[1] - ly[0]
                value = ly[0] + fx * dx
                dy = dy[0] + fx * (dy[1] - dy[0])
                part_z = jnp.where(low_half, fz, 1.0 - fz)
                dz = pltpu.roll(value, 4, axis=0) - value
                value = value + part_z * dz
                dx = dx + part_z * (pltpu.roll(dx, 4, axis=0) - dx)
                dy = dy + part_z * (pltpu.roll(dy, 4, axis=0) - dy)
                slots[patch * 2 + slot, 0:8, :] = jnp.where(low_half, value, dz)
                slots[patch * 2 + slot, 8:16, :] = jnp.where(low_half, dx, dy)

    def slots_copy(px):
        at = pl.ds(px * (2 * GY), 2 * GY)
        return pltpu.make_async_copy(slots.at[at], slots_out.at[at], out_sem.at[px])

    pass_on(0)
    pass_on(1)
    build(0)

    def gather_chunk(step, carry):
        @pl.when(step < GX - 2)
        def _():
            pass_on(step + 2)

        @pl.when(step < GX - 1)
        def _():
            build(step + 1)

        pick(order(step))
        slots_copy(order(step)).start()
        return carry

    lax.fori_loop(0, GX, gather_chunk, 0)

    def finish(px, carry):
        sib_copy(px).wait_send()
        forward(px).wait_send()
        slots_copy(px).wait()
        return carry

    lax.fori_loop(0, GX, finish, 0)
    pltpu.make_async_copy(many, many, sum_send).wait()
    own_vel = node_vel.at[core, pl.ds(0, GX - 1)]
    pltpu.make_async_copy(own_vel, own_vel, vel_send).wait()
    own_few = node_vel.at[core, 0, pl.ds(0, PY - 1)]
    pltpu.make_async_copy(own_few, own_few, vel_send).wait()
    found_copy.wait()
    mine_copy.wait()


def strain_kernel(
    dest_in, counts_in, params, found_in, strain_in, mats_in, slots_in, mine_in,
    out_vel, out_strain, out_node,
    lines, dest, counts, found, strain, mats, slots, mine, in_sem,
):
    loads = [
        pltpu.make_async_copy(src, dst, in_sem.at[k])
        for k, (src, dst) in enumerate(
            (
                (slots_in, slots),
                (strain_in, strain),
                (mats_in, mats),
                (dest_in, dest),
                (counts_in, counts),
                (found_in, found),
                (mine_in, mine),
            )
        )
    ]
    for load in loads:
        load.start()
    for load in loads:
        load.wait()

    for x in range(2):
        for yn in range(2):
            for c in range(3):
                out_node[c, x, yn : yn + 1, :] = mine[c, x * 2 + yn : x * 2 + yn + 1, :]

    def one_group(group, lane):
        at = pl.ds(pl.multiple_of(group * 8, 8), 8)
        for s in range(8):
            block = group * 8 + s
            d = dest[block]
            slot = d * 2 + jnp.where(found[0, d] == block, 0, 1)
            lines[lane * 128 + s * 16 : lane * 128 + s * 16 + 16, :] = slots[slot]

        def row(r):
            return lines[pl.ds(lane * 128 + r, 8, stride=16), :]

        speed = [row(c) for c in range(3)]
        grads = [(row(8 + c), row(12 + c), -row(4 + c)) for c in range(3)]
        live = live_mask(counts, group)
        limit = by_material(params, 2, mats[at, :])
        e = [strain[k, at, :] for k in range(6)]
        trial = [e[k] + DT * grads[k][k] for k in range(3)]
        for k, (r, c) in enumerate(((0, 1), (0, 2), (1, 2))):
            trial.append(e[3 + k] + (0.5 * DT) * (grads[r][c] + grads[c][r]))
        mean = (trial[0] + trial[1] + trial[2]) * (1.0 / 3.0)
        dev = [trial[k] - mean for k in range(3)] + trial[3:]
        square = [x * x for x in dev]
        size = jnp.sqrt(
            square[0] + square[1] + square[2] + 2.0 * (square[3] + square[4] + square[5])
        )
        factor = limit / jnp.maximum(size, limit)
        for k in range(3):
            out_vel[k, at, :] = jnp.where(live, speed[k], 0.0)
            out_strain[k, at, :] = jnp.where(live, mean + factor * dev[k], 0.0)
            out_strain[3 + k, at, :] = jnp.where(live, factor * dev[3 + k], 0.0)

    def groups(step, carry):
        for lane in range(UNROLL):
            one_group(step * UNROLL + lane, lane)
        return carry

    lax.fori_loop(0, NB // 8 // UNROLL, groups, 0)


def scatter(dest, counts, params, off, vel, strain, cells, mats):
    dma = pltpu.SemaphoreType.DMA
    chunks = pltpu.VMEM((GX, PY, 2, 8, 128), F32)
    return pl.pallas_call(
        scatter_kernel,
        out_shape=(
            jax.ShapeDtypeStruct((2 * GX * GY, 16, 128), F32),
            jax.ShapeDtypeStruct((8, 128), jnp.int32),
            jax.ShapeDtypeStruct((3, 4, 128), F32),
        ),
        in_specs=[SMEM] * 3 + [HBM] * 5,
        out_specs=[pl.BlockSpec(memory_space=pl.ANY)] * 3,
        scratch_shapes=[
            pltpu.VMEM((3, NB, 128), F32),
            pltpu.VMEM((3, NB, 128), F32),
            pltpu.VMEM((6, NB, 128), F32),
            pltpu.VMEM((NB, 128), jnp.int32),
            pltpu.VMEM((NB, 128), jnp.int32),
            pltpu.VMEM((8, 128), jnp.int32),
            pltpu.SMEM((8, 128), jnp.int32),
            pltpu.VMEM(((NB + 1) * ROWS, 128), F32),
            pltpu.VMEM((33, 17, 8, 128), F32),
            chunks, chunks, chunks,
            pltpu.VMEM((3, 4, 128), F32),
            pltpu.VMEM((GX * PY, 2, 8, 128), F32),
            pltpu.VMEM((2, GX, PY, 3, 4, 128), F32),
            pltpu.VMEM((33, 17, 8, 128), F32),
            pltpu.VMEM((2 * GX * GY, 16, 128), F32),
            dma((5,)), dma, dma((GX,)), dma((GX,)), dma, dma, dma, dma((GX,)), dma((GX,)),
            dma((GX,)), dma((GX,)), dma((2,)),
        ],
        compiler_params=pltpu.CompilerParams(
            collective_id=0, has_side_effects=True, vmem_limit_bytes=LIMIT
        ),
        name="scatter",
    )(dest, counts, params, off, vel, strain, cells, mats)


def finish_strain(dest, counts, params, found, strain, mats, slots, mine):
    return pl.pallas_call(
        strain_kernel,
        out_shape=(
            jax.ShapeDtypeStruct((3, NB, 128), F32),
            jax.ShapeDtypeStruct((6, NB, 128), F32),
            jax.ShapeDtypeStruct((3, 2, 2, 128), F32),
        ),
        in_specs=[HBM] * 2 + [SMEM] + [HBM] * 5,
        out_specs=(VMEM, VMEM, VMEM),
        scratch_shapes=[
            pltpu.VMEM((UNROLL * 128, 128), F32),
            pltpu.SMEM((NB,), jnp.int32),
            pltpu.SMEM((NB,), jnp.int32),
            pltpu.SMEM((8, 128), jnp.int32),
            pltpu.VMEM((6, NB, 128), F32),
            pltpu.VMEM((NB, 128), jnp.int32),
            pltpu.VMEM((2 * GX * GY, 16, 128), F32),
            pltpu.VMEM((3, 4, 128), F32),
            pltpu.SemaphoreType.DMA((7,)),
        ],
        compiler_params=pltpu.CompilerParams(vmem_limit_bytes=LIMIT),
        name="strain_map",
    )(dest, counts, params, found, strain, mats, slots, mine)


def shards(offsets, velocity, strain, cells, materials, counts, block_dest, material_params):
    off, vel, eps = (jnp.transpose(x, (1, 0, 2)) for x in (offsets, velocity, strain))
    dest = block_dest.reshape(NB)
    slots, found, mine = scatter(dest, counts, material_params, off, vel, eps, cells, materials)
    new_vel, new_eps, own = finish_strain(
        dest, counts, material_params, found, eps, materials, slots, mine
    )
    return jnp.transpose(new_vel, (1, 0, 2)), jnp.transpose(new_eps, (1, 0, 2)), own


def solution(mesh):
    blocks = P(("gx", "gy"), None, None)
    rows = P(("gx", "gy"), None)
    in_specs = (blocks, blocks, blocks, rows, rows, P(("gx", "gy")), rows, P())
    out_specs = (blocks, blocks, P(None, "gx", "gy", None))
    return jax.shard_map(shards, mesh=mesh, in_specs=in_specs, out_specs=out_specs, check_vma=False)
```

```python
import jax
import jax.numpy as jnp
from jax import lax
from jax.experimental import pallas as pl
from jax.experimental.pallas import tpu as pltpu
from jax.sharding import PartitionSpec as P

GX = 16
GY = 8
PY = 4
NZ = 128
NB = 192
DT = 0.25
VOLUME = 0.5
GRAVITY = 1.0
FLOOR = 0.25
MESH = pl.DeviceIdType.MESH
F32 = jnp.float32
BF16 = jnp.bfloat16
VMEM = pl.BlockSpec(memory_space=pltpu.VMEM)
SMEM = pl.BlockSpec(memory_space=pltpu.SMEM)
HBM = pl.BlockSpec(memory_space=pltpu.HBM)
LIMIT = 60 * 1024 * 1024
EMPTY = NB
ROWS = 32
FIRST = 15
STEPS = 4
UNROLL = 4
SEND_ORDER = (15, 0, 1, 2, 3, 4, 5, 6, 7, 8, 9, 10, 11, 12, 13, 14)


def iota(shape, dim):
    return lax.broadcasted_iota(jnp.int32, shape, dim)


def live_mask(counts, group):
    sub = iota((8, 128), 0)
    limit = jnp.zeros((8, 128), jnp.int32)
    for s in range(8):
        limit = jnp.where(sub == s, counts[group * 8 + s], limit)
    return iota((8, 128), 1) < limit


def by_material(params, row, mats):
    value = jnp.where(mats == 1, params[row, 1], params[row, 0])
    value = jnp.where(mats == 2, params[row, 2], value)
    return jnp.where(mats == 3, params[row, 3], value)


def source_rows(counts, params, off, vel, strain, cells, mats, rows, group):
    at = pl.ds(pl.multiple_of(group * 8, 8), 8)
    live = live_mask(counts, group)
    material = mats[at, :]
    mass = jnp.where(live, by_material(params, 0, material), 0.0)
    shear = jnp.where(live, by_material(params, 1, material), 0.0) * (-DT * VOLUME)
    e = [strain[k, at, :] for k in range(6)]
    trace = shear * (e[0] + e[1] + e[2])
    twice = 2.0 * shear
    xx, yy, zz = (twice * e[k] + trace for k in range(3))
    xy, xz, yz = (twice * e[k] for k in range(3, 6))
    fz = off[2, at, :]
    zero = jnp.zeros((8, 128), F32)
    full = [mass] + [mass * vel[k, at, :] for k in range(3)]
    base = group * (8 * ROWS)

    def put(row, value):
        rows[pl.ds(base + row, 8, stride=ROWS), :] = value

    for q, sz in enumerate((None, xz, yz, zz)):
        upper = fz * full[q]
        if sz is not None:
            upper = upper + sz
        put(4 + q, upper)
        put(q, full[q] - upper)
    for start, terms in ((8, (None, xx, xy, xz)), (16, (None, xy, yy, yz))):
        for q, term in enumerate(terms):
            if term is None:
                put(start + q, zero)
                put(start + 4 + q, zero)
            else:
                upper = fz * term
                put(start + 4 + q, upper)
                put(start + q, term - upper)
    cell = cells[at, :]
    put(24, off[0, at, :])
    put(25, off[1, at, :])
    put(26, (cell & (NZ - 1)).astype(F32))
    put(27, cell.astype(F32))
    put(28, (cell & NZ).astype(F32))
    put(29, fz)


def node_rows(source):
    t, sx, sy = source[0:8], source[8:16], source[16:24]
    fx, fy, z, in_x, in_y = (
        jnp.broadcast_to(source[24 + k : 25 + k], (8, 128)) for k in range(5)
    )
    in_x = in_x >= 2.0 * NZ
    in_y = in_y > 0.0
    u1 = fx * t + sx
    u0 = t - u1
    w1 = fx * sy
    w0 = sy - w1
    c11 = fy * u1 + w1
    c10 = u1 - c11
    c01 = fy * u0 + w0
    c00 = u0 - c01
    d = []
    for low, high in ((c00, c10), (c01, c11)):
        d.append(
            (jnp.where(in_x, 0.0, low), jnp.where(in_x, low, high), jnp.where(in_x, high, 0.0))
        )
    tiles = []
    for i in range(3):
        low, high = d[0][i], d[1][i]
        tiles += [jnp.where(in_y, 0.0, low), jnp.where(in_y, low, high), jnp.where(in_y, high, 0.0)]
    high = [tile.astype(BF16).astype(F32) for tile in tiles]
    low = [tile - part for tile, part in zip(tiles, high)]
    parts = jnp.concatenate(high + low, axis=0).astype(BF16)
    z16 = jnp.concatenate([z, z], axis=0).astype(BF16)
    z_all = jnp.concatenate([z16] * 8, axis=0)
    depth = iota((128, 128), 0).astype(F32).astype(BF16)
    hot = jnp.where(depth == z_all, jnp.ones((), BF16), jnp.zeros((), BF16))
    return parts, hot


def contract(left, right):
    return lax.dot_general(left, right, (((1,), (1,)), ((), ())), preferred_element_type=F32)


def find_blocks(dest):
    lane = iota((8, 128), 1)
    none = jnp.full((8, 128), EMPTY, jnp.int32)

    def look(step, found):
        first, last = found
        for s in range(8):
            block = step * 8 + s
            back = NB - 1 - block
            last = jnp.where(lane == dest[block], block, last)
            first = jnp.where(lane == dest[back], back, first)
        return first, last

    first, last = lax.fori_loop(0, NB // 8, look, (none, none))
    second = jnp.where(last == first, EMPTY, last)
    return jnp.where(iota((8, 128), 0) == 0, first, second)


def update(total):
    sub = iota((8, 128), 0)
    mass_e = jnp.broadcast_to(total[0:1], (8, 128))
    mass_o = jnp.broadcast_to(total[4:5], (8, 128))
    mass = jnp.where(sub < 4, mass_e, mass_o)
    moved = pltpu.roll(total, 7, axis=0)
    comp = sub % 4
    moved = moved + jnp.where(comp == 2, -DT * GRAVITY, 0.0) * mass
    value = moved / jnp.maximum(mass, FLOOR)
    keep = (comp < 3) & (iota((8, 128), 1) > 0)
    return jnp.where(keep, value, 0.0)


def scatter_kernel(
    dest, counts, params, off_in, vel_in, strain_in, cells_in, mats_in, slots_out, found_out, mine_out,
    off, vel, strain, cells, mats, found, blocks, rows, acc, part, for_sib, from_sib, mine, landed,
    node_vel, table, slots,
    in_sem, found_sem, sib_send, sib_recv, sum_send, sum_recv, vel_send, vel_recv, fwd_send, fwd_recv,
    out_sem, small_sem,
):
    gx = lax.axis_index("gx")
    gy = lax.axis_index("gy")
    core = lax.rem(gy, 2)
    y = gy // 2
    sibling = (gx, gy + 1 - 2 * core)
    chip = gx * PY + y

    def peer(step, dy):
        px = lax.rem(gx + step, GX)
        py = lax.rem(y + dy, PY)
        return px, py, (px, py * 2 + core)

    loads = [
        pltpu.make_async_copy(src, dst, in_sem.at[k])
        for k, (src, dst) in enumerate(
            (
                (off_in, off),
                (vel_in, vel),
                (strain_in, strain),
                (mats_in, mats),
                (cells_in, cells),
            )
        )
    ]
    for load in loads:
        load.start()

    barrier = pltpu.get_barrier_semaphore()
    pl.semaphore_signal(barrier, inc=1, device_id=sibling, device_id_type=MESH)

    def greet(step, carry):
        for dy in range(PY):
            pl.semaphore_signal(barrier, inc=1, device_id=peer(step, dy)[2], device_id_type=MESH)
        return carry

    lax.fori_loop(1, GX, greet, 0)
    for dy in range(1, PY):
        pl.semaphore_signal(barrier, inc=1, device_id=peer(0, dy)[2], device_id_type=MESH)

    found[...] = find_blocks(dest)
    to_scalars = pltpu.make_async_copy(found, blocks, found_sem)
    to_scalars.start()
    found_copy = pltpu.make_async_copy(found, found_out, small_sem.at[0])
    found_copy.start()

    rows[NB * ROWS : (NB + 1) * ROWS, :] = jnp.zeros((ROWS, 128), F32)
    by_block = rows.reshape(NB + 1, ROWS, 128)

    def clear(x, carry):
        acc[x] = jnp.zeros((17, 8, 128), F32)
        return carry

    lax.fori_loop(0, 33, clear, 0)
    for x in range(33):
        table[x, 16] = jnp.zeros((8, 128), F32)
    for yn in range(16):
        table[32, yn] = jnp.zeros((8, 128), F32)
    for load in loads:
        load.wait()

    def prepare(group, carry):
        source_rows(counts, params, off, vel, strain, cells, mats, rows, group)
        return carry

    lax.fori_loop(0, NB // 8, prepare, 0)
    to_scalars.wait()

    def spread(px):
        for gyp in range(GY):
            first, second = (
                node_rows(by_block[blocks[slot, px * GY + gyp]]) for slot in range(2)
            )
            sums = contract(
                jnp.concatenate([first[0], second[0]], axis=1),
                jnp.concatenate([first[1], second[1]], axis=1),
            )
            sums = sums[:72] + sums[72:]
            for i in range(3):
                for j in range(3):
                    n = i * 3 + j
                    acc[px * 2 + i, gyp * 2 + j] += sums[n * 8 : n * 8 + 8]

    low_half = iota((8, 128), 0) < 4
    above = iota((8, 128), 1) > 0

    def fold(px):
        for x in range(2):
            for yp in range(PY):
                both = []
                for c in range(2):
                    even = acc[px * 2 + x, yp * 4 + c * 2]
                    odd = acc[px * 2 + x, yp * 4 + c * 2 + 1]
                    first = jnp.where(low_half, even, pltpu.roll(odd, 4, axis=0))
                    second = jnp.where(low_half, pltpu.roll(even, 4, axis=0), odd)
                    second = jnp.where(above, pltpu.roll(second, 1, axis=1), 0.0)
                    both.append(first + second)
                part[px, yp, x] = jnp.where(core == 0, both[0], both[1])
                for_sib[px, yp, x] = jnp.where(core == 0, both[1], both[0])

    def sib_copy(px):
        return pltpu.make_async_remote_copy(
            src_ref=for_sib.at[px], dst_ref=from_sib.at[px], send_sem=sib_send.at[px],
            recv_sem=sib_recv.at[px], device_id=sibling, device_id_type=MESH,
        )

    def sum_copy(step, dy):
        px, py, device = peer(step, dy)
        return pltpu.make_async_remote_copy(
            src_ref=part.at[px, py], dst_ref=landed.at[chip], send_sem=sum_send,
            recv_sem=sum_recv, device_id=device, device_id_type=MESH,
        )

    def add_sib(step):
        px = lax.rem(gx + step, GX)
        sib_copy(px).wait_recv()
        part[px] = part[px] + from_sib[px]

    def send_sums(step):
        add_sib(step)
        for dy in range(PY):
            sum_copy(step, dy).start()

    def finish_chunk(px):
        fold(px)
        sib_copy(px).start()

    def down(step):
        return lax.rem(GX - 1 - step, GX)

    def finish_step(step):
        finish_chunk(lax.rem(gx + down(step), GX))

    def chunks_down(it, carry):
        for u in range(STEPS):
            spread(lax.rem(gx + down(it * STEPS + u), GX))

        @pl.when(it == 0)
        def _():
            pl.semaphore_wait(barrier, GX * PY)

        @pl.when(it > 0)
        def _():
            finish_step(it * STEPS - 1)

        for u in range(STEPS - 1):
            finish_step(it * STEPS + u)

        @pl.when(it > 1)
        def _():
            send_sums(down(it * STEPS - STEPS - 1))

        @pl.when(it > 0)
        def _():
            for u in range(STEPS - 1):
                send_sums(down(it * STEPS - STEPS + u))

        return carry

    lax.fori_loop(0, GX // STEPS, chunks_down, 0)
    finish_chunk(gx)
    for step in range(GX - STEPS - 1, GX - 1):
        send_sums(down(step))
    add_sib(0)
    for dy in range(1, PY):
        sum_copy(0, dy).start()
    landed[chip] = part[gx, y]

    many = landed.at[pl.ds(0, GX * PY - 1)]
    pltpu.make_async_copy(many, many, sum_recv).wait()

    def add_up(c, so_far):
        for k in range(8):
            so_far = so_far + landed[c * 8 + k]
        return so_far

    total = lax.fori_loop(0, GX * PY // 8, add_up, jnp.zeros((2, 8, 128), F32))
    for x in range(2):
        value = update(total[x])
        for yn in range(2):
            for c in range(3):
                mine[c, x * 2 + yn : x * 2 + yn + 1, :] = value[yn * 4 + c : yn * 4 + c + 1]

    def vel_copy(step, dy):
        device = peer(GX - step, dy)[2]
        return pltpu.make_async_remote_copy(
            src_ref=mine, dst_ref=node_vel.at[core, gx, y], send_sem=vel_send,
            recv_sem=vel_recv.at[gx], device_id=device, device_id_type=MESH,
        )

    for step in SEND_ORDER:
        for dy in range(PY):
            if step or dy:
                vel_copy(step, dy).start()
    node_vel[core, gx, y] = mine[...]
    mine_copy = pltpu.make_async_copy(mine, mine_out, small_sem.at[1])
    mine_copy.start()

    def forward(px):
        return pltpu.make_async_remote_copy(
            src_ref=node_vel.at[core, px], dst_ref=node_vel.at[core, px], send_sem=fwd_send.at[px],
            recv_sem=fwd_recv.at[px], device_id=sibling, device_id_type=MESH,
        )

    def order(step):
        return lax.rem(gx + (FIRST + step), GX)

    def pass_on(step):
        px = order(step)

        @pl.when(px == gx)
        def _():
            few = node_vel.at[core, px, pl.ds(0, PY - 1)]
            pltpu.make_async_copy(few, few, vel_recv.at[px]).wait()

        @pl.when(px != gx)
        def _():
            here = node_vel.at[core, px]
            pltpu.make_async_copy(here, here, vel_recv.at[px]).wait()

        forward(px).start()

    sub = iota((8, 128), 0)
    below = iota((8, 128), 1) < NZ - 1

    def build(step):
        px = order(step)
        forward(px).wait_recv()
        for x in range(2):
            for yn in range(2 * GY):
                gyp = yn // 2
                n = x * 2 + yn % 2
                c0, c1, c2 = (
                    jnp.broadcast_to(node_vel[gyp % 2, px, gyp // 2, c, n : n + 1, :], (8, 128))
                    for c in range(3)
                )
                level = jnp.where(sub % 4 == 0, c0, jnp.where(sub % 4 == 1, c1, c2))
                lifted = jnp.where(below, pltpu.roll(level, NZ - 1, axis=1), 0.0)
                table[px * 2 + x, yn] = jnp.where(low_half, level, lifted)

    def pick(px):
        for gyp in range(GY):
            tiles = [[table[px * 2 + i, gyp * 2 + j] for j in range(3)] for i in range(3)]
            for slot in range(2):
                patch = px * GY + gyp
                misc = by_block[blocks[slot, patch], 24:32, :]
                fx, fy, cz, in_x, in_y, fz = (
                    jnp.broadcast_to(misc[k : k + 1], (8, 128)) for k in range(6)
                )
                cz = cz.astype(jnp.int32)
                in_x = in_x >= 2.0 * NZ
                in_y = in_y > 0.0
                got = [
                    [
                        jnp.take_along_axis(tile, cz, axis=1, mode="promise_in_bounds")
                        for tile in line
                    ]
                    for line in tiles
                ]
                side = [
                    [jnp.where(in_y, line[b + 1], line[b]) for b in range(2)] for line in got
                ]
                p = [
                    [jnp.where(in_x, side[a + 1][b], side[a][b]) for b in range(2)]
                    for a in range(2)
                ]
                dy = [p[a][1] - p[a][0] for a in range(2)]
                ly = [p[a][0] + fy * dy[a] for a in range(2)]
                dx = ly[1] - ly[0]
                value = ly[0] + fx * dx
                dy = dy[0] + fx * (dy[1] - dy[0])
                part_z = jnp.where(low_half, fz, 1.0 - fz)
                dz = pltpu.roll(value, 4, axis=0) - value
                value = value + part_z * dz
                dx = dx + part_z * (pltpu.roll(dx, 4, axis=0) - dx)
                dy = dy + part_z * (pltpu.roll(dy, 4, axis=0) - dy)
                slots[patch * 2 + slot, 0:8, :] = jnp.where(low_half, value, dz)
                slots[patch * 2 + slot, 8:16, :] = jnp.where(low_half, dx, dy)

    def slots_copy(px):
        at = pl.ds(px * (2 * GY), 2 * GY)
        return pltpu.make_async_copy(slots.at[at], slots_out.at[at], out_sem.at[px])

    def pick_step(step):
        pick(order(step))
        slots_copy(order(step)).start()

    for step in range(STEPS):
        pass_on(step)

    def gather_chunks(it, carry):
        @pl.when(it < GX // STEPS - 1)
        def _():
            for u in range(STEPS):
                pass_on(it * STEPS + STEPS + u)

        for u in range(STEPS):
            build(it * STEPS + u)

        @pl.when(it > 0)
        def _():
            pick_step(it * STEPS - 1)

        for u in range(STEPS - 1):
            pick_step(it * STEPS + u)
        return carry

    lax.fori_loop(0, GX // STEPS, gather_chunks, 0)
    pick_step(GX - 1)

    def finish(px, carry):
        sib_copy(px).wait_send()
        forward(px).wait_send()
        slots_copy(px).wait()
        return carry

    lax.fori_loop(0, GX, finish, 0)
    pltpu.make_async_copy(many, many, sum_send).wait()
    own_vel = node_vel.at[core, pl.ds(0, GX - 1)]
    pltpu.make_async_copy(own_vel, own_vel, vel_send).wait()
    own_few = node_vel.at[core, 0, pl.ds(0, PY - 1)]
    pltpu.make_async_copy(own_few, own_few, vel_send).wait()
    found_copy.wait()
    mine_copy.wait()


def strain_kernel(
    dest_in, counts_in, params, found_in, strain_in, mats_in, slots_in, mine_in,
    out_vel, out_strain, out_node,
    lines, dest, counts, found, strain, mats, slots, mine, in_sem,
):
    loads = [
        pltpu.make_async_copy(src, dst, in_sem.at[k])
        for k, (src, dst) in enumerate(
            (
                (slots_in, slots),
                (strain_in, strain),
                (mats_in, mats),
                (dest_in, dest),
                (counts_in, counts),
                (found_in, found),
                (mine_in, mine),
            )
        )
    ]
    for load in loads:
        load.start()
    for load in loads:
        load.wait()

    for x in range(2):
        for yn in range(2):
            for c in range(3):
                out_node[c, x, yn : yn + 1, :] = mine[c, x * 2 + yn : x * 2 + yn + 1, :]

    def one_group(group, lane):
        at = pl.ds(pl.multiple_of(group * 8, 8), 8)
        for s in range(8):
            block = group * 8 + s
            d = dest[block]
            slot = d * 2 + jnp.where(found[0, d] == block, 0, 1)
            lines[lane * 128 + s * 16 : lane * 128 + s * 16 + 16, :] = slots[slot]

        def row(r):
            return lines[pl.ds(lane * 128 + r, 8, stride=16), :]

        speed = [row(c) for c in range(3)]
        grads = [(row(8 + c), row(12 + c), -row(4 + c)) for c in range(3)]
        live = live_mask(counts, group)
        limit = by_material(params, 2, mats[at, :])
        e = [strain[k, at, :] for k in range(6)]
        trial = [e[k] + DT * grads[k][k] for k in range(3)]
        for k, (r, c) in enumerate(((0, 1), (0, 2), (1, 2))):
            trial.append(e[3 + k] + (0.5 * DT) * (grads[r][c] + grads[c][r]))
        mean = (trial[0] + trial[1] + trial[2]) * (1.0 / 3.0)
        dev = [trial[k] - mean for k in range(3)] + trial[3:]
        square = [x * x for x in dev]
        size = jnp.sqrt(
            square[0] + square[1] + square[2] + 2.0 * (square[3] + square[4] + square[5])
        )
        factor = limit / jnp.maximum(size, limit)
        for k in range(3):
            out_vel[k, at, :] = jnp.where(live, speed[k], 0.0)
            out_strain[k, at, :] = jnp.where(live, mean + factor * dev[k], 0.0)
            out_strain[3 + k, at, :] = jnp.where(live, factor * dev[3 + k], 0.0)

    def groups(step, carry):
        for lane in range(UNROLL):
            one_group(step * UNROLL + lane, lane)
        return carry

    lax.fori_loop(0, NB // 8 // UNROLL, groups, 0)


def scatter(dest, counts, params, off, vel, strain, cells, mats):
    dma = pltpu.SemaphoreType.DMA
    chunks = pltpu.VMEM((GX, PY, 2, 8, 128), F32)
    return pl.pallas_call(
        scatter_kernel,
        out_shape=(
            jax.ShapeDtypeStruct((2 * GX * GY, 16, 128), F32),
            jax.ShapeDtypeStruct((8, 128), jnp.int32),
            jax.ShapeDtypeStruct((3, 4, 128), F32),
        ),
        in_specs=[SMEM] * 3 + [HBM] * 5,
        out_specs=[pl.BlockSpec(memory_space=pl.ANY)] * 3,
        scratch_shapes=[
            pltpu.VMEM((3, NB, 128), F32),
            pltpu.VMEM((3, NB, 128), F32),
            pltpu.VMEM((6, NB, 128), F32),
            pltpu.VMEM((NB, 128), jnp.int32),
            pltpu.VMEM((NB, 128), jnp.int32),
            pltpu.VMEM((8, 128), jnp.int32),
            pltpu.SMEM((8, 128), jnp.int32),
            pltpu.VMEM(((NB + 1) * ROWS, 128), F32),
            pltpu.VMEM((33, 17, 8, 128), F32),
            chunks, chunks, chunks,
            pltpu.VMEM((3, 4, 128), F32),
            pltpu.VMEM((GX * PY, 2, 8, 128), F32),
            pltpu.VMEM((2, GX, PY, 3, 4, 128), F32),
            pltpu.VMEM((33, 17, 8, 128), F32),
            pltpu.VMEM((2 * GX * GY, 16, 128), F32),
            dma((5,)), dma, dma((GX,)), dma((GX,)), dma, dma, dma, dma((GX,)), dma((GX,)),
            dma((GX,)), dma((GX,)), dma((2,)),
        ],
        compiler_params=pltpu.CompilerParams(
            collective_id=0, has_side_effects=True, vmem_limit_bytes=LIMIT
        ),
        name="scatter",
    )(dest, counts, params, off, vel, strain, cells, mats)


def finish_strain(dest, counts, params, found, strain, mats, slots, mine):
    return pl.pallas_call(
        strain_kernel,
        out_shape=(
            jax.ShapeDtypeStruct((3, NB, 128), F32),
            jax.ShapeDtypeStruct((6, NB, 128), F32),
            jax.ShapeDtypeStruct((3, 2, 2, 128), F32),
        ),
        in_specs=[HBM] * 2 + [SMEM] + [HBM] * 5,
        out_specs=(VMEM, VMEM, VMEM),
        scratch_shapes=[
            pltpu.VMEM((UNROLL * 128, 128), F32),
            pltpu.SMEM((NB,), jnp.int32),
            pltpu.SMEM((NB,), jnp.int32),
            pltpu.SMEM((8, 128), jnp.int32),
            pltpu.VMEM((6, NB, 128), F32),
            pltpu.VMEM((NB, 128), jnp.int32),
            pltpu.VMEM((2 * GX * GY, 16, 128), F32),
            pltpu.VMEM((3, 4, 128), F32),
            pltpu.SemaphoreType.DMA((7,)),
        ],
        compiler_params=pltpu.CompilerParams(vmem_limit_bytes=LIMIT),
        name="strain_map",
    )(dest, counts, params, found, strain, mats, slots, mine)


def shards(offsets, velocity, strain, cells, materials, counts, block_dest, material_params):
    off, vel, eps = (jnp.transpose(x, (1, 0, 2)) for x in (offsets, velocity, strain))
    dest = block_dest.reshape(NB)
    slots, found, mine = scatter(dest, counts, material_params, off, vel, eps, cells, materials)
    new_vel, new_eps, own = finish_strain(
        dest, counts, material_params, found, eps, materials, slots, mine
    )
    return jnp.transpose(new_vel, (1, 0, 2)), jnp.transpose(new_eps, (1, 0, 2)), own


def solution(mesh):
    blocks = P(("gx", "gy"), None, None)
    rows = P(("gx", "gy"), None)
    in_specs = (blocks, blocks, blocks, rows, rows, P(("gx", "gy")), rows, P())
    out_specs = (blocks, blocks, P(None, "gx", "gy", None))
    return jax.shard_map(shards, mesh=mesh, in_specs=in_specs, out_specs=out_specs, check_vma=False)
```

```python
import jax
import jax.numpy as jnp
from jax import lax
from jax.experimental import pallas as pl
from jax.experimental.pallas import tpu as pltpu
from jax.sharding import PartitionSpec as P

GX = 16
GY = 8
PY = 4
NZ = 128
NB = 192
DT = 0.25
VOLUME = 0.5
GRAVITY = 1.0
FLOOR = 0.25
MESH = pl.DeviceIdType.MESH
F32 = jnp.float32
BF16 = jnp.bfloat16
VMEM = pl.BlockSpec(memory_space=pltpu.VMEM)
SMEM = pl.BlockSpec(memory_space=pltpu.SMEM)
HBM = pl.BlockSpec(memory_space=pltpu.HBM)
LIMIT = 60 * 1024 * 1024
EMPTY = NB
ROWS = 32
FIRST = 15
STEPS = 4
UNROLL = 4
SEND_ORDER = (15, 0, 1, 2, 3, 4, 5, 6, 7, 8, 9, 10, 11, 12, 13, 14)


def iota(shape, dim):
    return lax.broadcasted_iota(jnp.int32, shape, dim)


def live_mask(counts, group):
    sub = iota((8, 128), 0)
    limit = jnp.zeros((8, 128), jnp.int32)
    for s in range(8):
        limit = jnp.where(sub == s, counts[group * 8 + s], limit)
    return iota((8, 128), 1) < limit


def by_material(params, row, mats):
    value = jnp.where(mats == 1, params[row, 1], params[row, 0])
    value = jnp.where(mats == 2, params[row, 2], value)
    return jnp.where(mats == 3, params[row, 3], value)


def source_rows(counts, params, off, vel, strain, cells, mats, rows, group):
    at = pl.ds(pl.multiple_of(group * 8, 8), 8)
    live = live_mask(counts, group)
    material = mats[at, :]
    mass = jnp.where(live, by_material(params, 0, material), 0.0)
    shear = jnp.where(live, by_material(params, 1, material), 0.0) * (-DT * VOLUME)
    e = [strain[k, at, :] for k in range(6)]
    trace = shear * (e[0] + e[1] + e[2])
    twice = 2.0 * shear
    xx, yy, zz = (twice * e[k] + trace for k in range(3))
    xy, xz, yz = (twice * e[k] for k in range(3, 6))
    fz = off[2, at, :]
    zero = jnp.zeros((8, 128), F32)
    full = [mass] + [mass * vel[k, at, :] for k in range(3)]
    base = group * (8 * ROWS)

    def put(row, value):
        rows[pl.ds(base + row, 8, stride=ROWS), :] = value

    for q, sz in enumerate((None, xz, yz, zz)):
        upper = fz * full[q]
        if sz is not None:
            upper = upper + sz
        put(4 + q, upper)
        put(q, full[q] - upper)
    for start, terms in ((8, (None, xx, xy, xz)), (16, (None, xy, yy, yz))):
        for q, term in enumerate(terms):
            if term is None:
                put(start + q, zero)
                put(start + 4 + q, zero)
            else:
                upper = fz * term
                put(start + 4 + q, upper)
                put(start + q, term - upper)
    cell = cells[at, :]
    put(24, off[0, at, :])
    put(25, off[1, at, :])
    put(26, (cell & (NZ - 1)).astype(F32))
    put(27, cell.astype(F32))
    put(28, (cell & NZ).astype(F32))
    put(29, fz)


def node_rows(source):
    t, sx, sy = source[0:8], source[8:16], source[16:24]
    fx, fy, z, in_x, in_y = (
        jnp.broadcast_to(source[24 + k : 25 + k], (8, 128)) for k in range(5)
    )
    in_x = in_x >= 2.0 * NZ
    in_y = in_y > 0.0
    u1 = fx * t + sx
    u0 = t - u1
    w1 = fx * sy
    w0 = sy - w1
    c11 = fy * u1 + w1
    c10 = u1 - c11
    c01 = fy * u0 + w0
    c00 = u0 - c01
    d = []
    for low, high in ((c00, c10), (c01, c11)):
        d.append(
            (jnp.where(in_x, 0.0, low), jnp.where(in_x, low, high), jnp.where(in_x, high, 0.0))
        )
    tiles = []
    for i in range(3):
        low, high = d[0][i], d[1][i]
        tiles += [jnp.where(in_y, 0.0, low), jnp.where(in_y, low, high), jnp.where(in_y, high, 0.0)]
    high = [tile.astype(BF16).astype(F32) for tile in tiles]
    low = [tile - part for tile, part in zip(tiles, high)]
    parts = jnp.concatenate(high + low, axis=0).astype(BF16)
    z16 = jnp.concatenate([z, z], axis=0).astype(BF16)
    z_all = jnp.concatenate([z16] * 8, axis=0)
    depth = iota((128, 128), 0).astype(F32).astype(BF16)
    hot = jnp.where(depth == z_all, jnp.ones((), BF16), jnp.zeros((), BF16))
    return parts, hot


def contract(left, right):
    return lax.dot_general(left, right, (((1,), (1,)), ((), ())), preferred_element_type=F32)


def find_blocks(dest):
    lane = iota((8, 128), 1)
    none = jnp.full((8, 128), EMPTY, jnp.int32)

    def look(step, found):
        first, last = found
        for s in range(8):
            block = step * 8 + s
            back = NB - 1 - block
            last = jnp.where(lane == dest[block], block, last)
            first = jnp.where(lane == dest[back], back, first)
        return first, last

    first, last = lax.fori_loop(0, NB // 8, look, (none, none))
    second = jnp.where(last == first, EMPTY, last)
    return jnp.where(iota((8, 128), 0) == 0, first, second)


def update(total):
    sub = iota((8, 128), 0)
    mass_e = jnp.broadcast_to(total[0:1], (8, 128))
    mass_o = jnp.broadcast_to(total[4:5], (8, 128))
    mass = jnp.where(sub < 4, mass_e, mass_o)
    moved = pltpu.roll(total, 7, axis=0)
    comp = sub % 4
    moved = moved + jnp.where(comp == 2, -DT * GRAVITY, 0.0) * mass
    value = moved / jnp.maximum(mass, FLOOR)
    keep = (comp < 3) & (iota((8, 128), 1) > 0)
    return jnp.where(keep, value, 0.0)


def scatter_kernel(
    dest_in, counts_in, params, off_in, vel_in, strain_in, cells_in, mats_in,
    new_vel, new_strain, own,
    dest, counts, lines,
    off, vel, strain, cells, mats, found, blocks, rows, acc, part, for_sib, from_sib, mine, landed,
    node_vel, table, slots,
    in_sem, found_sem, sib_send, sib_recv, sum_send, sum_recv, vel_send, vel_recv, fwd_send, fwd_recv,
):
    gx = lax.axis_index("gx")
    gy = lax.axis_index("gy")
    core = lax.rem(gy, 2)
    y = gy // 2
    sibling = (gx, gy + 1 - 2 * core)
    chip = gx * PY + y

    def peer(step, dy):
        px = lax.rem(gx + step, GX)
        py = lax.rem(y + dy, PY)
        return px, py, (px, py * 2 + core)

    loads = [
        pltpu.make_async_copy(src, dst, in_sem.at[k])
        for k, (src, dst) in enumerate(
            (
                (dest_in, dest),
                (counts_in, counts),
                (off_in, off),
                (vel_in, vel),
                (strain_in, strain),
                (mats_in, mats),
                (cells_in, cells),
            )
        )
    ]
    for load in loads:
        load.start()

    barrier = pltpu.get_barrier_semaphore()
    pl.semaphore_signal(barrier, inc=1, device_id=sibling, device_id_type=MESH)

    def greet(step, carry):
        for dy in range(PY):
            pl.semaphore_signal(barrier, inc=1, device_id=peer(step, dy)[2], device_id_type=MESH)
        return carry

    lax.fori_loop(1, GX, greet, 0)
    for dy in range(1, PY):
        pl.semaphore_signal(barrier, inc=1, device_id=peer(0, dy)[2], device_id_type=MESH)

    loads[0].wait()
    found[...] = find_blocks(dest)
    to_scalars = pltpu.make_async_copy(found, blocks, found_sem)
    to_scalars.start()

    rows[NB * ROWS : (NB + 1) * ROWS, :] = jnp.zeros((ROWS, 128), F32)
    by_block = rows.reshape(NB + 1, ROWS, 128)

    def clear(x, carry):
        acc[x] = jnp.zeros((17, 8, 128), F32)
        return carry

    lax.fori_loop(0, 33, clear, 0)
    for x in range(33):
        table[x, 16] = jnp.zeros((8, 128), F32)
    for yn in range(16):
        table[32, yn] = jnp.zeros((8, 128), F32)
    for load in loads[1:]:
        load.wait()

    def prepare(pair, carry):
        for u in range(2):
            source_rows(counts, params, off, vel, strain, cells, mats, rows, pair * 2 + u)
        return carry

    lax.fori_loop(0, NB // 16, prepare, 0)
    to_scalars.wait()

    def spread(px):
        for gyp in range(GY):
            first, second = (
                node_rows(by_block[blocks[slot, px * GY + gyp]]) for slot in range(2)
            )
            sums = contract(
                jnp.concatenate([first[0], second[0]], axis=1),
                jnp.concatenate([first[1], second[1]], axis=1),
            )
            sums = sums[:72] + sums[72:]
            for i in range(3):
                for j in range(3):
                    n = i * 3 + j
                    acc[px * 2 + i, gyp * 2 + j] += sums[n * 8 : n * 8 + 8]

    low_half = iota((8, 128), 0) < 4
    above = iota((8, 128), 1) > 0

    def fold(px):
        for x in range(2):
            for yp in range(PY):
                both = []
                for c in range(2):
                    even = acc[px * 2 + x, yp * 4 + c * 2]
                    odd = acc[px * 2 + x, yp * 4 + c * 2 + 1]
                    first = jnp.where(low_half, even, pltpu.roll(odd, 4, axis=0))
                    second = jnp.where(low_half, pltpu.roll(even, 4, axis=0), odd)
                    second = jnp.where(above, pltpu.roll(second, 1, axis=1), 0.0)
                    both.append(first + second)
                part[px, yp, x] = jnp.where(core == 0, both[0], both[1])
                for_sib[px, yp, x] = jnp.where(core == 0, both[1], both[0])

    def sib_copy(px):
        return pltpu.make_async_remote_copy(
            src_ref=for_sib.at[px], dst_ref=from_sib.at[px], send_sem=sib_send.at[px],
            recv_sem=sib_recv.at[px], device_id=sibling, device_id_type=MESH,
        )

    def sum_copy(step, dy):
        px, py, device = peer(step, dy)
        return pltpu.make_async_remote_copy(
            src_ref=part.at[px, py], dst_ref=landed.at[chip], send_sem=sum_send,
            recv_sem=sum_recv, device_id=device, device_id_type=MESH,
        )

    def add_sib(step):
        px = lax.rem(gx + step, GX)
        sib_copy(px).wait_recv()
        part[px] = part[px] + from_sib[px]

    def send_sums(step):
        add_sib(step)
        for dy in range(PY):
            sum_copy(step, dy).start()

    def finish_chunk(px):
        fold(px)
        sib_copy(px).start()

    def down(step):
        return lax.rem(GX - 1 - step, GX)

    def finish_step(step):
        finish_chunk(lax.rem(gx + down(step), GX))

    def chunks_down(it, carry):
        for u in range(STEPS):
            spread(lax.rem(gx + down(it * STEPS + u), GX))

        @pl.when(it == 0)
        def _():
            pl.semaphore_wait(barrier, GX * PY)

        @pl.when(it > 0)
        def _():
            finish_step(it * STEPS - 1)

        for u in range(STEPS - 1):
            finish_step(it * STEPS + u)

        @pl.when(it > 1)
        def _():
            send_sums(down(it * STEPS - STEPS - 1))

        @pl.when(it > 0)
        def _():
            for u in range(STEPS - 1):
                send_sums(down(it * STEPS - STEPS + u))

        return carry

    lax.fori_loop(0, GX // STEPS, chunks_down, 0)
    finish_chunk(gx)
    for step in range(GX - STEPS - 1, GX - 1):
        send_sums(down(step))
    add_sib(0)
    for dy in range(1, PY):
        sum_copy(0, dy).start()
    landed[chip] = part[gx, y]

    many = landed.at[pl.ds(0, GX * PY - 1)]
    pltpu.make_async_copy(many, many, sum_recv).wait()

    def add_up(c, so_far):
        for k in range(8):
            so_far = so_far + landed[c * 8 + k]
        return so_far

    total = lax.fori_loop(0, GX * PY // 8, add_up, jnp.zeros((2, 8, 128), F32))
    for x in range(2):
        value = update(total[x])
        for yn in range(2):
            for c in range(3):
                line = value[yn * 4 + c : yn * 4 + c + 1]
                mine[c, x * 2 + yn : x * 2 + yn + 1, :] = line
                own[c, x, yn : yn + 1, :] = line

    def vel_copy(step, dy):
        device = peer(GX - step, dy)[2]
        return pltpu.make_async_remote_copy(
            src_ref=mine, dst_ref=node_vel.at[core, gx, y], send_sem=vel_send,
            recv_sem=vel_recv.at[gx], device_id=device, device_id_type=MESH,
        )

    for step in SEND_ORDER:
        for dy in range(PY):
            if step or dy:
                vel_copy(step, dy).start()
    node_vel[core, gx, y] = mine[...]

    def forward(px):
        return pltpu.make_async_remote_copy(
            src_ref=node_vel.at[core, px], dst_ref=node_vel.at[core, px], send_sem=fwd_send.at[px],
            recv_sem=fwd_recv.at[px], device_id=sibling, device_id_type=MESH,
        )

    def order(step):
        return lax.rem(gx + (FIRST + step), GX)

    def pass_on(step):
        px = order(step)

        @pl.when(px == gx)
        def _():
            few = node_vel.at[core, px, pl.ds(0, PY - 1)]
            pltpu.make_async_copy(few, few, vel_recv.at[px]).wait()

        @pl.when(px != gx)
        def _():
            here = node_vel.at[core, px]
            pltpu.make_async_copy(here, here, vel_recv.at[px]).wait()

        forward(px).start()

    sub = iota((8, 128), 0)
    below = iota((8, 128), 1) < NZ - 1

    def build(step):
        px = order(step)
        forward(px).wait_recv()
        for x in range(2):
            for yn in range(2 * GY):
                gyp = yn // 2
                n = x * 2 + yn % 2
                c0, c1, c2 = (
                    jnp.broadcast_to(node_vel[gyp % 2, px, gyp // 2, c, n : n + 1, :], (8, 128))
                    for c in range(3)
                )
                level = jnp.where(sub % 4 == 0, c0, jnp.where(sub % 4 == 1, c1, c2))
                lifted = jnp.where(below, pltpu.roll(level, NZ - 1, axis=1), 0.0)
                table[px * 2 + x, yn] = jnp.where(low_half, level, lifted)

    def pick(px):
        for gyp in range(GY):
            tiles = [[table[px * 2 + i, gyp * 2 + j] for j in range(3)] for i in range(3)]
            for slot in range(2):
                patch = px * GY + gyp
                misc = by_block[blocks[slot, patch], 24:32, :]
                fx, fy, cz, in_x, in_y, fz = (
                    jnp.broadcast_to(misc[k : k + 1], (8, 128)) for k in range(6)
                )
                cz = cz.astype(jnp.int32)
                in_x = in_x >= 2.0 * NZ
                in_y = in_y > 0.0
                got = [
                    [
                        jnp.take_along_axis(tile, cz, axis=1, mode="promise_in_bounds")
                        for tile in line
                    ]
                    for line in tiles
                ]
                side = [
                    [jnp.where(in_y, line[b + 1], line[b]) for b in range(2)] for line in got
                ]
                p = [
                    [jnp.where(in_x, side[a + 1][b], side[a][b]) for b in range(2)]
                    for a in range(2)
                ]
                dy = [p[a][1] - p[a][0] for a in range(2)]
                ly = [p[a][0] + fy * dy[a] for a in range(2)]
                dx = ly[1] - ly[0]
                value = ly[0] + fx * dx
                dy = dy[0] + fx * (dy[1] - dy[0])
                part_z = jnp.where(low_half, fz, 1.0 - fz)
                dz = pltpu.roll(value, 4, axis=0) - value
                value = value + part_z * dz
                dx = dx + part_z * (pltpu.roll(dx, 4, axis=0) - dx)
                dy = dy + part_z * (pltpu.roll(dy, 4, axis=0) - dy)
                slots[patch * 2 + slot, 0:8, :] = jnp.where(low_half, value, dz)
                slots[patch * 2 + slot, 8:16, :] = jnp.where(low_half, dx, dy)

    def pick_step(step):
        pick(order(step))

    for step in range(STEPS):
        pass_on(step)

    def gather_chunks(it, carry):
        @pl.when(it < GX // STEPS - 1)
        def _():
            for u in range(STEPS):
                pass_on(it * STEPS + STEPS + u)

        for u in range(STEPS):
            build(it * STEPS + u)

        @pl.when(it > 0)
        def _():
            pick_step(it * STEPS - 1)

        for u in range(STEPS - 1):
            pick_step(it * STEPS + u)
        return carry

    lax.fori_loop(0, GX // STEPS, gather_chunks, 0)
    pick_step(GX - 1)

    def one_group(group, lane):
        at = pl.ds(pl.multiple_of(group * 8, 8), 8)
        for s in range(8):
            block = group * 8 + s
            d = dest[block]
            slot = d * 2 + jnp.where(blocks[0, d] == block, 0, 1)
            lines[lane * 128 + s * 16 : lane * 128 + s * 16 + 16, :] = slots[slot]

        def row(r):
            return lines[pl.ds(lane * 128 + r, 8, stride=16), :]

        speed = [row(c) for c in range(3)]
        grads = [(row(8 + c), row(12 + c), -row(4 + c)) for c in range(3)]
        live = live_mask(counts, group)
        limit = by_material(params, 2, mats[at, :])
        e = [strain[k, at, :] for k in range(6)]
        trial = [e[k] + DT * grads[k][k] for k in range(3)]
        for k, (r, c) in enumerate(((0, 1), (0, 2), (1, 2))):
            trial.append(e[3 + k] + (0.5 * DT) * (grads[r][c] + grads[c][r]))
        mean = (trial[0] + trial[1] + trial[2]) * (1.0 / 3.0)
        dev = [trial[k] - mean for k in range(3)] + trial[3:]
        square = [x * x for x in dev]
        size = jnp.sqrt(
            square[0] + square[1] + square[2] + 2.0 * (square[3] + square[4] + square[5])
        )
        factor = limit / jnp.maximum(size, limit)
        for k in range(3):
            new_vel[k, at, :] = jnp.where(live, speed[k], 0.0)
            new_strain[k, at, :] = jnp.where(live, mean + factor * dev[k], 0.0)
            new_strain[3 + k, at, :] = jnp.where(live, factor * dev[3 + k], 0.0)

    def groups(step, carry):
        for lane in range(UNROLL):
            one_group(step * UNROLL + lane, lane)
        return carry

    lax.fori_loop(0, NB // 8 // UNROLL, groups, 0)

    def finish(px, carry):
        sib_copy(px).wait_send()
        forward(px).wait_send()
        return carry

    lax.fori_loop(0, GX, finish, 0)
    pltpu.make_async_copy(many, many, sum_send).wait()
    own_vel = node_vel.at[core, pl.ds(0, GX - 1)]
    pltpu.make_async_copy(own_vel, own_vel, vel_send).wait()
    own_few = node_vel.at[core, 0, pl.ds(0, PY - 1)]
    pltpu.make_async_copy(own_few, own_few, vel_send).wait()


def scatter(dest, counts, params, off, vel, strain, cells, mats):
    dma = pltpu.SemaphoreType.DMA
    chunks = pltpu.VMEM((GX, PY, 2, 8, 128), F32)
    return pl.pallas_call(
        scatter_kernel,
        out_shape=(
            pltpu.VMEM((3, NB, 128), F32),
            pltpu.VMEM((6, NB, 128), F32),
            pltpu.VMEM((3, 2, 2, 128), F32),
        ),
        in_specs=[HBM] * 2 + [SMEM] + [HBM] * 5,
        out_specs=[VMEM] * 3,
        scratch_shapes=[
            pltpu.SMEM((NB,), jnp.int32),
            pltpu.SMEM((NB,), jnp.int32),
            pltpu.VMEM((UNROLL * 128, 128), F32),
            pltpu.VMEM((3, NB, 128), F32),
            pltpu.VMEM((3, NB, 128), F32),
            pltpu.VMEM((6, NB, 128), F32),
            pltpu.VMEM((NB, 128), jnp.int32),
            pltpu.VMEM((NB, 128), jnp.int32),
            pltpu.VMEM((8, 128), jnp.int32),
            pltpu.SMEM((8, 128), jnp.int32),
            pltpu.VMEM(((NB + 1) * ROWS, 128), F32),
            pltpu.VMEM((33, 17, 8, 128), F32),
            chunks, chunks, chunks,
            pltpu.VMEM((3, 4, 128), F32),
            pltpu.VMEM((GX * PY, 2, 8, 128), F32),
            pltpu.VMEM((2, GX, PY, 3, 4, 128), F32),
            pltpu.VMEM((33, 17, 8, 128), F32),
            pltpu.VMEM((2 * GX * GY, 16, 128), F32),
            dma((7,)), dma, dma((GX,)), dma((GX,)), dma, dma, dma, dma((GX,)), dma((GX,)),
            dma((GX,)),
        ],
        compiler_params=pltpu.CompilerParams(
            collective_id=0, has_side_effects=True, vmem_limit_bytes=LIMIT
        ),
        name="scatter",
    )(dest, counts, params, off, vel, strain, cells, mats)


def copy_kernel(a, b, c, x, y, z, sem):
    copies = [
        pltpu.make_async_copy(src, dst, sem.at[k])
        for k, (src, dst) in enumerate(((b, y), (a, x), (c, z)))
    ]
    for copy in copies:
        copy.start()
    for copy in copies:
        copy.wait()


def hand_out(*arrays):
    return pl.pallas_call(
        copy_kernel,
        out_shape=tuple(jax.ShapeDtypeStruct(a.shape, a.dtype) for a in arrays),
        in_specs=[VMEM] * 3,
        out_specs=[HBM] * 3,
        scratch_shapes=[pltpu.SemaphoreType.DMA((3,))],
        compiler_params=pltpu.CompilerParams(vmem_limit_bytes=4 * 1024 * 1024),
        name="hand_out",
    )(*arrays)


def shards(offsets, velocity, strain, cells, materials, counts, block_dest, material_params):
    off, vel, eps = (jnp.transpose(x, (1, 0, 2)) for x in (offsets, velocity, strain))
    dest = block_dest.reshape(NB)
    new_vel, new_eps, own = scatter(dest, counts, material_params, off, vel, eps, cells, materials)
    new_vel, new_eps, own = hand_out(new_vel, new_eps, own)
    return jnp.transpose(new_vel, (1, 0, 2)), jnp.transpose(new_eps, (1, 0, 2)), own


def solution(mesh):
    blocks = P(("gx", "gy"), None, None)
    rows = P(("gx", "gy"), None)
    in_specs = (blocks, blocks, blocks, rows, rows, P(("gx", "gy")), rows, P())
    out_specs = (blocks, blocks, P(None, "gx", "gy", None))
    return jax.shard_map(shards, mesh=mesh, in_specs=in_specs, out_specs=out_specs, check_vma=False)
```

```python
import jax
import jax.numpy as jnp
from jax import lax
from jax.experimental import pallas as pl
from jax.experimental.pallas import tpu as pltpu
from jax.sharding import PartitionSpec as P

GX = 16
GY = 8
PY = 4
NZ = 128
NB = 192
DT = 0.25
VOLUME = 0.5
GRAVITY = 1.0
FLOOR = 0.25
MESH = pl.DeviceIdType.MESH
F32 = jnp.float32
BF16 = jnp.bfloat16
VMEM = pl.BlockSpec(memory_space=pltpu.VMEM)
SMEM = pl.BlockSpec(memory_space=pltpu.SMEM)
HBM = pl.BlockSpec(memory_space=pltpu.HBM)
LIMIT = 60 * 1024 * 1024
EMPTY = NB
ROWS = 40
LINES = 24
PAIR = 4
HOLD = 1
FIRST = 15
STEPS = 4
UNROLL = 4
FAR_FIRST = sorted(
    ((dz, dx, dy) for dz in range(4) for dx in range(4) for dy in range(4) if dz + dx + dy),
    key=lambda o: -sum(min(d, 4 - d) for d in o),
)
SEND_ORDER = (15, 0, 1, 2, 3, 4, 5, 6, 7, 8, 9, 10, 11, 12, 13, 14)


def iota(shape, dim):
    return lax.broadcasted_iota(jnp.int32, shape, dim)


def live_mask(counts, group):
    sub = iota((8, 128), 0)
    limit = jnp.zeros((8, 128), jnp.int32)
    for s in range(8):
        limit = jnp.where(sub == s, counts[group * 8 + s], limit)
    return iota((8, 128), 1) < limit


def by_material(params, row, mats):
    value = jnp.where(mats == 1, params[row, 1], params[row, 0])
    value = jnp.where(mats == 2, params[row, 2], value)
    return jnp.where(mats == 3, params[row, 3], value)


def source_rows(counts, params, off, vel, strain, cells, mats, rows, group):
    at = pl.ds(pl.multiple_of(group * 8, 8), 8)
    live = live_mask(counts, group)
    material = mats[at, :]
    mass = jnp.where(live, by_material(params, 0, material), 0.0)
    shear = jnp.where(live, by_material(params, 1, material), 0.0) * (-DT * VOLUME)
    e = [strain[k, at, :] for k in range(6)]
    trace = shear * (e[0] + e[1] + e[2])
    twice = 2.0 * shear
    xx, yy, zz = (twice * e[k] + trace for k in range(3))
    xy, xz, yz = (twice * e[k] for k in range(3, 6))
    fz = off[2, at, :]
    zero = jnp.zeros((8, 128), F32)
    full = [mass] + [mass * vel[k, at, :] for k in range(3)]
    base = group * (8 * ROWS)

    def put(row, value):
        rows[pl.ds(base + row, 8, stride=ROWS), :] = value

    for q, sz in enumerate((None, xz, yz, zz)):
        upper = fz * full[q]
        if sz is not None:
            upper = upper + sz
        put(4 + q, upper)
        put(q, full[q] - upper)
    for start, terms in ((8, (None, xx, xy, xz)), (16, (None, xy, yy, yz))):
        for q, term in enumerate(terms):
            if term is None:
                put(start + q, zero)
                put(start + 4 + q, zero)
            else:
                upper = fz * term
                put(start + 4 + q, upper)
                put(start + q, term - upper)
    cell = cells[at, :]
    put(24, off[0, at, :])
    put(25, off[1, at, :])
    put(26, (cell & (NZ - 1)).astype(F32))
    put(27, cell.astype(F32))
    put(28, (cell & NZ).astype(F32))
    put(29, fz)


def node_rows(source):
    t, sx, sy = source[0:8], source[8:16], source[16:24]
    fx, fy, z, in_x, in_y = (
        jnp.broadcast_to(source[24 + k : 25 + k], (8, 128)) for k in range(5)
    )
    in_x = in_x >= 2.0 * NZ
    in_y = in_y > 0.0
    u1 = fx * t + sx
    u0 = t - u1
    w1 = fx * sy
    w0 = sy - w1
    c11 = fy * u1 + w1
    c10 = u1 - c11
    c01 = fy * u0 + w0
    c00 = u0 - c01
    d = []
    for low, high in ((c00, c10), (c01, c11)):
        d.append(
            (jnp.where(in_x, 0.0, low), jnp.where(in_x, low, high), jnp.where(in_x, high, 0.0))
        )
    tiles = []
    for i in range(3):
        low, high = d[0][i], d[1][i]
        tiles += [jnp.where(in_y, 0.0, low), jnp.where(in_y, low, high), jnp.where(in_y, high, 0.0)]
    high = [tile.astype(BF16).astype(F32) for tile in tiles]
    low = [tile - part for tile, part in zip(tiles, high)]
    parts = jnp.concatenate(high + low, axis=0).astype(BF16)
    z16 = jnp.concatenate([z, z], axis=0).astype(BF16)
    z_all = jnp.concatenate([z16] * 8, axis=0)
    depth = iota((128, 128), 0).astype(F32).astype(BF16)
    hot = jnp.where(depth == z_all, jnp.ones((), BF16), jnp.zeros((), BF16))
    return parts, hot


def contract(left, right):
    return lax.dot_general(left, right, (((1,), (1,)), ((), ())), preferred_element_type=F32)


def find_blocks(dest):
    lane = iota((8, 128), 1)
    none = jnp.full((8, 128), EMPTY, jnp.int32)

    def look(step, found):
        first, last = found
        for s in range(8):
            block = step * 8 + s
            back = NB - 1 - block
            last = jnp.where(lane == dest[block], block, last)
            first = jnp.where(lane == dest[back], back, first)
        return first, last

    first, last = lax.fori_loop(0, NB // 8, look, (none, none))
    second = jnp.where(last == first, EMPTY, last)
    return jnp.where(iota((8, 128), 0) == 0, first, second)


def update(total):
    sub = iota((8, 128), 0)
    mass_e = jnp.broadcast_to(total[0:1], (8, 128))
    mass_o = jnp.broadcast_to(total[4:5], (8, 128))
    mass = jnp.where(sub < 4, mass_e, mass_o)
    moved = pltpu.roll(total, 7, axis=0)
    comp = sub % 4
    moved = moved + jnp.where(comp == 2, -DT * GRAVITY, 0.0) * mass
    value = moved / jnp.maximum(mass, FLOOR)
    keep = (comp < 3) & (iota((8, 128), 1) > 0)
    return jnp.where(keep, value, 0.0)


def scatter_kernel(
    dest_in, counts_in, params_in, off_in, vel_in, strain_in, cells_in, mats_in,
    new_vel, new_strain, own,
    dest, counts, params, lines,
    off, vel, strain, cells, mats, found, blocks, rows, acc, part, for_sib, from_sib, mine, landed,
    node_vel, table, slots,
    in_sem, found_sem, sib_send, sib_recv, sum_send, sum_recv, vel_send, vel_recv, fwd_send, fwd_recv,
):
    gx = lax.axis_index("gx")
    gy = lax.axis_index("gy")
    core = lax.rem(gy, 2)
    y = gy // 2
    sibling = (gx, gy + 1 - 2 * core)
    chip = gx * PY + y

    def peer(step, dy):
        px = lax.rem(gx + step, GX)
        py = lax.rem(y + dy, PY)
        return px, py, (px, py * 2 + core)

    loads = [
        pltpu.make_async_copy(src, dst, in_sem.at[k])
        for k, (src, dst) in enumerate(
            (
                (dest_in, dest),
                (counts_in, counts),
                (params_in, params),
                (off_in, off),
                (vel_in, vel),
                (strain_in, strain),
                (mats_in, mats),
                (cells_in, cells),
            )
        )
    ]
    for load in loads:
        load.start()

    barrier = pltpu.get_barrier_semaphore()
    for dz, dx, dy in FAR_FIRST:
        near = (lax.rem(gx // 4 + dz, 4) * 4 + lax.rem(gx + dx, 4), lax.rem(y + dy, PY) * 2 + core)
        pl.semaphore_signal(barrier, inc=1, device_id=near, device_id_type=MESH)
    pl.semaphore_signal(barrier, inc=1, device_id=sibling, device_id_type=MESH)

    loads[0].wait()
    found[...] = find_blocks(dest)
    to_scalars = pltpu.make_async_copy(found, blocks, found_sem)
    to_scalars.start()

    rows[NB * ROWS : (NB + 1) * ROWS, :] = jnp.zeros((ROWS, 128), F32)
    by_block = rows.reshape(NB + 1, ROWS, 128)

    def clear(x, carry):
        acc[x] = jnp.zeros((17, 8, 128), F32)
        return carry

    lax.fori_loop(0, 33, clear, 0)
    for x in range(33):
        table[x, 16] = jnp.zeros((8, 128), F32)
    for yn in range(16):
        table[32, yn] = jnp.zeros((8, 128), F32)
    for load in loads[1:]:
        load.wait()

    def prepare(pair, carry):
        for u in range(2):
            source_rows(counts, params, off, vel, strain, cells, mats, rows, pair * 2 + u)
        return carry

    lax.fori_loop(0, NB // 16, prepare, 0)
    to_scalars.wait()

    def spread(px):
        for gyp in range(GY):
            first, second = (
                node_rows(by_block[blocks[slot, px * GY + gyp]]) for slot in range(2)
            )
            sums = contract(
                jnp.concatenate([first[0], second[0]], axis=1),
                jnp.concatenate([first[1], second[1]], axis=1),
            )
            sums = sums[:72] + sums[72:]
            for i in range(3):
                for j in range(3):
                    n = i * 3 + j
                    acc[px * 2 + i, gyp * 2 + j] += sums[n * 8 : n * 8 + 8]

    low_half = iota((8, 128), 0) < 4
    above = iota((8, 128), 1) > 0

    def fold(px):
        for x in range(2):
            for yp in range(PY):
                both = []
                for c in range(2):
                    even = acc[px * 2 + x, yp * 4 + c * 2]
                    odd = acc[px * 2 + x, yp * 4 + c * 2 + 1]
                    first = jnp.where(low_half, even, pltpu.roll(odd, 4, axis=0))
                    second = jnp.where(low_half, pltpu.roll(even, 4, axis=0), odd)
                    second = jnp.where(above, pltpu.roll(second, 1, axis=1), 0.0)
                    both.append(first + second)
                part[px, yp, x] = jnp.where(core == 0, both[0], both[1])
                for_sib[px, yp, x] = jnp.where(core == 0, both[1], both[0])

    def sib_copy(px):
        return pltpu.make_async_remote_copy(
            src_ref=for_sib.at[px], dst_ref=from_sib.at[px], send_sem=sib_send.at[px],
            recv_sem=sib_recv.at[px], device_id=sibling, device_id_type=MESH,
        )

    def sum_copy(step, dy):
        px, py, device = peer(step, dy)
        return pltpu.make_async_remote_copy(
            src_ref=part.at[px, py], dst_ref=landed.at[chip], send_sem=sum_send,
            recv_sem=sum_recv, device_id=device, device_id_type=MESH,
        )

    def add_sib(step):
        px = lax.rem(gx + step, GX)
        sib_copy(px).wait_recv()
        part[px] = part[px] + from_sib[px]

    def send_sums(step):
        add_sib(step)
        for dy in range(PY):
            sum_copy(step, dy).start()

    def down(step):
        return lax.rem(GX - 1 - step, GX)

    def at(step):
        return lax.rem(gx + down(step), GX)

    def send_part(step, carry):
        sib_copy(at(step)).start()
        return carry

    def send_sum(step, carry):
        send_sums(down(step))
        return carry

    def to_sibling(it):
        return jnp.where(it < HOLD, 0, (it + 1) * STEPS - 1)

    def to_owners(it):
        return jnp.where(it <= HOLD, 0, it * STEPS - 1)

    def chunks_down(it, carry):
        for u in range(STEPS):
            spread(at(it * STEPS + u))

        @pl.when(it > 0)
        def _():
            fold(at(it * STEPS - 1))

        for u in range(STEPS - 1):
            fold(at(it * STEPS + u))

        @pl.when(it == HOLD)
        def _():
            pl.semaphore_wait(barrier, GX * PY)

        lax.fori_loop(to_sibling(it - 1), to_sibling(it), send_part, 0)
        lax.fori_loop(to_owners(it - 1), to_owners(it), send_sum, 0)
        return carry

    lax.fori_loop(0, GX // STEPS, chunks_down, 0)
    fold(gx)
    sib_copy(gx).start()
    first = max(0, GX - STEPS - 1) if HOLD < GX // STEPS - 1 else 0
    lax.fori_loop(first, GX - 1, send_sum, 0)
    add_sib(0)
    for dy in range(1, PY):
        sum_copy(0, dy).start()
    landed[chip] = part[gx, y]

    many = landed.at[pl.ds(0, GX * PY - 1)]
    pltpu.make_async_copy(many, many, sum_recv).wait()

    def add_up(c, so_far):
        for k in range(8):
            so_far = so_far + landed[c * 8 + k]
        return so_far

    total = lax.fori_loop(0, GX * PY // 8, add_up, jnp.zeros((2, 8, 128), F32))
    for x in range(2):
        value = update(total[x])
        for yn in range(2):
            for c in range(3):
                line = value[yn * 4 + c : yn * 4 + c + 1]
                mine[c, x * 2 + yn : x * 2 + yn + 1, :] = line
                own[c, x, yn : yn + 1, :] = line

    def vel_copy(step, dy):
        device = peer(GX - step, dy)[2]
        return pltpu.make_async_remote_copy(
            src_ref=mine, dst_ref=node_vel.at[core, gx, y], send_sem=vel_send,
            recv_sem=vel_recv.at[gx], device_id=device, device_id_type=MESH,
        )

    for step in SEND_ORDER:
        for dy in range(PY):
            if step or dy:
                vel_copy(step, dy).start()
    node_vel[core, gx, y] = mine[...]

    def forward(px):
        return pltpu.make_async_remote_copy(
            src_ref=node_vel.at[core, px], dst_ref=node_vel.at[core, px], send_sem=fwd_send.at[px],
            recv_sem=fwd_recv.at[px], device_id=sibling, device_id_type=MESH,
        )

    def order(step):
        return lax.rem(gx + (FIRST + step), GX)

    def pass_on(step):
        px = order(step)

        @pl.when(px == gx)
        def _():
            few = node_vel.at[core, px, pl.ds(0, PY - 1)]
            pltpu.make_async_copy(few, few, vel_recv.at[px]).wait()

        @pl.when(px != gx)
        def _():
            here = node_vel.at[core, px]
            pltpu.make_async_copy(here, here, vel_recv.at[px]).wait()

        forward(px).start()

    sub = iota((8, 128), 0)
    below = iota((8, 128), 1) < NZ - 1

    def build(step):
        px = order(step)
        forward(px).wait_recv()
        for x in range(2):
            for yn in range(2 * GY):
                gyp = yn // 2
                n = x * 2 + yn % 2
                c0, c1, c2 = (
                    jnp.broadcast_to(node_vel[gyp % 2, px, gyp // 2, c, n : n + 1, :], (8, 128))
                    for c in range(3)
                )
                level = jnp.where(sub % 4 == 0, c0, jnp.where(sub % 4 == 1, c1, c2))
                lifted = jnp.where(below, pltpu.roll(level, NZ - 1, axis=1), 0.0)
                table[px * 2 + x, yn] = jnp.where(low_half, level, lifted)

    def pick(px):
        for gyp in range(GY):
            tiles = [[table[px * 2 + i, gyp * 2 + j] for j in range(3)] for i in range(3)]
            for slot in range(2):
                patch = px * GY + gyp
                misc = by_block[blocks[slot, patch], 24:32, :]
                fx, fy, cz, in_x, in_y, fz = (
                    jnp.broadcast_to(misc[k : k + 1], (8, 128)) for k in range(6)
                )
                cz = cz.astype(jnp.int32)
                in_x = in_x >= 2.0 * NZ
                in_y = in_y > 0.0
                got = [
                    [
                        jnp.take_along_axis(tile, cz, axis=1, mode="promise_in_bounds")
                        for tile in line
                    ]
                    for line in tiles
                ]
                side = [
                    [jnp.where(in_y, line[b + 1], line[b]) for b in range(2)] for line in got
                ]
                p = [
                    [jnp.where(in_x, side[a + 1][b], side[a][b]) for b in range(2)]
                    for a in range(2)
                ]
                dy = [p[a][1] - p[a][0] for a in range(2)]
                ly = [p[a][0] + fy * dy[a] for a in range(2)]
                dx = ly[1] - ly[0]
                value = ly[0] + fx * dx
                dy = dy[0] + fx * (dy[1] - dy[0])
                part_z = jnp.where(low_half, fz, 1.0 - fz)
                dz = pltpu.roll(value, 4, axis=0) - value
                value = value + part_z * dz
                dx = dx + part_z * (pltpu.roll(dx, 4, axis=0) - dx)
                dy = dy + part_z * (pltpu.roll(dy, 4, axis=0) - dy)
                slots[patch * 2 + slot, 0:8, :] = jnp.where(low_half, value, dz)
                slots[patch * 2 + slot, 8:16, :] = jnp.where(low_half, dx, dy)

    def pick_step(step):
        pick(order(step))

    for step in range(PAIR):
        pass_on(step)

    def gather_chunks(it, carry):
        @pl.when(it < GX // PAIR - 1)
        def _():
            for u in range(PAIR):
                pass_on((it + 1) * PAIR + u)

        for u in range(PAIR):
            build(it * PAIR + u)

        @pl.when(it > 0)
        def _():
            pick_step(it * PAIR - 1)

        for u in range(PAIR - 1):
            pick_step(it * PAIR + u)
        return carry

    lax.fori_loop(0, GX // PAIR, gather_chunks, 0)
    pick_step(GX - 1)

    def one_group(group, lane):
        at = pl.ds(pl.multiple_of(group * 8, 8), 8)
        for s in range(8):
            block = group * 8 + s
            d = dest[block]
            slot = d * 2 + jnp.where(blocks[0, d] == block, 0, 1)
            first = (lane * 8 + s) * LINES
            lines[first : first + 16, :] = slots[slot]

        def row(r):
            return lines[pl.ds(lane * 8 * LINES + r, 8, stride=LINES), :]

        speed = [row(c) for c in range(3)]
        grads = [(row(8 + c), row(12 + c), -row(4 + c)) for c in range(3)]
        live = live_mask(counts, group)
        limit = by_material(params, 2, mats[at, :])
        e = [strain[k, at, :] for k in range(6)]
        trial = [e[k] + DT * grads[k][k] for k in range(3)]
        for k, (r, c) in enumerate(((0, 1), (0, 2), (1, 2))):
            trial.append(e[3 + k] + (0.5 * DT) * (grads[r][c] + grads[c][r]))
        mean = (trial[0] + trial[1] + trial[2]) * (1.0 / 3.0)
        dev = [trial[k] - mean for k in range(3)] + trial[3:]
        square = [x * x for x in dev]
        size = jnp.sqrt(
            square[0] + square[1] + square[2] + 2.0 * (square[3] + square[4] + square[5])
        )
        factor = limit / jnp.maximum(size, limit)
        for k in range(3):
            new_vel[k, at, :] = jnp.where(live, speed[k], 0.0)
            new_strain[k, at, :] = jnp.where(live, mean + factor * dev[k], 0.0)
            new_strain[3 + k, at, :] = jnp.where(live, factor * dev[3 + k], 0.0)

    def groups(step, carry):
        for lane in range(UNROLL):
            one_group(step * UNROLL + lane, lane)
        return carry

    lax.fori_loop(0, NB // 8 // UNROLL, groups, 0)

    def finish(px, carry):
        sib_copy(px).wait_send()
        forward(px).wait_send()
        return carry

    lax.fori_loop(0, GX, finish, 0)
    pltpu.make_async_copy(many, many, sum_send).wait()
    own_vel = node_vel.at[core, pl.ds(0, GX - 1)]
    pltpu.make_async_copy(own_vel, own_vel, vel_send).wait()
    own_few = node_vel.at[core, 0, pl.ds(0, PY - 1)]
    pltpu.make_async_copy(own_few, own_few, vel_send).wait()


def scatter(dest, counts, params, off, vel, strain, cells, mats):
    dma = pltpu.SemaphoreType.DMA
    chunks = pltpu.VMEM((GX, PY, 2, 8, 128), F32)
    return pl.pallas_call(
        scatter_kernel,
        out_shape=(
            pltpu.VMEM((3, NB, 128), F32),
            pltpu.VMEM((6, NB, 128), F32),
            pltpu.VMEM((3, 2, 2, 128), F32),
        ),
        in_specs=[HBM] * 8,
        out_specs=[VMEM] * 3,
        scratch_shapes=[
            pltpu.SMEM((NB,), jnp.int32),
            pltpu.SMEM((NB,), jnp.int32),
            pltpu.SMEM((3, 4), F32),
            pltpu.VMEM((UNROLL * 8 * LINES, 128), F32),
            pltpu.VMEM((3, NB, 128), F32),
            pltpu.VMEM((3, NB, 128), F32),
            pltpu.VMEM((6, NB, 128), F32),
            pltpu.VMEM((NB, 128), jnp.int32),
            pltpu.VMEM((NB, 128), jnp.int32),
            pltpu.VMEM((8, 128), jnp.int32),
            pltpu.SMEM((8, 128), jnp.int32),
            pltpu.VMEM(((NB + 1) * ROWS, 128), F32),
            pltpu.VMEM((33, 17, 8, 128), F32),
            chunks, chunks, chunks,
            pltpu.VMEM((3, 4, 128), F32),
            pltpu.VMEM((GX * PY, 2, 8, 128), F32),
            pltpu.VMEM((2, GX, PY, 3, 4, 128), F32),
            pltpu.VMEM((33, 17, 8, 128), F32),
            pltpu.VMEM((2 * GX * GY, 16, 128), F32),
            dma((8,)), dma, dma((GX,)), dma((GX,)), dma, dma, dma, dma((GX,)), dma((GX,)),
            dma((GX,)),
        ],
        compiler_params=pltpu.CompilerParams(
            collective_id=0, has_side_effects=True, vmem_limit_bytes=LIMIT
        ),
        name="scatter",
    )(dest, counts, params, off, vel, strain, cells, mats)


def copy_kernel(a, b, c, x, y, z, sem):
    copies = [
        pltpu.make_async_copy(src, dst, sem.at[k])
        for k, (src, dst) in enumerate(((b, y), (a, x), (c, z)))
    ]
    for copy in copies:
        copy.start()
    for copy in copies:
        copy.wait()


def hand_out(*arrays):
    return pl.pallas_call(
        copy_kernel,
        out_shape=tuple(jax.ShapeDtypeStruct(a.shape, a.dtype) for a in arrays),
        in_specs=[VMEM] * 3,
        out_specs=[HBM] * 3,
        scratch_shapes=[pltpu.SemaphoreType.DMA((3,))],
        compiler_params=pltpu.CompilerParams(vmem_limit_bytes=4 * 1024 * 1024),
        name="hand_out",
    )(*arrays)


def shards(offsets, velocity, strain, cells, materials, counts, block_dest, material_params):
    off, vel, eps = (jnp.transpose(x, (1, 0, 2)) for x in (offsets, velocity, strain))
    dest = block_dest.reshape(NB)
    new_vel, new_eps, own = scatter(dest, counts, material_params, off, vel, eps, cells, materials)
    new_vel, new_eps, own = hand_out(new_vel, new_eps, own)
    return jnp.transpose(new_vel, (1, 0, 2)), jnp.transpose(new_eps, (1, 0, 2)), own


def solution(mesh):
    blocks = P(("gx", "gy"), None, None)
    rows = P(("gx", "gy"), None)
    in_specs = (blocks, blocks, blocks, rows, rows, P(("gx", "gy")), rows, P())
    out_specs = (blocks, blocks, P(None, "gx", "gy", None))
    return jax.shard_map(shards, mesh=mesh, in_specs=in_specs, out_specs=out_specs, check_vma=False)
```

```python
import jax
import jax.numpy as jnp
from jax import lax
from jax.experimental import pallas as pl
from jax.experimental.pallas import tpu as pltpu
from jax.sharding import PartitionSpec as P

GX = 16
GY = 8
PY = 4
NZ = 128
NB = 192
DT = 0.25
VOLUME = 0.5
GRAVITY = 1.0
FLOOR = 0.25
MESH = pl.DeviceIdType.MESH
F32 = jnp.float32
BF16 = jnp.bfloat16
VMEM = pl.BlockSpec(memory_space=pltpu.VMEM)
SMEM = pl.BlockSpec(memory_space=pltpu.SMEM)
HBM = pl.BlockSpec(memory_space=pltpu.HBM)
LIMIT = 60 * 1024 * 1024
EMPTY = NB
ROWS = 40
LINES = 24
LINE = 17
BEHIND = 4
HOLD = 1
FIRST = 15
STEPS = 4
UNROLL = 3
FAR_FIRST = sorted(
    ((dz, dx, dy) for dz in range(4) for dx in range(4) for dy in range(4) if dz + dx + dy),
    key=lambda o: -sum(min(d, 4 - d) for d in o),
)
SEND_ORDER = (15, 0, 1, 2, 3, 4, 5, 6, 7, 8, 9, 10, 11, 12, 13, 14)


def iota(shape, dim):
    return lax.broadcasted_iota(jnp.int32, shape, dim)


def live_mask(counts, group):
    sub = iota((8, 128), 0)
    limit = jnp.zeros((8, 128), jnp.int32)
    for s in range(8):
        limit = jnp.where(sub == s, counts[group * 8 + s], limit)
    return iota((8, 128), 1) < limit


def by_material(params, row, mats):
    value = jnp.where(mats == 1, params[row, 1], params[row, 0])
    value = jnp.where(mats == 2, params[row, 2], value)
    return jnp.where(mats == 3, params[row, 3], value)


def source_rows(counts, params, off, vel, strain, cells, mats, rows, group):
    at = pl.ds(pl.multiple_of(group * 8, 8), 8)
    live = live_mask(counts, group)
    material = mats[at, :]
    mass = jnp.where(live, by_material(params, 0, material), 0.0)
    shear = jnp.where(live, by_material(params, 1, material), 0.0) * (-DT * VOLUME)
    e = [strain[k, at, :] for k in range(6)]
    trace = shear * (e[0] + e[1] + e[2])
    twice = 2.0 * shear
    xx, yy, zz = (twice * e[k] + trace for k in range(3))
    xy, xz, yz = (twice * e[k] for k in range(3, 6))
    fz = off[2, at, :]
    zero = jnp.zeros((8, 128), F32)
    full = [mass] + [mass * vel[k, at, :] for k in range(3)]
    base = group * (8 * ROWS)

    def put(row, value):
        rows[pl.ds(base + row, 8, stride=ROWS), :] = value

    for q, sz in enumerate((None, xz, yz, zz)):
        upper = fz * full[q]
        if sz is not None:
            upper = upper + sz
        put(4 + q, upper)
        put(q, full[q] - upper)
    for start, terms in ((8, (None, xx, xy, xz)), (16, (None, xy, yy, yz))):
        for q, term in enumerate(terms):
            if term is None:
                put(start + q, zero)
                put(start + 4 + q, zero)
            else:
                upper = fz * term
                put(start + 4 + q, upper)
                put(start + q, term - upper)
    cell = cells[at, :]
    put(24, off[0, at, :])
    put(25, off[1, at, :])
    put(26, (cell & (NZ - 1)).astype(F32))
    put(27, cell.astype(F32))
    put(28, (cell & NZ).astype(F32))


def node_rows(source):
    t, sx, sy = source[0:8], source[8:16], source[16:24]
    fx, fy, z, in_x, in_y = (
        jnp.broadcast_to(source[24 + k : 25 + k], (8, 128)) for k in range(5)
    )
    in_x = in_x >= 2.0 * NZ
    in_y = in_y > 0.0
    u1 = fx * t + sx
    u0 = t - u1
    w1 = fx * sy
    w0 = sy - w1
    c11 = fy * u1 + w1
    c10 = u1 - c11
    c01 = fy * u0 + w0
    c00 = u0 - c01
    d = []
    for low, high in ((c00, c10), (c01, c11)):
        d.append(
            (jnp.where(in_x, 0.0, low), jnp.where(in_x, low, high), jnp.where(in_x, high, 0.0))
        )
    tiles = []
    for i in range(3):
        low, high = d[0][i], d[1][i]
        tiles += [jnp.where(in_y, 0.0, low), jnp.where(in_y, low, high), jnp.where(in_y, high, 0.0)]
    high = [tile.astype(BF16).astype(F32) for tile in tiles]
    low = [tile - part for tile, part in zip(tiles, high)]
    parts = jnp.concatenate(high + low, axis=0).astype(BF16)
    z16 = jnp.concatenate([z, z], axis=0).astype(BF16)
    z_all = jnp.concatenate([z16] * 8, axis=0)
    depth = iota((128, 128), 0).astype(F32).astype(BF16)
    hot = jnp.where(depth == z_all, jnp.ones((), BF16), jnp.zeros((), BF16))
    return parts, hot


def contract(left, right):
    return lax.dot_general(left, right, (((1,), (1,)), ((), ())), preferred_element_type=F32)


def find_blocks(dest):
    lane = iota((8, 128), 1)
    none = jnp.full((8, 128), EMPTY, jnp.int32)

    def look(step, found):
        first, last = found
        for s in range(8):
            block = step * 8 + s
            back = NB - 1 - block
            last = jnp.where(lane == dest[block], block, last)
            first = jnp.where(lane == dest[back], back, first)
        return first, last

    first, last = lax.fori_loop(0, NB // 8, look, (none, none))
    second = jnp.where(last == first, EMPTY, last)
    return jnp.where(iota((8, 128), 0) == 0, first, second)


def update(total):
    sub = iota((8, 128), 0)
    mass_e = jnp.broadcast_to(total[0:1], (8, 128))
    mass_o = jnp.broadcast_to(total[4:5], (8, 128))
    mass = jnp.where(sub < 4, mass_e, mass_o)
    moved = pltpu.roll(total, 7, axis=0)
    comp = sub % 4
    moved = moved + jnp.where(comp == 2, -DT * GRAVITY, 0.0) * mass
    value = moved / jnp.maximum(mass, FLOOR)
    keep = (comp < 3) & (iota((8, 128), 1) > 0)
    return jnp.where(keep, value, 0.0)


def scatter_kernel(
    dest_in, counts_in, params_in, off_in, vel_in, strain_in, cells_in, mats_in,
    new_vel, new_strain, own,
    dest, counts, params, lines,
    off, vel, strain, cells, mats, found, blocks, rows, acc, part, for_sib, from_sib, mine, landed,
    node_vel, table,
    in_sem, found_sem, sib_send, sib_recv, sum_send, sum_recv, vel_send, vel_recv, fwd_send, fwd_recv,
):
    gx = lax.axis_index("gx")
    gy = lax.axis_index("gy")
    core = lax.rem(gy, 2)
    y = gy // 2
    sibling = (gx, gy + 1 - 2 * core)
    chip = gx * PY + y

    def peer(step, dy):
        px = lax.rem(gx + step, GX)
        py = lax.rem(y + dy, PY)
        return px, py, (px, py * 2 + core)

    loads = [
        pltpu.make_async_copy(src, dst, in_sem.at[k])
        for k, (src, dst) in enumerate(
            (
                (dest_in, dest),
                (counts_in, counts),
                (params_in, params),
                (off_in, off),
                (vel_in, vel),
                (strain_in, strain),
                (mats_in, mats),
                (cells_in, cells),
            )
        )
    ]
    for load in loads:
        load.start()

    barrier = pltpu.get_barrier_semaphore()
    for dz, dx, dy in FAR_FIRST:
        near = (lax.rem(gx // 4 + dz, 4) * 4 + lax.rem(gx + dx, 4), lax.rem(y + dy, PY) * 2 + core)
        pl.semaphore_signal(barrier, inc=1, device_id=near, device_id_type=MESH)
    pl.semaphore_signal(barrier, inc=1, device_id=sibling, device_id_type=MESH)

    loads[0].wait()
    found[...] = find_blocks(dest)
    to_scalars = pltpu.make_async_copy(found, blocks, found_sem)
    to_scalars.start()

    rows[NB * ROWS : (NB + 1) * ROWS, :] = jnp.zeros((ROWS, 128), F32)
    by_block = rows.reshape(NB + 1, ROWS, 128)

    def clear(x, carry):
        acc[x] = jnp.zeros((17, 8, 128), F32)
        return carry

    lax.fori_loop(0, 33, clear, 0)
    for x in range(33):
        table[x * LINE + 16] = jnp.zeros((8, 128), F32)
    for yn in range(16):
        table[32 * LINE + yn] = jnp.zeros((8, 128), F32)
    for load in loads[1:]:
        load.wait()

    def prepare(pair, carry):
        for u in range(2):
            source_rows(counts, params, off, vel, strain, cells, mats, rows, pair * 2 + u)
        return carry

    lax.fori_loop(0, NB // 16, prepare, 0)
    to_scalars.wait()

    def spread(px):
        for gyp in range(GY):
            first, second = (
                node_rows(by_block[blocks[slot, px * GY + gyp]]) for slot in range(2)
            )
            sums = contract(
                jnp.concatenate([first[0], second[0]], axis=1),
                jnp.concatenate([first[1], second[1]], axis=1),
            )
            sums = sums[:72] + sums[72:]
            for i in range(3):
                for j in range(3):
                    n = i * 3 + j
                    acc[px * 2 + i, gyp * 2 + j] += sums[n * 8 : n * 8 + 8]

    low_half = iota((8, 128), 0) < 4
    above = iota((8, 128), 1) > 0

    def fold(px):
        for x in range(2):
            for yp in range(PY):
                both = []
                for c in range(2):
                    even = acc[px * 2 + x, yp * 4 + c * 2]
                    odd = acc[px * 2 + x, yp * 4 + c * 2 + 1]
                    first = jnp.where(low_half, even, pltpu.roll(odd, 4, axis=0))
                    second = jnp.where(low_half, pltpu.roll(even, 4, axis=0), odd)
                    second = jnp.where(above, pltpu.roll(second, 1, axis=1), 0.0)
                    both.append(first + second)
                part[px, yp, x] = jnp.where(core == 0, both[0], both[1])
                for_sib[px, yp, x] = jnp.where(core == 0, both[1], both[0])

    def sib_copy(px):
        return pltpu.make_async_remote_copy(
            src_ref=for_sib.at[px], dst_ref=from_sib.at[px], send_sem=sib_send.at[px],
            recv_sem=sib_recv.at[px], device_id=sibling, device_id_type=MESH,
        )

    def sum_copy(step, dy):
        px, py, device = peer(step, dy)
        return pltpu.make_async_remote_copy(
            src_ref=part.at[px, py], dst_ref=landed.at[chip], send_sem=sum_send,
            recv_sem=sum_recv, device_id=device, device_id_type=MESH,
        )

    def add_sib(step):
        px = lax.rem(gx + step, GX)
        sib_copy(px).wait_recv()
        part[px] = part[px] + from_sib[px]

    def send_sums(step):
        add_sib(step)
        for dy in range(PY):
            sum_copy(step, dy).start()

    def down(step):
        return lax.rem(GX - 1 - step, GX)

    def at(step):
        return lax.rem(gx + down(step), GX)

    def send_part(step, carry):
        sib_copy(at(step)).start()
        return carry

    def send_sum(step, carry):
        send_sums(down(step))
        return carry

    def to_sibling(it):
        return jnp.where(it < HOLD, 0, (it + 1) * STEPS - 1)

    def to_owners(it):
        return jnp.where(it <= HOLD, 0, it * STEPS - 1)

    def chunks_down(it, carry):
        for u in range(STEPS):
            spread(at(it * STEPS + u))

        @pl.when(it > 0)
        def _():
            fold(at(it * STEPS - 1))

        for u in range(STEPS - 1):
            fold(at(it * STEPS + u))

        @pl.when(it == HOLD)
        def _():
            pl.semaphore_wait(barrier, GX * PY)

        lax.fori_loop(to_sibling(it - 1), to_sibling(it), send_part, 0)
        lax.fori_loop(to_owners(it - 1), to_owners(it), send_sum, 0)
        return carry

    lax.fori_loop(0, GX // STEPS, chunks_down, 0)
    fold(gx)
    sib_copy(gx).start()
    first = max(0, GX - STEPS - 1) if HOLD < GX // STEPS - 1 else 0
    lax.fori_loop(first, GX - 1, send_sum, 0)
    add_sib(0)
    for dy in range(1, PY):
        sum_copy(0, dy).start()
    landed[chip] = part[gx, y]

    many = landed.at[pl.ds(0, GX * PY - 1)]
    pltpu.make_async_copy(many, many, sum_recv).wait()

    def add_up(c, so_far):
        for k in range(8):
            so_far = so_far + landed[c * 8 + k]
        return so_far

    total = lax.fori_loop(0, GX * PY // 8, add_up, jnp.zeros((2, 8, 128), F32))
    for x in range(2):
        value = update(total[x])
        for yn in range(2):
            for c in range(3):
                line = value[yn * 4 + c : yn * 4 + c + 1]
                mine[c, x * 2 + yn : x * 2 + yn + 1, :] = line
                own[c, x, yn : yn + 1, :] = line

    def vel_copy(step, dy):
        device = peer(GX - step, dy)[2]
        return pltpu.make_async_remote_copy(
            src_ref=mine, dst_ref=node_vel.at[core, gx, y], send_sem=vel_send,
            recv_sem=vel_recv.at[gx], device_id=device, device_id_type=MESH,
        )

    for step in SEND_ORDER:
        for dy in range(PY):
            if step or dy:
                vel_copy(step, dy).start()
    node_vel[core, gx, y] = mine[...]

    def forward(px):
        return pltpu.make_async_remote_copy(
            src_ref=node_vel.at[core, px], dst_ref=node_vel.at[core, px], send_sem=fwd_send.at[px],
            recv_sem=fwd_recv.at[px], device_id=sibling, device_id_type=MESH,
        )

    def order(step):
        return lax.rem(gx + (FIRST + step), GX)

    def pass_on(step):
        px = order(step)

        @pl.when(px == gx)
        def _():
            few = node_vel.at[core, px, pl.ds(0, PY - 1)]
            pltpu.make_async_copy(few, few, vel_recv.at[px]).wait()

        @pl.when(px != gx)
        def _():
            here = node_vel.at[core, px]
            pltpu.make_async_copy(here, here, vel_recv.at[px]).wait()

        forward(px).start()

    sub = iota((8, 128), 0)
    below = iota((8, 128), 1) < NZ - 1

    def build(step):
        px = order(step)
        forward(px).wait_recv()
        for x in range(2):
            for yn in range(2 * GY):
                gyp = yn // 2
                n = x * 2 + yn % 2
                c0, c1, c2 = (
                    jnp.broadcast_to(node_vel[gyp % 2, px, gyp // 2, c, n : n + 1, :], (8, 128))
                    for c in range(3)
                )
                level = jnp.where(sub % 4 == 0, c0, jnp.where(sub % 4 == 1, c1, c2))
                lifted = jnp.where(below, pltpu.roll(level, NZ - 1, axis=1), 0.0)
                table[(px * 2 + x) * LINE + yn] = jnp.where(low_half, level, lifted)

    def arrive(step, carry):
        pass_on(step)

        @pl.when(step >= BEHIND)
        def _():
            build(step - BEHIND)

        return carry

    lax.fori_loop(0, GX, arrive, 0)
    lax.fori_loop(GX - BEHIND, GX, lambda step, carry: (build(step), carry)[1], 0)

    def pick(group, lane):
        at = pl.ds(pl.multiple_of(group * 8, 8), 8)
        cell8, fx8, fy8 = cells[at, :], off[0, at, :], off[1, at, :]
        for s in range(8):
            d = dest[group * 8 + s]
            corner = d // GY * (2 * LINE) + d % GY * 2
            cell, fx, fy = (jnp.broadcast_to(v[s : s + 1], (8, 128)) for v in (cell8, fx8, fy8))
            cz = cell & (NZ - 1)
            in_x = cell >= 2 * NZ
            in_y = (cell & NZ) != 0
            got = [
                [
                    jnp.take_along_axis(
                        table[corner + (i * LINE + j)], cz, axis=1, mode="promise_in_bounds"
                    )
                    for j in range(3)
                ]
                for i in range(3)
            ]
            side = [[jnp.where(in_y, line[b + 1], line[b]) for b in range(2)] for line in got]
            p = [[jnp.where(in_x, side[a + 1][b], side[a][b]) for b in range(2)] for a in range(2)]
            dy = [p[a][1] - p[a][0] for a in range(2)]
            ly = [p[a][0] + fy * dy[a] for a in range(2)]
            dx = ly[1] - ly[0]
            first = (lane * 8 + s) * LINES
            lines[first : first + 8, :] = ly[0] + fx * dx
            lines[first + 8 : first + 16, :] = dx
            lines[first + 16 : first + 24, :] = dy[0] + fx * (dy[1] - dy[0])

    def one_group(group, lane):
        at = pl.ds(pl.multiple_of(group * 8, 8), 8)

        def row(r):
            return lines[pl.ds(lane * 8 * LINES + r, 8, stride=LINES), :]

        fz = off[2, at, :]
        speed = []
        grads = []
        for c in range(3):
            v0 = row(c)
            dz = row(4 + c) - v0
            speed.append(v0 + fz * dz)
            dx, dy = row(8 + c), row(16 + c)
            grads.append((dx + fz * (row(12 + c) - dx), dy + fz * (row(20 + c) - dy), dz))
        live = live_mask(counts, group)
        limit = by_material(params, 2, mats[at, :])
        e = [strain[k, at, :] for k in range(6)]
        trial = [e[k] + DT * grads[k][k] for k in range(3)]
        for k, (r, c) in enumerate(((0, 1), (0, 2), (1, 2))):
            trial.append(e[3 + k] + (0.5 * DT) * (grads[r][c] + grads[c][r]))
        mean = (trial[0] + trial[1] + trial[2]) * (1.0 / 3.0)
        dev = [trial[k] - mean for k in range(3)] + trial[3:]
        square = [x * x for x in dev]
        size = jnp.sqrt(
            square[0] + square[1] + square[2] + 2.0 * (square[3] + square[4] + square[5])
        )
        factor = limit / jnp.maximum(size, limit)
        for k in range(3):
            new_vel[k, at, :] = jnp.where(live, speed[k], 0.0)
            new_strain[k, at, :] = jnp.where(live, mean + factor * dev[k], 0.0)
            new_strain[3 + k, at, :] = jnp.where(live, factor * dev[3 + k], 0.0)

    def pick_step(step, half):
        for lane in range(UNROLL):
            pick(step * UNROLL + lane, half * UNROLL + lane)

    def map_step(step, half):
        for lane in range(UNROLL):
            one_group(step * UNROLL + lane, half * UNROLL + lane)

    def groups(pair, carry):
        for half in range(2):
            pick_step(pair * 2 + half + 1, 1 - half)
            map_step(pair * 2 + half, half)
        return carry

    last = NB // 8 // UNROLL - 1
    pick_step(0, 0)
    lax.fori_loop(0, last // 2, groups, 0)
    pick_step(last, 1)
    map_step(last - 1, 0)
    map_step(last, 1)

    def finish(px, carry):
        sib_copy(px).wait_send()
        forward(px).wait_send()
        return carry

    lax.fori_loop(0, GX, finish, 0)
    pltpu.make_async_copy(many, many, sum_send).wait()
    own_vel = node_vel.at[core, pl.ds(0, GX - 1)]
    pltpu.make_async_copy(own_vel, own_vel, vel_send).wait()
    own_few = node_vel.at[core, 0, pl.ds(0, PY - 1)]
    pltpu.make_async_copy(own_few, own_few, vel_send).wait()


def scatter(dest, counts, params, off, vel, strain, cells, mats):
    dma = pltpu.SemaphoreType.DMA
    chunks = pltpu.VMEM((GX, PY, 2, 8, 128), F32)
    return pl.pallas_call(
        scatter_kernel,
        out_shape=(
            pltpu.VMEM((3, NB, 128), F32),
            pltpu.VMEM((6, NB, 128), F32),
            pltpu.VMEM((3, 2, 2, 128), F32),
        ),
        in_specs=[HBM] * 8,
        out_specs=[VMEM] * 3,
        scratch_shapes=[
            pltpu.SMEM((NB,), jnp.int32),
            pltpu.SMEM((NB,), jnp.int32),
            pltpu.SMEM((3, 4), F32),
            pltpu.VMEM((2 * UNROLL * 8 * LINES, 128), F32),
            pltpu.VMEM((3, NB, 128), F32),
            pltpu.VMEM((3, NB, 128), F32),
            pltpu.VMEM((6, NB, 128), F32),
            pltpu.VMEM((NB, 128), jnp.int32),
            pltpu.VMEM((NB, 128), jnp.int32),
            pltpu.VMEM((8, 128), jnp.int32),
            pltpu.SMEM((8, 128), jnp.int32),
            pltpu.VMEM(((NB + 1) * ROWS, 128), F32),
            pltpu.VMEM((33, 17, 8, 128), F32),
            chunks, chunks, chunks,
            pltpu.VMEM((3, 4, 128), F32),
            pltpu.VMEM((GX * PY, 2, 8, 128), F32),
            pltpu.VMEM((2, GX, PY, 3, 4, 128), F32),
            pltpu.VMEM((33 * LINE, 8, 128), F32),
            dma((8,)), dma, dma((GX,)), dma((GX,)), dma, dma, dma, dma((GX,)), dma((GX,)),
            dma((GX,)),
        ],
        compiler_params=pltpu.CompilerParams(
            collective_id=0, has_side_effects=True, vmem_limit_bytes=LIMIT
        ),
        name="scatter",
    )(dest, counts, params, off, vel, strain, cells, mats)


def copy_kernel(a, b, c, x, y, z, sem):
    copies = [
        pltpu.make_async_copy(src, dst, sem.at[k])
        for k, (src, dst) in enumerate(((b, y), (a, x), (c, z)))
    ]
    for copy in copies:
        copy.start()
    for copy in copies:
        copy.wait()


def hand_out(*arrays):
    return pl.pallas_call(
        copy_kernel,
        out_shape=tuple(jax.ShapeDtypeStruct(a.shape, a.dtype) for a in arrays),
        in_specs=[VMEM] * 3,
        out_specs=[HBM] * 3,
        scratch_shapes=[pltpu.SemaphoreType.DMA((3,))],
        compiler_params=pltpu.CompilerParams(vmem_limit_bytes=4 * 1024 * 1024),
        name="hand_out",
    )(*arrays)


def shards(offsets, velocity, strain, cells, materials, counts, block_dest, material_params):
    off, vel, eps = (jnp.transpose(x, (1, 0, 2)) for x in (offsets, velocity, strain))
    dest = block_dest.reshape(NB)
    new_vel, new_eps, own = scatter(dest, counts, material_params, off, vel, eps, cells, materials)
    new_vel, new_eps, own = hand_out(new_vel, new_eps, own)
    return jnp.transpose(new_vel, (1, 0, 2)), jnp.transpose(new_eps, (1, 0, 2)), own


def solution(mesh):
    blocks = P(("gx", "gy"), None, None)
    rows = P(("gx", "gy"), None)
    in_specs = (blocks, blocks, blocks, rows, rows, P(("gx", "gy")), rows, P())
    out_specs = (blocks, blocks, P(None, "gx", "gy", None))
    return jax.shard_map(shards, mesh=mesh, in_specs=in_specs, out_specs=out_specs, check_vma=False)
```

```python
import jax
import jax.numpy as jnp
from jax import lax
from jax.experimental import pallas as pl
from jax.experimental.pallas import tpu as pltpu
from jax.sharding import PartitionSpec as P

GX = 16
GY = 8
PY = 4
NZ = 128
NB = 192
DT = 0.25
VOLUME = 0.5
GRAVITY = 1.0
FLOOR = 0.25
MESH = pl.DeviceIdType.MESH
F32 = jnp.float32
BF16 = jnp.bfloat16
VMEM = pl.BlockSpec(memory_space=pltpu.VMEM)
SMEM = pl.BlockSpec(memory_space=pltpu.SMEM)
HBM = pl.BlockSpec(memory_space=pltpu.HBM)
LIMIT = 60 * 1024 * 1024
EMPTY = NB
ROWS = 40
LINES = 24
LINE = 17
BEHIND = 8
HOLD = 1
STEPS = 4
UNROLL = 3
FAR_FIRST = sorted(
    ((dz, dx, dy) for dz in range(4) for dx in range(4) for dy in range(4) if dz + dx + dy),
    key=lambda o: -sum(min(d, 4 - d) for d in o),
)


def iota(shape, dim):
    return lax.broadcasted_iota(jnp.int32, shape, dim)


def live_mask(counts, group):
    sub = iota((8, 128), 0)
    limit = jnp.zeros((8, 128), jnp.int32)
    for s in range(8):
        limit = jnp.where(sub == s, counts[group * 8 + s], limit)
    return iota((8, 128), 1) < limit


def by_material(params, row, mats):
    value = jnp.where(mats == 1, params[row, 1], params[row, 0])
    value = jnp.where(mats == 2, params[row, 2], value)
    return jnp.where(mats == 3, params[row, 3], value)


def source_rows(counts, params, off, vel, strain, cells, mats, rows, group):
    at = pl.ds(pl.multiple_of(group * 8, 8), 8)
    live = live_mask(counts, group)
    material = mats[at, :]
    mass = jnp.where(live, by_material(params, 0, material), 0.0)
    shear = jnp.where(live, by_material(params, 1, material), 0.0) * (-DT * VOLUME)
    e = [strain[k, at, :] for k in range(6)]
    trace = shear * (e[0] + e[1] + e[2])
    twice = 2.0 * shear
    xx, yy, zz = (twice * e[k] + trace for k in range(3))
    xy, xz, yz = (twice * e[k] for k in range(3, 6))
    fz = off[2, at, :]
    zero = jnp.zeros((8, 128), F32)
    full = [mass] + [mass * vel[k, at, :] for k in range(3)]
    base = group * (8 * ROWS)

    def put(row, value):
        rows[pl.ds(base + row, 8, stride=ROWS), :] = value

    for q, sz in enumerate((None, xz, yz, zz)):
        upper = fz * full[q]
        if sz is not None:
            upper = upper + sz
        put(4 + q, upper)
        put(q, full[q] - upper)
    for start, terms in ((8, (None, xx, xy, xz)), (16, (None, xy, yy, yz))):
        for q, term in enumerate(terms):
            if term is None:
                put(start + q, zero)
                put(start + 4 + q, zero)
            else:
                upper = fz * term
                put(start + 4 + q, upper)
                put(start + q, term - upper)
    cell = cells[at, :]
    put(24, off[0, at, :])
    put(25, off[1, at, :])
    put(26, (cell & (NZ - 1)).astype(F32))
    put(27, cell.astype(F32))
    put(28, (cell & NZ).astype(F32))


def node_rows(source):
    t, sx, sy = source[0:8], source[8:16], source[16:24]
    fx, fy, z, in_x, in_y = (
        jnp.broadcast_to(source[24 + k : 25 + k], (8, 128)) for k in range(5)
    )
    in_x = in_x >= 2.0 * NZ
    in_y = in_y > 0.0
    u1 = fx * t + sx
    u0 = t - u1
    w1 = fx * sy
    w0 = sy - w1
    c11 = fy * u1 + w1
    c10 = u1 - c11
    c01 = fy * u0 + w0
    c00 = u0 - c01
    d = []
    for low, high in ((c00, c10), (c01, c11)):
        d.append(
            (jnp.where(in_x, 0.0, low), jnp.where(in_x, low, high), jnp.where(in_x, high, 0.0))
        )
    tiles = []
    for i in range(3):
        low, high = d[0][i], d[1][i]
        tiles += [jnp.where(in_y, 0.0, low), jnp.where(in_y, low, high), jnp.where(in_y, high, 0.0)]
    high = [tile.astype(BF16).astype(F32) for tile in tiles]
    low = [tile - part for tile, part in zip(tiles, high)]
    parts = jnp.concatenate(high + low, axis=0).astype(BF16)
    z16 = jnp.concatenate([z, z], axis=0).astype(BF16)
    z_all = jnp.concatenate([z16] * 8, axis=0)
    depth = iota((128, 128), 0).astype(F32).astype(BF16)
    hot = jnp.where(depth == z_all, jnp.ones((), BF16), jnp.zeros((), BF16))
    return parts, hot


def contract(left, right):
    return lax.dot_general(left, right, (((1,), (1,)), ((), ())), preferred_element_type=F32)


def find_blocks(dest):
    lane = iota((8, 128), 1)
    none = jnp.full((8, 128), EMPTY, jnp.int32)

    def look(step, found):
        first, last = found
        for s in range(8):
            block = step * 8 + s
            back = NB - 1 - block
            last = jnp.where(lane == dest[block], block, last)
            first = jnp.where(lane == dest[back], back, first)
        return first, last

    first, last = lax.fori_loop(0, NB // 8, look, (none, none))
    second = jnp.where(last == first, EMPTY, last)
    return jnp.where(iota((8, 128), 0) == 0, first, second)


def update(total):
    sub = iota((8, 128), 0)
    mass_e = jnp.broadcast_to(total[0:1], (8, 128))
    mass_o = jnp.broadcast_to(total[4:5], (8, 128))
    mass = jnp.where(sub < 4, mass_e, mass_o)
    moved = pltpu.roll(total, 7, axis=0)
    comp = sub % 4
    moved = moved + jnp.where(comp == 2, -DT * GRAVITY, 0.0) * mass
    value = moved / jnp.maximum(mass, FLOOR)
    keep = (comp < 3) & (iota((8, 128), 1) > 0)
    return jnp.where(keep, value, 0.0)


def scatter_kernel(
    dest_in, counts_in, params_in, off_in, vel_in, strain_in, cells_in, mats_in,
    new_vel, new_strain, own,
    dest, counts, params, lines,
    off, vel, strain, cells, mats, found, blocks, rows, acc, part, for_sib, from_sib, mine, landed,
    node_vel, table,
    in_sem, found_sem, sib_send, sib_recv, sum_send, sum_recv, vel_send, vel_recv, fwd_send, fwd_recv,
):
    gx = lax.axis_index("gx")
    gy = lax.axis_index("gy")
    core = lax.rem(gy, 2)
    y = gy // 2
    sibling = (gx, gy + 1 - 2 * core)
    chip = gx * PY + y

    def peer(step, dy):
        px = lax.rem(gx + step, GX)
        py = lax.rem(y + dy, PY)
        return px, py, (px, py * 2 + core)

    loads = [
        pltpu.make_async_copy(src, dst, in_sem.at[k])
        for k, (src, dst) in enumerate(
            (
                (dest_in, dest),
                (counts_in, counts),
                (params_in, params),
                (off_in, off),
                (vel_in, vel),
                (strain_in, strain),
                (mats_in, mats),
                (cells_in, cells),
            )
        )
    ]
    for load in loads:
        load.start()

    barrier = pltpu.get_barrier_semaphore()
    for dz, dx, dy in FAR_FIRST:
        near = (lax.rem(gx // 4 + dz, 4) * 4 + lax.rem(gx + dx, 4), lax.rem(y + dy, PY) * 2 + core)
        pl.semaphore_signal(barrier, inc=1, device_id=near, device_id_type=MESH)
    pl.semaphore_signal(barrier, inc=1, device_id=sibling, device_id_type=MESH)

    loads[0].wait()
    found[...] = find_blocks(dest)
    to_scalars = pltpu.make_async_copy(found, blocks, found_sem)
    to_scalars.start()

    rows[NB * ROWS : (NB + 1) * ROWS, :] = jnp.zeros((ROWS, 128), F32)
    by_block = rows.reshape(NB + 1, ROWS, 128)

    def clear(x, carry):
        acc[x] = jnp.zeros((17, 8, 128), F32)
        return carry

    lax.fori_loop(0, 33, clear, 0)
    for x in range(33):
        table[x * LINE + 16] = jnp.zeros((8, 128), F32)
    for yn in range(16):
        table[32 * LINE + yn] = jnp.zeros((8, 128), F32)
    for load in loads[1:]:
        load.wait()

    def prepare(pair, carry):
        for u in range(2):
            source_rows(counts, params, off, vel, strain, cells, mats, rows, pair * 2 + u)
        return carry

    lax.fori_loop(0, NB // 16, prepare, 0)
    to_scalars.wait()

    def spread(px):
        for gyp in range(GY):
            first, second = (
                node_rows(by_block[blocks[slot, px * GY + gyp]]) for slot in range(2)
            )
            sums = contract(
                jnp.concatenate([first[0], second[0]], axis=1),
                jnp.concatenate([first[1], second[1]], axis=1),
            )
            sums = sums[:72] + sums[72:]
            for i in range(3):
                for j in range(3):
                    n = i * 3 + j
                    acc[px * 2 + i, gyp * 2 + j] += sums[n * 8 : n * 8 + 8]

    low_half = iota((8, 128), 0) < 4
    above = iota((8, 128), 1) > 0

    def fold(px):
        for x in range(2):
            for yp in range(PY):
                both = []
                for c in range(2):
                    even = acc[px * 2 + x, yp * 4 + c * 2]
                    odd = acc[px * 2 + x, yp * 4 + c * 2 + 1]
                    first = jnp.where(low_half, even, pltpu.roll(odd, 4, axis=0))
                    second = jnp.where(low_half, pltpu.roll(even, 4, axis=0), odd)
                    second = jnp.where(above, pltpu.roll(second, 1, axis=1), 0.0)
                    both.append(first + second)
                part[px, yp, x] = jnp.where(core == 0, both[0], both[1])
                for_sib[px, yp, x] = jnp.where(core == 0, both[1], both[0])

    def sib_copy(px):
        return pltpu.make_async_remote_copy(
            src_ref=for_sib.at[px], dst_ref=from_sib.at[px], send_sem=sib_send.at[px],
            recv_sem=sib_recv.at[px], device_id=sibling, device_id_type=MESH,
        )

    def sum_copy(step, dy):
        px, py, device = peer(step, dy)
        return pltpu.make_async_remote_copy(
            src_ref=part.at[px, py], dst_ref=landed.at[chip], send_sem=sum_send,
            recv_sem=sum_recv, device_id=device, device_id_type=MESH,
        )

    def send_sums(step):
        px = lax.rem(gx + step, GX)
        sib_copy(px).wait_recv()
        part[px] = part[px] + from_sib[px]
        for dy in (2, 1, 3):
            sum_copy(step, dy).start()

        @pl.when(px != gx)
        def _():
            sum_copy(step, 0).start()

        @pl.when(px == gx)
        def _():
            landed[chip] = part[gx, y]

    def down(step):
        return lax.rem(2 * GX + (-1 - lax.rem(gx, 4)) - step, GX)

    def at(step):
        return lax.rem(gx + down(step), GX)

    def send_part(step, carry):
        sib_copy(at(step)).start()
        return carry

    def send_sum(step, carry):
        send_sums(down(step))
        return carry

    def to_sibling(it):
        return jnp.where(it < HOLD, 0, (it + 1) * STEPS - 1)

    def to_owners(it):
        return jnp.where(it <= HOLD, 0, it * STEPS - 1)

    def chunks_down(it, carry):
        for u in range(STEPS):
            spread(at(it * STEPS + u))

        @pl.when(it > 0)
        def _():
            fold(at(it * STEPS - 1))

        for u in range(STEPS - 1):
            fold(at(it * STEPS + u))

        @pl.when(it == HOLD)
        def _():
            pl.semaphore_wait(barrier, GX * PY)

        lax.fori_loop(to_sibling(it - 1), to_sibling(it), send_part, 0)
        lax.fori_loop(to_owners(it - 1), to_owners(it), send_sum, 0)
        return carry

    lax.fori_loop(0, GX // STEPS, chunks_down, 0)
    fold(at(GX - 1))
    sib_copy(at(GX - 1)).start()
    first = max(0, GX - STEPS - 1) if HOLD < GX // STEPS - 1 else 0
    lax.fori_loop(first, GX, send_sum, 0)

    many = landed.at[pl.ds(0, GX * PY - 1)]
    pltpu.make_async_copy(many, many, sum_recv).wait()

    def add_up(c, so_far):
        for k in range(8):
            so_far = so_far + landed[c * 8 + k]
        return so_far

    total = lax.fori_loop(0, GX * PY // 8, add_up, jnp.zeros((2, 8, 128), F32))
    for x in range(2):
        value = update(total[x])
        for yn in range(2):
            for c in range(3):
                line = value[yn * 4 + c : yn * 4 + c + 1]
                mine[c, x * 2 + yn : x * 2 + yn + 1, :] = line
                own[c, x, yn : yn + 1, :] = line

    z = gx // 4

    def vel_copy(pz, dx, dy):
        device = (pz * 4 + lax.rem(gx + dx, 4), lax.rem(y + dy, PY) * 2 + core)
        return pltpu.make_async_remote_copy(
            src_ref=mine, dst_ref=node_vel.at[core, gx, y], send_sem=vel_send,
            recv_sem=vel_recv.at[gx], device_id=device, device_id_type=MESH,
        )

    def send_row(pz):
        @pl.when(pz != z)
        def _():
            vel_copy(pz, 0, 0).start()

        for dx in (0, 1, 3, 2):
            for dy in (0, 1, 3, 2):
                if dx or dy:
                    vel_copy(pz, dx, dy).start()

    send_row(0)
    for k in range(3):
        send_row(1 + lax.rem(z + k + 2, 3))

    node_vel[core, gx, y] = mine[...]

    def forward(px):
        return pltpu.make_async_remote_copy(
            src_ref=node_vel.at[core, px], dst_ref=node_vel.at[core, px], send_sem=fwd_send.at[px],
            recv_sem=fwd_recv.at[px], device_id=sibling, device_id_type=MESH,
        )

    def order(step):
        row = step // 4
        dz = jnp.where(row < 2, row, 5 - row)
        return lax.rem(gx // 4 + dz, 4) * 4 + lax.rem(gx + step, 4)

    def pass_on(step):
        px = order(step)

        @pl.when(px == gx)
        def _():
            few = node_vel.at[core, px, pl.ds(0, PY - 1)]
            pltpu.make_async_copy(few, few, vel_recv.at[px]).wait()

        @pl.when(px != gx)
        def _():
            here = node_vel.at[core, px]
            pltpu.make_async_copy(here, here, vel_recv.at[px]).wait()

        forward(px).start()

    sub = iota((8, 128), 0)
    below = iota((8, 128), 1) < NZ - 1

    def build(step):
        px = order(step)
        forward(px).wait_recv()
        for x in range(2):
            for yn in range(2 * GY):
                gyp = yn // 2
                n = x * 2 + yn % 2
                c0, c1, c2 = (
                    jnp.broadcast_to(node_vel[gyp % 2, px, gyp // 2, c, n : n + 1, :], (8, 128))
                    for c in range(3)
                )
                level = jnp.where(sub % 4 == 0, c0, jnp.where(sub % 4 == 1, c1, c2))
                lifted = jnp.where(below, pltpu.roll(level, NZ - 1, axis=1), 0.0)
                table[(px * 2 + x) * LINE + yn] = jnp.where(low_half, level, lifted)

    def arrive(step, carry):
        pass_on(step)

        @pl.when(step >= BEHIND)
        def _():
            build(step - BEHIND)

        return carry

    lax.fori_loop(0, GX, arrive, 0)
    lax.fori_loop(GX - BEHIND, GX, lambda step, carry: (build(step), carry)[1], 0)

    def pick(group, lane):
        at = pl.ds(pl.multiple_of(group * 8, 8), 8)
        cell8, fx8, fy8 = cells[at, :], off[0, at, :], off[1, at, :]
        for s in range(8):
            d = dest[group * 8 + s]
            corner = d // GY * (2 * LINE) + d % GY * 2
            cell, fx, fy = (jnp.broadcast_to(v[s : s + 1], (8, 128)) for v in (cell8, fx8, fy8))
            cz = cell & (NZ - 1)
            in_x = cell >= 2 * NZ
            in_y = (cell & NZ) != 0
            got = [
                [
                    jnp.take_along_axis(
                        table[corner + (i * LINE + j)], cz, axis=1, mode="promise_in_bounds"
                    )
                    for j in range(3)
                ]
                for i in range(3)
            ]
            side = [[jnp.where(in_y, line[b + 1], line[b]) for b in range(2)] for line in got]
            p = [[jnp.where(in_x, side[a + 1][b], side[a][b]) for b in range(2)] for a in range(2)]
            dy = [p[a][1] - p[a][0] for a in range(2)]
            ly = [p[a][0] + fy * dy[a] for a in range(2)]
            dx = ly[1] - ly[0]
            first = (lane * 8 + s) * LINES
            lines[first : first + 8, :] = ly[0] + fx * dx
            lines[first + 8 : first + 16, :] = dx
            lines[first + 16 : first + 24, :] = dy[0] + fx * (dy[1] - dy[0])

    def one_group(group, lane):
        at = pl.ds(pl.multiple_of(group * 8, 8), 8)

        def row(r):
            return lines[pl.ds(lane * 8 * LINES + r, 8, stride=LINES), :]

        fz = off[2, at, :]
        speed = []
        grads = []
        for c in range(3):
            v0 = row(c)
            dz = row(4 + c) - v0
            speed.append(v0 + fz * dz)
            dx, dy = row(8 + c), row(16 + c)
            grads.append((dx + fz * (row(12 + c) - dx), dy + fz * (row(20 + c) - dy), dz))
        live = live_mask(counts, group)
        limit = by_material(params, 2, mats[at, :])
        e = [strain[k, at, :] for k in range(6)]
        trial = [e[k] + DT * grads[k][k] for k in range(3)]
        for k, (r, c) in enumerate(((0, 1), (0, 2), (1, 2))):
            trial.append(e[3 + k] + (0.5 * DT) * (grads[r][c] + grads[c][r]))
        mean = (trial[0] + trial[1] + trial[2]) * (1.0 / 3.0)
        dev = [trial[k] - mean for k in range(3)] + trial[3:]
        square = [x * x for x in dev]
        size = jnp.sqrt(
            square[0] + square[1] + square[2] + 2.0 * (square[3] + square[4] + square[5])
        )
        factor = limit / jnp.maximum(size, limit)
        for k in range(3):
            new_vel[k, at, :] = jnp.where(live, speed[k], 0.0)
            new_strain[k, at, :] = jnp.where(live, mean + factor * dev[k], 0.0)
            new_strain[3 + k, at, :] = jnp.where(live, factor * dev[3 + k], 0.0)

    def pick_step(step, half):
        for lane in range(UNROLL):
            pick(step * UNROLL + lane, half * UNROLL + lane)

    def map_step(step, half):
        for lane in range(UNROLL):
            one_group(step * UNROLL + lane, half * UNROLL + lane)

    def groups(pair, carry):
        for half in range(2):
            pick_step(pair * 2 + half + 1, 1 - half)
            map_step(pair * 2 + half, half)
        return carry

    last = NB // 8 // UNROLL - 1
    pick_step(0, 0)
    lax.fori_loop(0, last // 2, groups, 0)
    pick_step(last, 1)
    map_step(last - 1, 0)
    map_step(last, 1)

    def finish(px, carry):
        sib_copy(px).wait_send()
        forward(px).wait_send()
        return carry

    lax.fori_loop(0, GX, finish, 0)
    pltpu.make_async_copy(many, many, sum_send).wait()
    own_vel = node_vel.at[core, pl.ds(0, GX - 1)]
    pltpu.make_async_copy(own_vel, own_vel, vel_send).wait()
    own_few = node_vel.at[core, 0, pl.ds(0, PY - 1)]
    pltpu.make_async_copy(own_few, own_few, vel_send).wait()


def scatter(dest, counts, params, off, vel, strain, cells, mats):
    dma = pltpu.SemaphoreType.DMA
    chunks = pltpu.VMEM((GX, PY, 2, 8, 128), F32)
    return pl.pallas_call(
        scatter_kernel,
        out_shape=(
            pltpu.VMEM((3, NB, 128), F32),
            pltpu.VMEM((6, NB, 128), F32),
            pltpu.VMEM((3, 2, 2, 128), F32),
        ),
        in_specs=[HBM] * 8,
        out_specs=[VMEM] * 3,
        scratch_shapes=[
            pltpu.SMEM((NB,), jnp.int32),
            pltpu.SMEM((NB,), jnp.int32),
            pltpu.SMEM((3, 4), F32),
            pltpu.VMEM((2 * UNROLL * 8 * LINES, 128), F32),
            pltpu.VMEM((3, NB, 128), F32),
            pltpu.VMEM((3, NB, 128), F32),
            pltpu.VMEM((6, NB, 128), F32),
            pltpu.VMEM((NB, 128), jnp.int32),
            pltpu.VMEM((NB, 128), jnp.int32),
            pltpu.VMEM((8, 128), jnp.int32),
            pltpu.SMEM((8, 128), jnp.int32),
            pltpu.VMEM(((NB + 1) * ROWS, 128), F32),
            pltpu.VMEM((33, 17, 8, 128), F32),
            chunks, chunks, chunks,
            pltpu.VMEM((3, 4, 128), F32),
            pltpu.VMEM((GX * PY, 2, 8, 128), F32),
            pltpu.VMEM((2, GX, PY, 3, 4, 128), F32),
            pltpu.VMEM((33 * LINE, 8, 128), F32),
            dma((8,)), dma, dma((GX,)), dma((GX,)), dma, dma, dma, dma((GX,)), dma((GX,)),
            dma((GX,)),
        ],
        compiler_params=pltpu.CompilerParams(
            collective_id=0, has_side_effects=True, vmem_limit_bytes=LIMIT
        ),
        name="scatter",
    )(dest, counts, params, off, vel, strain, cells, mats)


def copy_kernel(a, b, c, x, y, z, sem):
    copies = [
        pltpu.make_async_copy(src, dst, sem.at[k])
        for k, (src, dst) in enumerate(((b, y), (a, x), (c, z)))
    ]
    for copy in copies:
        copy.start()
    for copy in copies:
        copy.wait()


def hand_out(*arrays):
    return pl.pallas_call(
        copy_kernel,
        out_shape=tuple(jax.ShapeDtypeStruct(a.shape, a.dtype) for a in arrays),
        in_specs=[VMEM] * 3,
        out_specs=[HBM] * 3,
        scratch_shapes=[pltpu.SemaphoreType.DMA((3,))],
        compiler_params=pltpu.CompilerParams(vmem_limit_bytes=4 * 1024 * 1024),
        name="hand_out",
    )(*arrays)


def shards(offsets, velocity, strain, cells, materials, counts, block_dest, material_params):
    off, vel, eps = (jnp.transpose(x, (1, 0, 2)) for x in (offsets, velocity, strain))
    dest = block_dest.reshape(NB)
    new_vel, new_eps, own = scatter(dest, counts, material_params, off, vel, eps, cells, materials)
    new_vel, new_eps, own = hand_out(new_vel, new_eps, own)
    return jnp.transpose(new_vel, (1, 0, 2)), jnp.transpose(new_eps, (1, 0, 2)), own


def solution(mesh):
    blocks = P(("gx", "gy"), None, None)
    rows = P(("gx", "gy"), None)
    in_specs = (blocks, blocks, blocks, rows, rows, P(("gx", "gy")), rows, P())
    out_specs = (blocks, blocks, P(None, "gx", "gy", None))
    return jax.shard_map(shards, mesh=mesh, in_specs=in_specs, out_specs=out_specs, check_vma=False)
```

```python
import jax
import jax.numpy as jnp
from jax import lax
from jax.experimental import pallas as pl
from jax.experimental.pallas import tpu as pltpu
from jax.sharding import PartitionSpec as P

GX = 16
GY = 8
PY = 4
NZ = 128
NB = 192
DT = 0.25
VOLUME = 0.5
GRAVITY = 1.0
FLOOR = 0.25
MESH = pl.DeviceIdType.MESH
F32 = jnp.float32
BF16 = jnp.bfloat16
VMEM = pl.BlockSpec(memory_space=pltpu.VMEM)
SMEM = pl.BlockSpec(memory_space=pltpu.SMEM)
HBM = pl.BlockSpec(memory_space=pltpu.HBM)
LIMIT = 60 * 1024 * 1024
EMPTY = NB
ROWS = 40
LINES = 24
LINE = 17
BEHIND = 8
HOLD = 1
STEPS = 4
UNROLL = 3
FAR_FIRST = sorted(
    ((dz, dx, dy) for dz in range(4) for dx in range(4) for dy in range(4) if dz + dx + dy),
    key=lambda o: -sum(min(d, 4 - d) for d in o),
)


def iota(shape, dim):
    return lax.broadcasted_iota(jnp.int32, shape, dim)


def live_mask(counts, group):
    sub = iota((8, 128), 0)
    limit = jnp.zeros((8, 128), jnp.int32)
    for s in range(8):
        limit = jnp.where(sub == s, counts[group * 8 + s], limit)
    return iota((8, 128), 1) < limit


def by_material(params, row, mats):
    value = jnp.where(mats == 1, params[row, 1], params[row, 0])
    value = jnp.where(mats == 2, params[row, 2], value)
    return jnp.where(mats == 3, params[row, 3], value)


def source_rows(counts, params, off, vel, strain, cells, mats, rows, group):
    at = pl.ds(pl.multiple_of(group * 8, 8), 8)
    live = live_mask(counts, group)
    material = mats[at, :]
    mass = jnp.where(live, by_material(params, 0, material), 0.0)
    shear = jnp.where(live, by_material(params, 1, material), 0.0) * (-DT * VOLUME)
    e = [strain[k, at, :] for k in range(6)]
    trace = shear * (e[0] + e[1] + e[2])
    twice = 2.0 * shear
    xx, yy, zz = (twice * e[k] + trace for k in range(3))
    xy, xz, yz = (twice * e[k] for k in range(3, 6))
    fz = off[2, at, :]
    zero = jnp.zeros((8, 128), F32)
    full = [mass] + [mass * vel[k, at, :] for k in range(3)]
    base = group * (8 * ROWS)

    def put(row, value):
        rows[pl.ds(base + row, 8, stride=ROWS), :] = value

    for q, sz in enumerate((None, xz, yz, zz)):
        upper = fz * full[q]
        if sz is not None:
            upper = upper + sz
        put(4 + q, upper)
        put(q, full[q] - upper)
    for start, terms in ((8, (None, xx, xy, xz)), (16, (None, xy, yy, yz))):
        for q, term in enumerate(terms):
            if term is None:
                put(start + q, zero)
                put(start + 4 + q, zero)
            else:
                upper = fz * term
                put(start + 4 + q, upper)
                put(start + q, term - upper)
    cell = cells[at, :]
    put(24, off[0, at, :])
    put(25, off[1, at, :])
    put(26, (cell & (NZ - 1)).astype(F32))
    put(27, cell.astype(F32))
    put(28, (cell & NZ).astype(F32))


def node_rows(source):
    t, sx, sy = source[0:8], source[8:16], source[16:24]
    fx, fy, z, in_x, in_y = (
        jnp.broadcast_to(source[24 + k : 25 + k], (8, 128)) for k in range(5)
    )
    in_x = in_x >= 2.0 * NZ
    in_y = in_y > 0.0
    u1 = fx * t + sx
    u0 = t - u1
    w1 = fx * sy
    w0 = sy - w1
    c11 = fy * u1 + w1
    c10 = u1 - c11
    c01 = fy * u0 + w0
    c00 = u0 - c01
    d = []
    for low, high in ((c00, c10), (c01, c11)):
        d.append(
            (jnp.where(in_x, 0.0, low), jnp.where(in_x, low, high), jnp.where(in_x, high, 0.0))
        )
    tiles = []
    for i in range(3):
        low, high = d[0][i], d[1][i]
        tiles += [jnp.where(in_y, 0.0, low), jnp.where(in_y, low, high), jnp.where(in_y, high, 0.0)]
    high = [tile.astype(BF16).astype(F32) for tile in tiles]
    low = [tile - part for tile, part in zip(tiles, high)]
    parts = jnp.concatenate(high + low, axis=0).astype(BF16)
    z16 = jnp.concatenate([z, z], axis=0).astype(BF16)
    z_all = jnp.concatenate([z16] * 8, axis=0)
    depth = iota((128, 128), 0).astype(F32).astype(BF16)
    hot = jnp.where(depth == z_all, jnp.ones((), BF16), jnp.zeros((), BF16))
    return parts, hot


def contract(left, right):
    return lax.dot_general(left, right, (((1,), (1,)), ((), ())), preferred_element_type=F32)


def find_blocks(dest):
    lane = iota((8, 128), 1)
    none = jnp.full((8, 128), EMPTY, jnp.int32)

    def look(step, found):
        first, last = found
        for s in range(8):
            block = step * 8 + s
            back = NB - 1 - block
            last = jnp.where(lane == dest[block], block, last)
            first = jnp.where(lane == dest[back], back, first)
        return first, last

    first, last = lax.fori_loop(0, NB // 8, look, (none, none))
    second = jnp.where(last == first, EMPTY, last)
    return jnp.where(iota((8, 128), 0) == 0, first, second)


def update(total):
    sub = iota((8, 128), 0)
    mass_e = jnp.broadcast_to(total[0:1], (8, 128))
    mass_o = jnp.broadcast_to(total[4:5], (8, 128))
    mass = jnp.where(sub < 4, mass_e, mass_o)
    moved = pltpu.roll(total, 7, axis=0)
    comp = sub % 4
    moved = moved + jnp.where(comp == 2, -DT * GRAVITY, 0.0) * mass
    value = moved / jnp.maximum(mass, FLOOR)
    keep = (comp < 3) & (iota((8, 128), 1) > 0)
    return jnp.where(keep, value, 0.0)


def scatter_kernel(
    dest_in, counts_in, params_in, off_in, vel_in, strain_in, cells_in, mats_in,
    new_vel, new_strain, own,
    dest, counts, params, lines,
    off, vel, strain, cells, mats, found, blocks, rows, acc, part, for_sib, from_sib, mine, landed,
    node_vel, table,
    in_sem, found_sem, sib_send, sib_recv, sum_send, sum_recv, vel_send, vel_recv, fwd_send, fwd_recv,
):
    gx = lax.axis_index("gx")
    gy = lax.axis_index("gy")
    core = lax.rem(gy, 2)
    y = gy // 2
    sibling = (gx, gy + 1 - 2 * core)
    chip = gx * PY + y

    def peer(step, dy):
        px = lax.rem(gx + step, GX)
        py = lax.rem(y + dy, PY)
        return px, py, (px, py * 2 + core)

    loads = [
        pltpu.make_async_copy(src, dst, in_sem.at[k])
        for k, (src, dst) in enumerate(
            (
                (dest_in, dest),
                (counts_in, counts),
                (params_in, params),
                (off_in, off),
                (vel_in, vel),
                (strain_in, strain),
                (mats_in, mats),
                (cells_in, cells),
            )
        )
    ]
    for load in loads:
        load.start()

    barrier = pltpu.get_barrier_semaphore()
    for dz, dx, dy in FAR_FIRST:
        near = (lax.rem(gx // 4 + dz, 4) * 4 + lax.rem(gx + dx, 4), lax.rem(y + dy, PY) * 2 + core)
        pl.semaphore_signal(barrier, inc=1, device_id=near, device_id_type=MESH)
    pl.semaphore_signal(barrier, inc=1, device_id=sibling, device_id_type=MESH)

    loads[0].wait()
    found[...] = find_blocks(dest)
    to_scalars = pltpu.make_async_copy(found, blocks, found_sem)
    to_scalars.start()

    rows[NB * ROWS : (NB + 1) * ROWS, :] = jnp.zeros((ROWS, 128), F32)
    by_block = rows.reshape(NB + 1, ROWS, 128)

    def clear(x, carry):
        acc[x] = jnp.zeros((17, 8, 128), F32)
        return carry

    lax.fori_loop(0, 33, clear, 0)
    for x in range(33):
        table[x * LINE + 16] = jnp.zeros((8, 128), F32)
    for yn in range(16):
        table[32 * LINE + yn] = jnp.zeros((8, 128), F32)
    for load in loads[1:]:
        load.wait()

    def prepare(pair, carry):
        for u in range(2):
            source_rows(counts, params, off, vel, strain, cells, mats, rows, pair * 2 + u)
        return carry

    lax.fori_loop(0, NB // 16, prepare, 0)
    to_scalars.wait()

    def spread(px):
        for gyp in range(GY):
            first, second = (
                node_rows(by_block[blocks[slot, px * GY + gyp]]) for slot in range(2)
            )
            sums = contract(
                jnp.concatenate([first[0], second[0]], axis=1),
                jnp.concatenate([first[1], second[1]], axis=1),
            )
            sums = sums[:72] + sums[72:]
            for i in range(3):
                for j in range(3):
                    n = i * 3 + j
                    acc[px * 2 + i, gyp * 2 + j] += sums[n * 8 : n * 8 + 8]

    low_half = iota((8, 128), 0) < 4
    above = iota((8, 128), 1) > 0

    def fold(px):
        for x in range(2):
            for yp in range(PY):
                both = []
                for c in range(2):
                    even = acc[px * 2 + x, yp * 4 + c * 2]
                    odd = acc[px * 2 + x, yp * 4 + c * 2 + 1]
                    first = jnp.where(low_half, even, pltpu.roll(odd, 4, axis=0))
                    second = jnp.where(low_half, pltpu.roll(even, 4, axis=0), odd)
                    second = jnp.where(above, pltpu.roll(second, 1, axis=1), 0.0)
                    both.append(first + second)
                part[px, yp, x] = jnp.where(core == 0, both[0], both[1])
                for_sib[px, yp, x] = jnp.where(core == 0, both[1], both[0])

    def sib_copy(px):
        return pltpu.make_async_remote_copy(
            src_ref=for_sib.at[px], dst_ref=from_sib.at[px], send_sem=sib_send.at[px],
            recv_sem=sib_recv.at[px], device_id=sibling, device_id_type=MESH,
        )

    def sum_copy(step, dy):
        px, py, device = peer(step, dy)
        return pltpu.make_async_remote_copy(
            src_ref=part.at[px, py], dst_ref=landed.at[chip], send_sem=sum_send,
            recv_sem=sum_recv, device_id=device, device_id_type=MESH,
        )

    def send_sums(step):
        px = lax.rem(gx + step, GX)
        sib_copy(px).wait_recv()
        part[px] = part[px] + from_sib[px]
        for dy in (2, 1, 3):
            sum_copy(step, dy).start()

        @pl.when(px != gx)
        def _():
            sum_copy(step, 0).start()

        @pl.when(px == gx)
        def _():
            landed[chip] = part[gx, y]

    def down(step):
        return lax.rem(2 * GX + (-1 - lax.rem(gx, 4)) - step, GX)

    def at(step):
        return lax.rem(gx + down(step), GX)

    def send_part(step, carry):
        sib_copy(at(step)).start()
        return carry

    def send_sum(step, carry):
        send_sums(down(step))
        return carry

    def to_sibling(it):
        return jnp.where(it < HOLD, 0, (it + 1) * STEPS - 1)

    def to_owners(it):
        return jnp.where(it <= HOLD, 0, it * STEPS - 1)

    def chunks_down(it, carry):
        for u in range(STEPS):
            spread(at(it * STEPS + u))

        @pl.when(it > 0)
        def _():
            fold(at(it * STEPS - 1))

        for u in range(STEPS - 1):
            fold(at(it * STEPS + u))

        @pl.when(it == HOLD)
        def _():
            pl.semaphore_wait(barrier, GX * PY)

        lax.fori_loop(to_sibling(it - 1), to_sibling(it), send_part, 0)
        lax.fori_loop(to_owners(it - 1), to_owners(it), send_sum, 0)
        return carry

    lax.fori_loop(0, GX // STEPS, chunks_down, 0)
    fold(at(GX - 1))
    sib_copy(at(GX - 1)).start()
    first = max(0, GX - STEPS - 1) if HOLD < GX // STEPS - 1 else 0
    lax.fori_loop(first, GX, send_sum, 0)

    many = landed.at[pl.ds(0, GX * PY - 1)]
    pltpu.make_async_copy(many, many, sum_recv).wait()

    def add_up(c, so_far):
        for k in range(8):
            so_far = so_far + landed[c * 8 + k]
        return so_far

    total = lax.fori_loop(0, GX * PY // 8, add_up, jnp.zeros((2, 8, 128), F32))
    for x in range(2):
        value = update(total[x])
        for yn in range(2):
            for c in range(3):
                line = value[yn * 4 + c : yn * 4 + c + 1]
                mine[c, x * 2 + yn : x * 2 + yn + 1, :] = line
                own[c, x, yn : yn + 1, :] = line

    z = gx // 4

    def vel_copy(pz, dx, dy):
        device = (pz * 4 + lax.rem(gx + dx, 4), dy * 2 + core)
        return pltpu.make_async_remote_copy(
            src_ref=mine, dst_ref=node_vel.at[core, gx, y], send_sem=vel_send,
            recv_sem=vel_recv.at[gx], device_id=device, device_id_type=MESH,
        )

    def send_row(pz):
        for py in range(PY):
            @pl.when((pz != z) | (py != y))
            def _():
                vel_copy(pz, 0, py).start()

            for dx in (1, 3, 2):
                vel_copy(pz, dx, py).start()

    send_row(0)
    for k in range(3):
        send_row(1 + lax.rem(z + k + 2, 3))

    node_vel[core, gx, y] = mine[...]

    def forward(px):
        return pltpu.make_async_remote_copy(
            src_ref=node_vel.at[core, px], dst_ref=node_vel.at[core, px], send_sem=fwd_send.at[px],
            recv_sem=fwd_recv.at[px], device_id=sibling, device_id_type=MESH,
        )

    def order(step):
        row = step // 4
        dz = jnp.where(row < 2, row, 5 - row)
        return lax.rem(gx // 4 + dz, 4) * 4 + lax.rem(gx + step, 4)

    def pass_on(step):
        px = order(step)

        @pl.when(px == gx)
        def _():
            few = node_vel.at[core, px, pl.ds(0, PY - 1)]
            pltpu.make_async_copy(few, few, vel_recv.at[px]).wait()

        @pl.when(px != gx)
        def _():
            here = node_vel.at[core, px]
            pltpu.make_async_copy(here, here, vel_recv.at[px]).wait()

        forward(px).start()

    sub = iota((8, 128), 0)
    below = iota((8, 128), 1) < NZ - 1

    def build(step):
        px = order(step)
        forward(px).wait_recv()
        for x in range(2):
            for yn in range(2 * GY):
                gyp = yn // 2
                n = x * 2 + yn % 2
                c0, c1, c2 = (
                    jnp.broadcast_to(node_vel[gyp % 2, px, gyp // 2, c, n : n + 1, :], (8, 128))
                    for c in range(3)
                )
                level = jnp.where(sub % 4 == 0, c0, jnp.where(sub % 4 == 1, c1, c2))
                lifted = jnp.where(below, pltpu.roll(level, NZ - 1, axis=1), 0.0)
                table[(px * 2 + x) * LINE + yn] = jnp.where(low_half, level, lifted)

    def arrive(step, carry):
        pass_on(step)

        @pl.when(step >= BEHIND)
        def _():
            build(step - BEHIND)

        return carry

    lax.fori_loop(0, GX, arrive, 0)
    lax.fori_loop(GX - BEHIND, GX, lambda step, carry: (build(step), carry)[1], 0)

    def pick(group, lane):
        at = pl.ds(pl.multiple_of(group * 8, 8), 8)
        cell8, fx8, fy8 = cells[at, :], off[0, at, :], off[1, at, :]
        for s in range(8):
            d = dest[group * 8 + s]
            corner = d // GY * (2 * LINE) + d % GY * 2
            cell, fx, fy = (jnp.broadcast_to(v[s : s + 1], (8, 128)) for v in (cell8, fx8, fy8))
            cz = cell & (NZ - 1)
            in_x = cell >= 2 * NZ
            in_y = (cell & NZ) != 0
            got = [
                [
                    jnp.take_along_axis(
                        table[corner + (i * LINE + j)], cz, axis=1, mode="promise_in_bounds"
                    )
                    for j in range(3)
                ]
                for i in range(3)
            ]
            side = [[jnp.where(in_y, line[b + 1], line[b]) for b in range(2)] for line in got]
            p = [[jnp.where(in_x, side[a + 1][b], side[a][b]) for b in range(2)] for a in range(2)]
            dy = [p[a][1] - p[a][0] for a in range(2)]
            ly = [p[a][0] + fy * dy[a] for a in range(2)]
            dx = ly[1] - ly[0]
            first = (lane * 8 + s) * LINES
            lines[first : first + 8, :] = ly[0] + fx * dx
            lines[first + 8 : first + 16, :] = dx
            lines[first + 16 : first + 24, :] = dy[0] + fx * (dy[1] - dy[0])

    def one_group(group, lane):
        at = pl.ds(pl.multiple_of(group * 8, 8), 8)

        def row(r):
            return lines[pl.ds(lane * 8 * LINES + r, 8, stride=LINES), :]

        fz = off[2, at, :]
        speed = []
        grads = []
        for c in range(3):
            v0 = row(c)
            dz = row(4 + c) - v0
            speed.append(v0 + fz * dz)
            dx, dy = row(8 + c), row(16 + c)
            grads.append((dx + fz * (row(12 + c) - dx), dy + fz * (row(20 + c) - dy), dz))
        live = live_mask(counts, group)
        limit = by_material(params, 2, mats[at, :])
        e = [strain[k, at, :] for k in range(6)]
        trial = [e[k] + DT * grads[k][k] for k in range(3)]
        for k, (r, c) in enumerate(((0, 1), (0, 2), (1, 2))):
            trial.append(e[3 + k] + (0.5 * DT) * (grads[r][c] + grads[c][r]))
        mean = (trial[0] + trial[1] + trial[2]) * (1.0 / 3.0)
        dev = [trial[k] - mean for k in range(3)] + trial[3:]
        square = [x * x for x in dev]
        size = jnp.sqrt(
            square[0] + square[1] + square[2] + 2.0 * (square[3] + square[4] + square[5])
        )
        factor = limit / jnp.maximum(size, limit)
        for k in range(3):
            new_vel[k, at, :] = jnp.where(live, speed[k], 0.0)
            new_strain[k, at, :] = jnp.where(live, mean + factor * dev[k], 0.0)
            new_strain[3 + k, at, :] = jnp.where(live, factor * dev[3 + k], 0.0)

    def pick_step(step, half):
        for lane in range(UNROLL):
            pick(step * UNROLL + lane, half * UNROLL + lane)

    def map_step(step, half):
        for lane in range(UNROLL):
            one_group(step * UNROLL + lane, half * UNROLL + lane)

    def groups(pair, carry):
        for half in range(2):
            pick_step(pair * 2 + half + 1, 1 - half)
            map_step(pair * 2 + half, half)
        return carry

    last = NB // 8 // UNROLL - 1
    pick_step(0, 0)
    lax.fori_loop(0, last // 2, groups, 0)
    pick_step(last, 1)
    map_step(last - 1, 0)
    map_step(last, 1)

    def finish(px, carry):
        sib_copy(px).wait_send()
        forward(px).wait_send()
        return carry

    lax.fori_loop(0, GX, finish, 0)
    pltpu.make_async_copy(many, many, sum_send).wait()
    own_vel = node_vel.at[core, pl.ds(0, GX - 1)]
    pltpu.make_async_copy(own_vel, own_vel, vel_send).wait()
    own_few = node_vel.at[core, 0, pl.ds(0, PY - 1)]
    pltpu.make_async_copy(own_few, own_few, vel_send).wait()


def scatter(dest, counts, params, off, vel, strain, cells, mats):
    dma = pltpu.SemaphoreType.DMA
    chunks = pltpu.VMEM((GX, PY, 2, 8, 128), F32)
    return pl.pallas_call(
        scatter_kernel,
        out_shape=(
            pltpu.VMEM((3, NB, 128), F32),
            pltpu.VMEM((6, NB, 128), F32),
            pltpu.VMEM((3, 2, 2, 128), F32),
        ),
        in_specs=[HBM] * 8,
        out_specs=[VMEM] * 3,
        scratch_shapes=[
            pltpu.SMEM((NB,), jnp.int32),
            pltpu.SMEM((NB,), jnp.int32),
            pltpu.SMEM((3, 4), F32),
            pltpu.VMEM(((2 * UNROLL * 8 + 1) * LINES, 128), F32),
            pltpu.VMEM((3, NB, 128), F32),
            pltpu.VMEM((3, NB, 128), F32),
            pltpu.VMEM((6, NB, 128), F32),
            pltpu.VMEM((NB, 128), jnp.int32),
            pltpu.VMEM((NB, 128), jnp.int32),
            pltpu.VMEM((8, 128), jnp.int32),
            pltpu.SMEM((8, 128), jnp.int32),
            pltpu.VMEM(((NB + 1) * ROWS, 128), F32),
            pltpu.VMEM((33, 17, 8, 128), F32),
            chunks, chunks, chunks,
            pltpu.VMEM((3, 4, 128), F32),
            pltpu.VMEM((GX * PY, 2, 8, 128), F32),
            pltpu.VMEM((2, GX, PY, 3, 4, 128), F32),
            pltpu.VMEM((33 * LINE, 8, 128), F32),
            dma((8,)), dma, dma((GX,)), dma((GX,)), dma, dma, dma, dma((GX,)), dma((GX,)),
            dma((GX,)),
        ],
        compiler_params=pltpu.CompilerParams(
            collective_id=0, has_side_effects=True, vmem_limit_bytes=LIMIT
        ),
        name="scatter",
    )(dest, counts, params, off, vel, strain, cells, mats)


def copy_kernel(a, b, c, x, y, z, sem):
    copies = [
        pltpu.make_async_copy(src, dst, sem.at[k])
        for k, (src, dst) in enumerate(((b, y), (a, x), (c, z)))
    ]
    for copy in copies:
        copy.start()
    for copy in copies:
        copy.wait()


def hand_out(*arrays):
    return pl.pallas_call(
        copy_kernel,
        out_shape=tuple(jax.ShapeDtypeStruct(a.shape, a.dtype) for a in arrays),
        in_specs=[VMEM] * 3,
        out_specs=[HBM] * 3,
        scratch_shapes=[pltpu.SemaphoreType.DMA((3,))],
        compiler_params=pltpu.CompilerParams(vmem_limit_bytes=4 * 1024 * 1024),
        name="hand_out",
    )(*arrays)


def shards(offsets, velocity, strain, cells, materials, counts, block_dest, material_params):
    off, vel, eps = (jnp.transpose(x, (1, 0, 2)) for x in (offsets, velocity, strain))
    dest = block_dest.reshape(NB)
    new_vel, new_eps, own = scatter(dest, counts, material_params, off, vel, eps, cells, materials)
    new_vel, new_eps, own = hand_out(new_vel, new_eps, own)
    return jnp.transpose(new_vel, (1, 0, 2)), jnp.transpose(new_eps, (1, 0, 2)), own


def solution(mesh):
    blocks = P(("gx", "gy"), None, None)
    rows = P(("gx", "gy"), None)
    in_specs = (blocks, blocks, blocks, rows, rows, P(("gx", "gy")), rows, P())
    out_specs = (blocks, blocks, P(None, "gx", "gy", None))
    return jax.shard_map(shards, mesh=mesh, in_specs=in_specs, out_specs=out_specs, check_vma=False)
```

```python
import jax
import jax.numpy as jnp
from jax import lax
from jax.experimental import pallas as pl
from jax.experimental.pallas import tpu as pltpu
from jax.sharding import PartitionSpec as P

GX = 16
GY = 8
PY = 4
NZ = 128
NB = 192
DT = 0.25
VOLUME = 0.5
GRAVITY = 1.0
FLOOR = 0.25
MESH = pl.DeviceIdType.MESH
F32 = jnp.float32
BF16 = jnp.bfloat16
VMEM = pl.BlockSpec(memory_space=pltpu.VMEM)
SMEM = pl.BlockSpec(memory_space=pltpu.SMEM)
HBM = pl.BlockSpec(memory_space=pltpu.HBM)
LIMIT = 60 * 1024 * 1024
EMPTY = NB
ROWS = 40
LINES = 24
LINE = 17
BEHIND = 12
HOLD = 1
STEPS = 4
UNROLL = 3
FAR_FIRST = sorted(
    ((dz, dx, dy) for dz in range(4) for dx in range(4) for dy in range(4) if dz + dx + dy),
    key=lambda o: -sum(min(d, 4 - d) for d in o),
)


def iota(shape, dim):
    return lax.broadcasted_iota(jnp.int32, shape, dim)


def live_mask(counts, group):
    sub = iota((8, 128), 0)
    limit = jnp.zeros((8, 128), jnp.int32)
    for s in range(8):
        limit = jnp.where(sub == s, counts[group * 8 + s], limit)
    return iota((8, 128), 1) < limit


def by_material(params, row, mats):
    value = jnp.where(mats == 1, params[row, 1], params[row, 0])
    value = jnp.where(mats == 2, params[row, 2], value)
    return jnp.where(mats == 3, params[row, 3], value)


def source_rows(counts, params, off, vel, strain, cells, mats, rows, group):
    at = pl.ds(pl.multiple_of(group * 8, 8), 8)
    live = live_mask(counts, group)
    material = mats[at, :]
    mass = jnp.where(live, by_material(params, 0, material), 0.0)
    shear = jnp.where(live, by_material(params, 1, material), 0.0) * (-DT * VOLUME)
    e = [strain[k, at, :] for k in range(6)]
    trace = shear * (e[0] + e[1] + e[2])
    twice = 2.0 * shear
    xx, yy, zz = (twice * e[k] + trace for k in range(3))
    xy, xz, yz = (twice * e[k] for k in range(3, 6))
    fz = off[2, at, :]
    zero = jnp.zeros((8, 128), F32)
    full = [mass] + [mass * vel[k, at, :] for k in range(3)]
    base = group * (8 * ROWS)

    def put(row, value):
        rows[pl.ds(base + row, 8, stride=ROWS), :] = value

    for q, sz in enumerate((None, xz, yz, zz)):
        upper = fz * full[q]
        if sz is not None:
            upper = upper + sz
        put(4 + q, upper)
        put(q, full[q] - upper)
    for start, terms in ((8, (None, xx, xy, xz)), (16, (None, xy, yy, yz))):
        for q, term in enumerate(terms):
            if term is None:
                put(start + q, zero)
                put(start + 4 + q, zero)
            else:
                upper = fz * term
                put(start + 4 + q, upper)
                put(start + q, term - upper)
    cell = cells[at, :]
    put(24, off[0, at, :])
    put(25, off[1, at, :])
    put(26, (cell & (NZ - 1)).astype(F32))
    put(27, cell.astype(F32))
    put(28, (cell & NZ).astype(F32))


def node_rows(source):
    t, sx, sy = source[0:8], source[8:16], source[16:24]
    fx, fy, z, in_x, in_y = (
        jnp.broadcast_to(source[24 + k : 25 + k], (8, 128)) for k in range(5)
    )
    in_x = in_x >= 2.0 * NZ
    in_y = in_y > 0.0
    u1 = fx * t + sx
    u0 = t - u1
    w1 = fx * sy
    w0 = sy - w1
    c11 = fy * u1 + w1
    c10 = u1 - c11
    c01 = fy * u0 + w0
    c00 = u0 - c01
    d = []
    for low, high in ((c00, c10), (c01, c11)):
        d.append(
            (jnp.where(in_x, 0.0, low), jnp.where(in_x, low, high), jnp.where(in_x, high, 0.0))
        )
    tiles = []
    for i in range(3):
        low, high = d[0][i], d[1][i]
        tiles += [jnp.where(in_y, 0.0, low), jnp.where(in_y, low, high), jnp.where(in_y, high, 0.0)]
    high = [tile.astype(BF16).astype(F32) for tile in tiles]
    low = [tile - part for tile, part in zip(tiles, high)]
    parts = jnp.concatenate(high + low, axis=0).astype(BF16)
    z16 = jnp.concatenate([z, z], axis=0).astype(BF16)
    z_all = jnp.concatenate([z16] * 8, axis=0)
    depth = iota((128, 128), 0).astype(F32).astype(BF16)
    hot = jnp.where(depth == z_all, jnp.ones((), BF16), jnp.zeros((), BF16))
    return parts, hot


def contract(left, right):
    return lax.dot_general(left, right, (((1,), (1,)), ((), ())), preferred_element_type=F32)


def find_blocks(dest):
    lane = iota((8, 128), 1)
    none = jnp.full((8, 128), EMPTY, jnp.int32)

    def look(step, found):
        first, last = found
        for s in range(8):
            block = step * 8 + s
            back = NB - 1 - block
            last = jnp.where(lane == dest[block], block, last)
            first = jnp.where(lane == dest[back], back, first)
        return first, last

    first, last = lax.fori_loop(0, NB // 8, look, (none, none))
    second = jnp.where(last == first, EMPTY, last)
    return jnp.where(iota((8, 128), 0) == 0, first, second)


def update(total):
    sub = iota((8, 128), 0)
    mass_e = jnp.broadcast_to(total[0:1], (8, 128))
    mass_o = jnp.broadcast_to(total[4:5], (8, 128))
    mass = jnp.where(sub < 4, mass_e, mass_o)
    moved = pltpu.roll(total, 7, axis=0)
    comp = sub % 4
    moved = moved + jnp.where(comp == 2, -DT * GRAVITY, 0.0) * mass
    value = moved / jnp.maximum(mass, FLOOR)
    keep = (comp < 3) & (iota((8, 128), 1) > 0)
    return jnp.where(keep, value, 0.0)


def scatter_kernel(
    dest_in, counts_in, params_in, off_in, vel_in, strain_in, cells_in, mats_in,
    new_vel, new_strain, own,
    dest, counts, params, lines,
    off, vel, strain, cells, mats, found, blocks, rows, acc, part, for_sib, from_sib, mine, landed,
    node_vel, table,
    in_sem, found_sem, sib_send, sib_recv, sum_send, sum_recv, vel_send, vel_recv, fwd_send, fwd_recv,
):
    gx = lax.axis_index("gx")
    gy = lax.axis_index("gy")
    core = lax.rem(gy, 2)
    y = gy // 2
    sibling = (gx, gy + 1 - 2 * core)
    chip = gx * PY + y

    def peer(step, dy):
        px = lax.rem(gx + step, GX)
        py = lax.rem(y + dy, PY)
        return px, py, (px, py * 2 + core)

    loads = [
        pltpu.make_async_copy(src, dst, in_sem.at[k])
        for k, (src, dst) in enumerate(
            (
                (dest_in, dest),
                (counts_in, counts),
                (params_in, params),
                (off_in, off),
                (vel_in, vel),
                (strain_in, strain),
                (mats_in, mats),
                (cells_in, cells),
            )
        )
    ]
    for load in loads:
        load.start()

    barrier = pltpu.get_barrier_semaphore()
    for dz, dx, dy in FAR_FIRST:
        near = (lax.rem(gx // 4 + dz, 4) * 4 + lax.rem(gx + dx, 4), lax.rem(y + dy, PY) * 2 + core)
        pl.semaphore_signal(barrier, inc=1, device_id=near, device_id_type=MESH)
    pl.semaphore_signal(barrier, inc=1, device_id=sibling, device_id_type=MESH)

    loads[0].wait()
    found[...] = find_blocks(dest)
    to_scalars = pltpu.make_async_copy(found, blocks, found_sem)
    to_scalars.start()

    rows[NB * ROWS : (NB + 1) * ROWS, :] = jnp.zeros((ROWS, 128), F32)
    by_block = rows.reshape(NB + 1, ROWS, 128)

    def clear(x, carry):
        acc[x] = jnp.zeros((17, 8, 128), F32)
        return carry

    lax.fori_loop(0, 33, clear, 0)
    for x in range(33):
        table[x * LINE + 16] = jnp.zeros((8, 128), F32)
    for yn in range(16):
        table[32 * LINE + yn] = jnp.zeros((8, 128), F32)
    for load in loads[1:]:
        load.wait()

    def prepare(pair, carry):
        for u in range(2):
            source_rows(counts, params, off, vel, strain, cells, mats, rows, pair * 2 + u)
        return carry

    lax.fori_loop(0, NB // 16, prepare, 0)
    to_scalars.wait()

    def spread(px):
        for gyp in range(GY):
            first, second = (
                node_rows(by_block[blocks[slot, px * GY + gyp]]) for slot in range(2)
            )
            sums = contract(
                jnp.concatenate([first[0], second[0]], axis=1),
                jnp.concatenate([first[1], second[1]], axis=1),
            )
            sums = sums[:72] + sums[72:]
            for i in range(3):
                for j in range(3):
                    n = i * 3 + j
                    acc[px * 2 + i, gyp * 2 + j] += sums[n * 8 : n * 8 + 8]

    low_half = iota((8, 128), 0) < 4
    above = iota((8, 128), 1) > 0

    def fold(px):
        for x in range(2):
            for yp in range(PY):
                both = []
                for c in range(2):
                    even = acc[px * 2 + x, yp * 4 + c * 2]
                    odd = acc[px * 2 + x, yp * 4 + c * 2 + 1]
                    first = jnp.where(low_half, even, pltpu.roll(odd, 4, axis=0))
                    second = jnp.where(low_half, pltpu.roll(even, 4, axis=0), odd)
                    second = jnp.where(above, pltpu.roll(second, 1, axis=1), 0.0)
                    both.append(first + second)
                part[px, yp, x] = jnp.where(core == 0, both[0], both[1])
                for_sib[px, yp, x] = jnp.where(core == 0, both[1], both[0])

    def sib_copy(px):
        return pltpu.make_async_remote_copy(
            src_ref=for_sib.at[px], dst_ref=from_sib.at[px], send_sem=sib_send.at[px],
            recv_sem=sib_recv.at[px], device_id=sibling, device_id_type=MESH,
        )

    def sum_copy(step, dy):
        px, py, device = peer(step, dy)
        return pltpu.make_async_remote_copy(
            src_ref=part.at[px, py], dst_ref=landed.at[chip], send_sem=sum_send,
            recv_sem=sum_recv, device_id=device, device_id_type=MESH,
        )

    def send_sums(step):
        px = lax.rem(gx + step, GX)
        sib_copy(px).wait_recv()
        part[px] = part[px] + from_sib[px]
        for dy in (2, 1, 3):
            sum_copy(step, dy).start()

        @pl.when(px != gx)
        def _():
            sum_copy(step, 0).start()

        @pl.when(px == gx)
        def _():
            landed[chip] = part[gx, y]

    def down(step):
        return lax.rem(2 * GX + (-1 - lax.rem(gx, 4)) - step, GX)

    def at(step):
        return lax.rem(gx + down(step), GX)

    def send_part(step, carry):
        sib_copy(at(step)).start()
        return carry

    def send_sum(step, carry):
        send_sums(down(step))
        return carry

    def to_sibling(it):
        return jnp.where(it < HOLD, 0, (it + 1) * STEPS - 1)

    def to_owners(it):
        return jnp.where(it <= HOLD, 0, it * STEPS - 1)

    def chunks_down(it, carry):
        for u in range(STEPS):
            spread(at(it * STEPS + u))

        @pl.when(it > 0)
        def _():
            fold(at(it * STEPS - 1))

        for u in range(STEPS - 1):
            fold(at(it * STEPS + u))

        @pl.when(it == HOLD)
        def _():
            pl.semaphore_wait(barrier, GX * PY)

        lax.fori_loop(to_sibling(it - 1), to_sibling(it), send_part, 0)
        lax.fori_loop(to_owners(it - 1), to_owners(it), send_sum, 0)
        return carry

    lax.fori_loop(0, GX // STEPS, chunks_down, 0)
    fold(at(GX - 1))
    sib_copy(at(GX - 1)).start()
    first = max(0, GX - STEPS - 1) if HOLD < GX // STEPS - 1 else 0
    lax.fori_loop(first, GX, send_sum, 0)

    many = landed.at[pl.ds(0, GX * PY - 1)]
    pltpu.make_async_copy(many, many, sum_recv).wait()

    def add_up(c, so_far):
        for k in range(8):
            so_far = so_far + landed[c * 8 + k]
        return so_far

    total = lax.fori_loop(0, GX * PY // 8, add_up, jnp.zeros((2, 8, 128), F32))
    for x in range(2):
        value = update(total[x])
        for yn in range(2):
            for c in range(3):
                line = value[yn * 4 + c : yn * 4 + c + 1]
                mine[c, x * 2 + yn : x * 2 + yn + 1, :] = line
                own[c, x, yn : yn + 1, :] = line

    z = gx // 4

    def vel_copy(pz, dx, dy):
        device = (pz * 4 + lax.rem(gx + dx, 4), dy * 2 + core)
        return pltpu.make_async_remote_copy(
            src_ref=mine, dst_ref=node_vel.at[core, gx, y], send_sem=vel_send,
            recv_sem=vel_recv.at[gx], device_id=device, device_id_type=MESH,
        )

    def send_row(pz):
        for py in range(PY):
            @pl.when((pz != z) | (py != y))
            def _():
                vel_copy(pz, 0, py).start()

            for dx in (1, 3, 2):
                vel_copy(pz, dx, py).start()

    send_row(0)
    for k in range(3):
        send_row(1 + lax.rem(z + k + 2, 3))

    node_vel[core, gx, y] = mine[...]

    def forward(px):
        return pltpu.make_async_remote_copy(
            src_ref=node_vel.at[core, px], dst_ref=node_vel.at[core, px], send_sem=fwd_send.at[px],
            recv_sem=fwd_recv.at[px], device_id=sibling, device_id_type=MESH,
        )

    def order(step):
        row = step // 4
        dz = jnp.where(row < 2, row, 5 - row)
        return lax.rem(gx // 4 + dz, 4) * 4 + lax.rem(gx + step, 4)

    def pass_on(step):
        px = order(step)

        @pl.when(px == gx)
        def _():
            few = node_vel.at[core, px, pl.ds(0, PY - 1)]
            pltpu.make_async_copy(few, few, vel_recv.at[px]).wait()

        @pl.when(px != gx)
        def _():
            here = node_vel.at[core, px]
            pltpu.make_async_copy(here, here, vel_recv.at[px]).wait()

        forward(px).start()

    sub = iota((8, 128), 0)
    below = iota((8, 128), 1) < NZ - 1

    def build(step):
        px = order(step)
        forward(px).wait_recv()
        for x in range(2):
            for yn in range(2 * GY):
                gyp = yn // 2
                n = x * 2 + yn % 2
                c0, c1, c2 = (
                    jnp.broadcast_to(node_vel[gyp % 2, px, gyp // 2, c, n : n + 1, :], (8, 128))
                    for c in range(3)
                )
                level = jnp.where(sub % 4 == 0, c0, jnp.where(sub % 4 == 1, c1, c2))
                lifted = jnp.where(below, pltpu.roll(level, NZ - 1, axis=1), 0.0)
                table[(px * 2 + x) * LINE + yn] = jnp.where(low_half, level, lifted)

    def arrive(step, carry):
        pass_on(step)

        @pl.when(step >= BEHIND)
        def _():
            build(step - BEHIND)

        return carry

    lax.fori_loop(0, GX, arrive, 0)
    lax.fori_loop(GX - BEHIND, GX, lambda step, carry: (build(step), carry)[1], 0)

    def pick(group, lane):
        at = pl.ds(pl.multiple_of(group * 8, 8), 8)
        cell8, fx8, fy8 = cells[at, :], off[0, at, :], off[1, at, :]
        for s in range(8):
            d = dest[group * 8 + s]
            corner = d // GY * (2 * LINE) + d % GY * 2
            cell, fx, fy = (jnp.broadcast_to(v[s : s + 1], (8, 128)) for v in (cell8, fx8, fy8))
            cz = cell & (NZ - 1)
            in_x = cell >= 2 * NZ
            in_y = (cell & NZ) != 0
            got = [
                [
                    jnp.take_along_axis(
                        table[corner + (i * LINE + j)], cz, axis=1, mode="promise_in_bounds"
                    )
                    for j in range(3)
                ]
                for i in range(3)
            ]
            side = [[jnp.where(in_y, line[b + 1], line[b]) for b in range(2)] for line in got]
            p = [[jnp.where(in_x, side[a + 1][b], side[a][b]) for b in range(2)] for a in range(2)]
            dy = [p[a][1] - p[a][0] for a in range(2)]
            ly = [p[a][0] + fy * dy[a] for a in range(2)]
            dx = ly[1] - ly[0]
            first = (lane * 8 + s) * LINES
            lines[first : first + 8, :] = ly[0] + fx * dx
            lines[first + 8 : first + 16, :] = dx
            lines[first + 16 : first + 24, :] = dy[0] + fx * (dy[1] - dy[0])

    def one_group(group, lane):
        at = pl.ds(pl.multiple_of(group * 8, 8), 8)

        def row(r):
            return lines[pl.ds(lane * 8 * LINES + r, 8, stride=LINES), :]

        fz = off[2, at, :]
        speed = []
        grads = []
        for c in range(3):
            v0 = row(c)
            dz = row(4 + c) - v0
            speed.append(v0 + fz * dz)
            dx, dy = row(8 + c), row(16 + c)
            grads.append((dx + fz * (row(12 + c) - dx), dy + fz * (row(20 + c) - dy), dz))
        live = live_mask(counts, group)
        limit = by_material(params, 2, mats[at, :])
        e = [strain[k, at, :] for k in range(6)]
        trial = [e[k] + DT * grads[k][k] for k in range(3)]
        for k, (r, c) in enumerate(((0, 1), (0, 2), (1, 2))):
            trial.append(e[3 + k] + (0.5 * DT) * (grads[r][c] + grads[c][r]))
        mean = (trial[0] + trial[1] + trial[2]) * (1.0 / 3.0)
        dev = [trial[k] - mean for k in range(3)] + trial[3:]
        square = [x * x for x in dev]
        size = jnp.sqrt(
            square[0] + square[1] + square[2] + 2.0 * (square[3] + square[4] + square[5])
        )
        factor = limit / jnp.maximum(size, limit)
        for k in range(3):
            new_vel[k, at, :] = jnp.where(live, speed[k], 0.0)
            new_strain[k, at, :] = jnp.where(live, mean + factor * dev[k], 0.0)
            new_strain[3 + k, at, :] = jnp.where(live, factor * dev[3 + k], 0.0)

    def pick_step(step, half):
        for lane in range(UNROLL):
            pick(step * UNROLL + lane, half * UNROLL + lane)

    def map_step(step, half):
        for lane in range(UNROLL):
            one_group(step * UNROLL + lane, half * UNROLL + lane)

    def groups(pair, carry):
        for half in range(2):
            pick_step(pair * 2 + half + 1, 1 - half)
            map_step(pair * 2 + half, half)
        return carry

    last = NB // 8 // UNROLL - 1
    pick_step(0, 0)
    lax.fori_loop(0, last // 2, groups, 0)
    pick_step(last, 1)
    map_step(last - 1, 0)
    map_step(last, 1)

    def finish(px, carry):
        sib_copy(px).wait_send()
        forward(px).wait_send()
        return carry

    lax.fori_loop(0, GX, finish, 0)
    pltpu.make_async_copy(many, many, sum_send).wait()
    own_vel = node_vel.at[core, pl.ds(0, GX - 1)]
    pltpu.make_async_copy(own_vel, own_vel, vel_send).wait()
    own_few = node_vel.at[core, 0, pl.ds(0, PY - 1)]
    pltpu.make_async_copy(own_few, own_few, vel_send).wait()


def scatter(dest, counts, params, off, vel, strain, cells, mats):
    dma = pltpu.SemaphoreType.DMA
    chunks = pltpu.VMEM((GX, PY, 2, 8, 128), F32)
    return pl.pallas_call(
        scatter_kernel,
        out_shape=(
            pltpu.VMEM((3, NB, 128), F32),
            pltpu.VMEM((6, NB, 128), F32),
            pltpu.VMEM((3, 2, 2, 128), F32),
        ),
        in_specs=[HBM] * 8,
        out_specs=[VMEM] * 3,
        scratch_shapes=[
            pltpu.SMEM((NB,), jnp.int32),
            pltpu.SMEM((NB,), jnp.int32),
            pltpu.SMEM((3, 4), F32),
            pltpu.VMEM(((2 * UNROLL * 8 + 1) * LINES, 128), F32),
            pltpu.VMEM((3, NB, 128), F32),
            pltpu.VMEM((3, NB, 128), F32),
            pltpu.VMEM((6, NB, 128), F32),
            pltpu.VMEM((NB, 128), jnp.int32),
            pltpu.VMEM((NB, 128), jnp.int32),
            pltpu.VMEM((8, 128), jnp.int32),
            pltpu.SMEM((8, 128), jnp.int32),
            pltpu.VMEM(((NB + 1) * ROWS, 128), F32),
            pltpu.VMEM((33, 17, 8, 128), F32),
            chunks, chunks, chunks,
            pltpu.VMEM((3, 4, 128), F32),
            pltpu.VMEM((GX * PY, 2, 8, 128), F32),
            pltpu.VMEM((2, GX, PY, 3, 4, 128), F32),
            pltpu.VMEM((33 * LINE, 8, 128), F32),
            dma((8,)), dma, dma((GX,)), dma((GX,)), dma, dma, dma, dma((GX,)), dma((GX,)),
            dma((GX,)),
        ],
        compiler_params=pltpu.CompilerParams(
            collective_id=0, has_side_effects=True, vmem_limit_bytes=LIMIT
        ),
        name="scatter",
    )(dest, counts, params, off, vel, strain, cells, mats)


def copy_kernel(a, b, c, x, y, z, sem):
    copies = [
        pltpu.make_async_copy(src, dst, sem.at[k])
        for k, (src, dst) in enumerate(((b, y), (a, x), (c, z)))
    ]
    for copy in copies:
        copy.start()
    for copy in copies:
        copy.wait()


def hand_out(*arrays):
    return pl.pallas_call(
        copy_kernel,
        out_shape=tuple(jax.ShapeDtypeStruct(a.shape, a.dtype) for a in arrays),
        in_specs=[VMEM] * 3,
        out_specs=[HBM] * 3,
        scratch_shapes=[pltpu.SemaphoreType.DMA((3,))],
        compiler_params=pltpu.CompilerParams(vmem_limit_bytes=4 * 1024 * 1024),
        name="hand_out",
    )(*arrays)


def shards(offsets, velocity, strain, cells, materials, counts, block_dest, material_params):
    off, vel, eps = (jnp.transpose(x, (1, 0, 2)) for x in (offsets, velocity, strain))
    dest = block_dest.reshape(NB)
    new_vel, new_eps, own = scatter(dest, counts, material_params, off, vel, eps, cells, materials)
    new_vel, new_eps, own = hand_out(new_vel, new_eps, own)
    return jnp.transpose(new_vel, (1, 0, 2)), jnp.transpose(new_eps, (1, 0, 2)), own


def solution(mesh):
    blocks = P(("gx", "gy"), None, None)
    rows = P(("gx", "gy"), None)
    in_specs = (blocks, blocks, blocks, rows, rows, P(("gx", "gy")), rows, P())
    out_specs = (blocks, blocks, P(None, "gx", "gy", None))
    return jax.shard_map(shards, mesh=mesh, in_specs=in_specs, out_specs=out_specs, check_vma=False)
```
